32 devices in a mesh: gx: 4 (over y, x), gy: 8 (over z, core).
Axes of the slice: x: 2, y: 2, z: 4, core: 2. Of those that a mesh axis runs over, the one named last changes fastest.
Arguments:
- charges: float32 [256, 128, 128], P('gx', 'gy'), may hold values from -6 to 6
- kernel_fine: bfloat16 [9, 9, 9], replicated, may hold values from -0.21875 to 0.21875
- kernel_mid: bfloat16 [9, 9, 9], replicated, may hold values from -0.109375 to 0.109375
- kernel_coarse: bfloat16 [9, 9, 9], replicated, may hold values from -0.0546875 to 0.0546875
Outputs:
- potential: float32 [256, 128, 128], P('gx', 'gy')
The draws below stay inside these ranges and needn't reach their ends.
All inputs are finite; a program needn't handle non-finite values.
Results may differ from the reference program's by a relative error of at most 0.0028.
Values may be sent and summed in bfloat16 or wider, within the bound.
No kernel may reach another device: no remote copies, remote signals or barrier semaphores. Data moves between devices by JAX's collectives and lax.ppermute only.
A program may use at most 128 MiB of HBM per device.

```python
import math
import jax
import jax.numpy as jnp
from jax import lax

CZ = 128
GRID_X = 256
GRID_Y = 128


def level_of(stream_key, extent, split, smallest, high):
    loudness, own = 1.0, jax.random.fold_in(stream_key, 6)
    for axis_at, blocks in split:
        heights = jnp.exp(jax.random.uniform(jax.random.fold_in(own, axis_at), (blocks,), jnp.float32, smallest / len(split), high / len(split)))
        loudness = loudness * jnp.repeat(heights, extent[axis_at] // blocks).reshape([-1 if axis == axis_at else 1 for axis in range(len(extent))])
    return loudness


def bell_draw(rng, dims, width, limit, pieces=(), held_as=jnp.bfloat16):
    drawn = jax.random.normal(rng, dims, jnp.float32) * width
    if len(pieces) > 0:
        drawn = level_of(rng, dims, pieces, -0.22, 0.18) * drawn
    return jnp.clip(drawn, min=-limit, max=limit).astype(held_as)


def setup_inputs(seed: int = 0) -> dict:
    seeds = jax.random.split(jax.random.key(seed), 5)
    return {
        "charges": bell_draw(seeds[0], (GRID_X, GRID_Y, CZ), 1.0, 6.0, ((0, 4), (1, 8)), jnp.float32),
        "kernel_fine": bell_draw(seeds[1], (9, 9, 9), 729 ** -0.5, 0.21875),
        "kernel_mid": bell_draw(seeds[2], (9, 9, 9), 2916 ** -0.5, 0.109375),
        "kernel_coarse": bell_draw(seeds[3], (9, 9, 9), 11664 ** -0.5, 0.0546875),
    }


restrict_taps = ((-3, -0.0625), (-1, 0.5625), (0, 1.0), (1, 0.5625), (3, -0.0625))


def restrict_matrix(fine_cells):
    fine_index = lax.broadcasted_iota(jnp.int32, (fine_cells, fine_cells // 2), 0)
    coarse_index = lax.broadcasted_iota(jnp.int32, (fine_cells, fine_cells // 2), 1)
    spacing = fine_index - 2 * coarse_index
    matrix = jnp.zeros((fine_cells, fine_cells // 2), jnp.float32)
    for offset, factor in restrict_taps:
        matrix = matrix + jnp.where(spacing == offset, jnp.float32(factor), jnp.float32(0.0))
    return matrix


def restrict_axis(padded, axis, coarse_cells):
    result = None
    for offset, factor in restrict_taps:
        sliced = lax.slice_in_dim(padded, 3 + offset, 3 + offset + 2 * coarse_cells - 1, 2, axis)
        result = factor * sliced if result is None else result + factor * sliced
    return result


def restrict(padded):
    along_x = restrict_axis(padded, 0, (padded.shape[0] - 6) // 2)
    along_y = restrict_axis(along_x, 1, (padded.shape[1] - 6) // 2)
    matrix = restrict_matrix(along_y.shape[2])
    return jnp.einsum("xyz,zc->xyc", along_y, matrix, precision=lax.Precision.HIGHEST)


def prolong_axis(padded, axis, coarse_cells):
    def shifted(first_index):
        return lax.slice_in_dim(padded, first_index, first_index + coarse_cells, 1, axis)
    even_cells = shifted(2)
    odd_cells = 0.5625 * (shifted(2) + shifted(3)) - 0.0625 * (shifted(1) + shifted(4))
    paired = jnp.stack([even_cells, odd_cells], axis=axis + 1)
    new_shape = list(even_cells.shape)
    new_shape[axis] = 2 * coarse_cells
    return paired.reshape(new_shape)


def prolong(padded):
    along_x = prolong_axis(padded, 0, padded.shape[0] - 4)
    along_y = prolong_axis(along_x, 1, padded.shape[1] - 4)
    matrix = restrict_matrix(2 * along_y.shape[2])
    return jnp.einsum("xyc,zc->xyz", along_y, matrix, precision=lax.Precision.HIGHEST)


def grid_convolve(field, kernel):
    cells_x, cells_y, cells_z = field.shape
    slab_rows = math.gcd(cells_x, 64)
    size_x = slab_rows + 16
    size_y = ((cells_y + 8 + 63) // 64) * 64
    size_z = ((cells_z + 8 + 63) // 64) * 64
    fft_shape = (size_x, size_y, size_z)
    flipped = kernel[::-1, ::-1, ::-1]
    kernel_hat = jnp.fft.rfftn(flipped, s=fft_shape)
    padded = jnp.pad(field, ((4, 4), (0, 0), (0, 0)))

    def one_slab(first_row):
        slab_input = lax.dynamic_slice_in_dim(padded, first_row, slab_rows + 8, 0)
        product = jnp.fft.irfftn(jnp.fft.rfftn(slab_input, s=fft_shape) * kernel_hat, s=fft_shape)
        return product[8:8 + slab_rows, 4:4 + cells_y, 4:4 + cells_z]

    slab_starts = jnp.arange(cells_x // slab_rows, dtype=jnp.int32) * slab_rows
    slab_results = lax.map(one_slab, slab_starts)
    return slab_results.reshape(cells_x, cells_y, cells_z)


def rounded_copy(field):
    narrow = lax.optimization_barrier(field.astype(jnp.bfloat16))
    return narrow.astype(jnp.float32)


def reference(charges, kernel_fine, kernel_mid, kernel_coarse):
    fine_potential = grid_convolve(rounded_copy(charges), kernel_fine.astype(jnp.float32))
    mid_charges = restrict(jnp.pad(charges, ((3, 3), (3, 3), (0, 0))))
    mid_potential = grid_convolve(rounded_copy(mid_charges), kernel_mid.astype(jnp.float32))
    coarse_charges = restrict(jnp.pad(mid_charges, ((3, 3), (3, 3), (0, 0))))
    coarse_potential = grid_convolve(rounded_copy(coarse_charges), kernel_coarse.astype(jnp.float32))
    mid_total = mid_potential + prolong(jnp.pad(coarse_potential, ((2, 2), (2, 2), (0, 0))))
    return fine_potential + prolong(jnp.pad(mid_total, ((2, 2), (2, 2), (0, 0))))
```

```python
import functools

import jax
import jax.numpy as jnp
import numpy as np
from jax import lax
from jax.experimental import pallas as pl
from jax.experimental.pallas import tpu as pltpu
from jax.sharding import PartitionSpec as P

F32 = jnp.float32
BF16 = jnp.bfloat16
WIDE = 256
HALF = 128
VMEM_LIMIT = 56 * 1024 * 1024


def split_pair(v):
    high = v.astype(BF16).astype(F32)
    low = (v - high).astype(BF16).astype(F32)
    return high, low


def pair_lanes(v):
    return jnp.concatenate(split_pair(v), axis=-1)


def exact_dot(v, matrix):
    high, low = split_pair(v)
    return jnp.dot(high.astype(BF16), matrix, preferred_element_type=F32) + jnp.dot(
        low.astype(BF16), matrix, preferred_element_type=F32
    )


def transfer_matrix(fine, coarse, transpose):
    shape = (coarse, fine) if transpose else (fine, coarse)
    fine_at = lax.broadcasted_iota(jnp.int32, shape, 1 if transpose else 0)
    coarse_at = lax.broadcasted_iota(jnp.int32, shape, 0 if transpose else 1)
    d = fine_at - 2 * coarse_at
    one = jnp.where(d == 0, F32(1.0), F32(0.0))
    near = jnp.where((d == 1) | (d == -1), F32(0.5625), F32(0.0))
    far = jnp.where((d == 3) | (d == -3), F32(-0.0625), F32(0.0))
    return (one + near + far).astype(BF16)


def dot_last(v, matrix):
    lead = v.shape[:-1]
    return exact_dot(v.reshape(-1, v.shape[-1]), matrix).reshape(lead + (matrix.shape[1],))


def rows_at(v, first, low, count):
    begin, end = low - first, low - first + count
    inner = v[max(begin, 0) : min(end, v.shape[0])]
    parts = []
    if begin < 0:
        parts.append(jnp.zeros((-begin,) + v.shape[1:], v.dtype))
    parts.append(inner)
    if end > v.shape[0]:
        parts.append(jnp.zeros((end - v.shape[0],) + v.shape[1:], v.dtype))
    return jnp.concatenate(parts, axis=0) if len(parts) > 1 else inner


def weigh_restrict(even, odd0, odd_m1, odd_p1, odd_m2):
    return even + 0.5625 * (odd0 + odd_m1) - 0.0625 * (odd_p1 + odd_m2)


def restrict_rows(even, even_at, odd, odd_at, low, count):
    return weigh_restrict(
        rows_at(even, even_at, low, count),
        *(rows_at(odd, odd_at, low + s, count) for s in (0, -1, 1, -2)),
    )


def pairs_of_rows(v):
    v = v.reshape((v.shape[0] // 2, 2) + v.shape[1:])
    return v[:, 0], v[:, 1]


def inside(shape, axis, first, cells, index, count):
    at = lax.broadcasted_iota(jnp.int32, shape, axis) + first
    return ((at >= 0) | (index > 0)) & ((at < cells) | (index < count - 1))


def spread_kernel(counts, charges, up, down, mid_own, coarse_own, even_pad, odd_pad, crs):
    gx, gy = lax.axis_index("gx"), lax.axis_index("gy")
    nx, ny = counts
    cells_x, cells_y, cells_z = charges.shape
    mx, my, mz = cells_x // 2, cells_y // 2, cells_z // 2
    cx, cy, cz = cells_x // 4, cells_y // 4, cells_z // 4
    frame = mid_own.shape[1]
    even, odd = pairs_of_rows(charges[...])
    mid = restrict_rows(even, 0, odd, 0, -1, mx + 3)
    mid = dot_last(mid, transfer_matrix(cells_z, mz, False))
    even_pad[...] = jnp.zeros_like(even_pad)
    odd_pad[...] = jnp.zeros_like(odd_pad)
    mid_own[...] = mid
    even_pad[:, 8 : 8 + my] = mid_own[:, pl.ds(0, my, stride=2), :]
    odd_pad[:, 8 : 8 + my] = mid_own[:, pl.ds(1, my, stride=2), :]
    mid = weigh_restrict(
        even_pad[:, 7 : 7 + frame],
        *(odd_pad[:, 7 + s : 7 + s + frame] for s in (0, -1, 1, -2)),
    )
    keep = inside(mid.shape, 0, -1, mx, gx, nx) & inside(mid.shape, 1, -1, my, gy, ny)
    mid = jnp.where(keep, mid, 0.0)
    mid_own[...] = mid
    odd, even = pairs_of_rows(jnp.concatenate([mid, jnp.zeros_like(mid[:1])], axis=0))
    crs[...] = restrict_rows(even, 0, odd, -1, -2, cx + 5)
    n = cx + 5
    odd_pad[:n, 8 : 8 + frame // 2] = crs[:, pl.ds(0, frame // 2, stride=2), :]
    even_pad[:n, 8 : 8 + frame // 2] = crs[:, pl.ds(1, frame // 2, stride=2), :]
    coarse = weigh_restrict(
        even_pad[:n, 6 : 6 + frame],
        *(odd_pad[:n, 7 + s : 7 + s + frame] for s in (0, -1, 1, -2)),
    )
    coarse = dot_last(coarse, transfer_matrix(mz, cz, False))
    keep = inside(coarse.shape, 0, -2, cx, gx, nx) & inside(coarse.shape, 1, -2, cy, gy, ny)
    coarse = jnp.where(keep, coarse, 0.0)
    coarse_own[...] = coarse
    for out, fine_at, mid_at, coarse_at in ((up, cells_x - 4, mx - 4, cx - 4), (down, 0, 0, 0)):
        out[0:4] = charges[fine_at : fine_at + 4].astype(BF16)
        out[4:11] = pair_lanes(mid[mid_at : mid_at + 7]).astype(BF16)
        packed = pair_lanes(coarse[coarse_at : coarse_at + 9])
        blank = jnp.zeros(packed.shape[:-1] + (out.shape[2] - packed.shape[2],), F32)
        out[11:20] = jnp.concatenate([packed, blank], axis=-1).astype(BF16)


def unpair(v, width):
    return v[..., :width] + v[..., width : 2 * width]


def join_x_kernel(charges, mid_own, coarse_own, before, after, fine_x, mid_x, coarse_x, up, down, buf):
    cells_x, cells_y, _ = charges.shape
    mx, cx = cells_x // 2, cells_x // 4
    mz, cz = mid_own.shape[2], coarse_own.shape[2]
    my = cells_y // 2
    fine_x[0:4] = before[0:4].astype(F32)
    fine_x[4 : 4 + cells_x] = charges[...].astype(BF16).astype(F32)
    fine_x[4 + cells_x : 8 + cells_x] = after[0:4].astype(F32)
    low, high = before[4:11].astype(F32), after[4:11].astype(F32)
    mid = (
        rows_at(mid_own[...], -1, -5, mx + 11)
        + rows_at(unpair(low, mz), -5, -5, mx + 11)
        + rows_at(unpair(high, mz), mx - 1, -5, mx + 11)
    )
    mid_x[...] = mid
    low, high = before[11:20].astype(F32), after[11:20].astype(F32)
    coarse = (
        rows_at(coarse_own[...], -2, -6, cx + 13)
        + rows_at(unpair(low, cz), -6, -6, cx + 13)
        + rows_at(unpair(high, cz), cx - 2, -6, cx + 13)
    )
    coarse_x[...] = coarse
    buf[...] = jnp.zeros_like(buf)
    for out, fine_at, mid_at in ((up, cells_y - 4, my - 4), (down, 0, 0)):
        buf[:, 0:4, :] = fine_x[:, fine_at : fine_at + 4, :]
        buf[0 : mx + 11, 4:11, :] = pair_lanes(mid_x[:, mid_at : mid_at + 7, :])
        buf[mx + 11 : mx + cx + 24, 4:13, 0 : 2 * cz] = pair_lanes(coarse_x[:, 0:9, :])
        out[...] = buf[...].astype(BF16)


def join_y_kernel(
    fine_x, mid_x, coarse_x, before, after, fine_xy, mid_xy, coarse_xy, up, down, low, high, buf, side
):
    cells_y = fine_x.shape[1]
    my, cy = cells_y // 2, cells_y // 4
    rows_m, rows_c = mid_x.shape[0], coarse_x.shape[0]
    mz, cz = mid_x.shape[2], coarse_x.shape[2]
    low[...] = before[...].astype(F32)
    high[...] = after[...].astype(F32)
    fine_xy[:, 0:4, :] = low[:, 0:4, :]
    fine_xy[:, 4 : 4 + cells_y, :] = fine_x[...]
    fine_xy[:, 4 + cells_y : 8 + cells_y, :] = high[:, 0:4, :]
    mid_xy[...] = jnp.zeros_like(mid_xy)
    mid_xy[:, 4 : 7 + my, :] = mid_x[:, 0 : my + 3, :]
    mid_xy[:, 0:7, :] += unpair(low[0:rows_m, 4:11, :], mz)
    mid_xy[:, 4 + my : 11 + my, :] += unpair(high[0:rows_m, 4:11, :], mz)
    from_low = unpair(low[rows_m : rows_m + rows_c, 4:13, :], cz)
    from_high = unpair(high[rows_m : rows_m + rows_c, 4:13, :], cz)
    side[...] = jnp.zeros_like(side)
    side[:, 4 : 9 + cy, :] = coarse_x[:, 0 : cy + 5, :]
    coarse_xy[...] = side[...]
    coarse_xy[:, 0:9, :] += from_low
    half = up.shape[0]
    buf[...] = jnp.zeros_like(buf)

    def pack(rows, out):
        buf[:, 0:5, 0 : 2 * cz] = pair_lanes(rows[0:half])
        buf[0 : rows_c - half, 8:13, 0 : 2 * cz] = pair_lanes(rows[half:rows_c])
        out[...] = buf[...].astype(BF16)

    pack(coarse_xy[:, 4 + cy : 9 + cy, :], up)
    coarse_xy[:, 4 + cy : 13 + cy, :] += from_high
    side[:, 4 + cy : 13 + cy, :] += from_high
    pack(side[:, 4:9, :], down)


def base_plan(depth, groups):
    per = HALF // depth
    offsets = range(-1, 2 * groups)
    plan = np.full((len(offsets), 2, HALF), -1, np.int64)
    for i, offset in enumerate(offsets):
        for sign in (0, 1):
            for t in range(HALF):
                d = t - HALF * sign
                j = int(np.floor(d / depth + 0.5))
                e = d - depth * j
                tap = per * offset - j
                if abs(e) <= 4 and 0 <= tap <= 8 and abs(j) < per:
                    plan[i, sign, t] = tap * 9 + 4 - e
    return plan


def one_hot_of(plan):
    flat = plan.reshape(-1)
    return (np.arange(HALF)[:, None] == flat[None, :]).astype(jnp.bfloat16)


def bands_kernel(depth, groups, stencil, one_hot, out, bases):
    per = HALF // depth
    values = jnp.dot(stencil[...], one_hot[...], preferred_element_type=F32)
    for dx in range(9):
        bases[dx] = jnp.broadcast_to(values[dx : dx + 1], bases.shape[1:])
    row = lax.broadcasted_iota(jnp.int32, (HALF, HALF), 0)
    col = lax.broadcasted_iota(jnp.int32, (HALF, HALF), 1)
    apart = lax.rem(row, depth) - lax.rem(col, depth)
    band = (apart <= 4) & (apart >= -4)
    right = band & (col >= row)
    left = band & (col < row)

    def one_dx(dx, carry):
        def rolled(i, sign):
            at = (2 * i + sign) * HALF
            line = bases[dx, :, at : at + HALF]
            full = jnp.concatenate([line] * (HALF // 8), axis=0)
            return pltpu.roll(full, 0, 1, stride=1, stride_axis=0)

        for i in range(2 * groups + 1):
            offset = i - 1
            block = jnp.where(right, rolled(i, 0), jnp.where(left, rolled(i, 1), 0.0)).astype(BF16)
            for group in range(groups):
                for a in (0, 1):
                    b = 2 * group + a - offset
                    if b in (0, 1):
                        out[
                            dx,
                            group * WIDE + a * HALF : group * WIDE + (a + 1) * HALF,
                            b * HALF : (b + 1) * HALF,
                        ] = block
        return carry

    lax.fori_loop(0, 9, one_dx, 0)


def bands(stencil, depth, groups):
    one_hot = jnp.asarray(one_hot_of(base_plan(depth, groups)))
    flat = jnp.pad(stencil.reshape(9, 81), ((0, 7), (0, HALF - 81)))
    return pl.pallas_call(
        functools.partial(bands_kernel, depth, groups),
        out_shape=jax.ShapeDtypeStruct((9, groups * WIDE, WIDE), BF16),
        in_specs=[whole(), whole()],
        out_specs=whole(),
        scratch_shapes=[pltpu.VMEM((9, 8, one_hot.shape[1]), F32)],
        compiler_params=pltpu.CompilerParams(vmem_limit_bytes=VMEM_LIMIT),
        cost_estimate=pl.CostEstimate(flops=2 * 10**9, bytes_accessed=4 * 10**6, transcendentals=0),
    )(flat, one_hot)


def gather_rows(field, rows, per, groups, depth, lhs):
    for parity in (0, 1):
        count = rows - parity
        for group in range(groups):
            for a in range(per):
                lane = group * WIDE + a * depth
                part = field[parity:rows, pl.ds(a + per * group, 8, stride=per), :]
                lhs[parity, 0 : count * 8, lane : lane + depth] = part.reshape(count * 8, depth).astype(BF16)


def convolve(lhs, weights, out_rows, acc):
    n = out_rows * 8
    for dx in range(9):
        start = 16 * (dx // 2)
        part = jnp.dot(lhs[dx % 2, start : start + n, :], weights[dx], preferred_element_type=F32)
        acc[...] = part if dx == 0 else acc[...] + part


def conv_kernel(fine_xy, mid_xy, fine_w, mid_w, fine_acc, mid_acc, mid_pad, fine_lhs, mid_lhs):
    rows = fine_xy.shape[0]
    gather_rows(fine_xy, rows, 2, 5, fine_xy.shape[2], fine_lhs)
    convolve(fine_lhs, fine_w, rows - 8, fine_acc)
    mid_pad[...] = jnp.zeros_like(mid_pad)
    mid_pad[:, 0 : mid_xy.shape[1], :] = mid_xy[...]
    gather_rows(mid_pad, mid_pad.shape[0], 4, 3, mid_xy.shape[2], mid_lhs)
    convolve(mid_lhs, mid_w, mid_pad.shape[0] - 8, mid_acc)


def prolong_odd(a, b, c, d):
    return 0.5625 * (b + c) - 0.0625 * (a + d)


def finish_kernel(
    counts, coarse_xy, before, after, coarse_w, fine_acc, mid_acc, out,
    crs_pad, crs_lhs, crs_acc, msg, crs_pot, wide, mid_tot,
):
    gx, gy = lax.axis_index("gx"), lax.axis_index("gy")
    nx, ny = counts
    rows_c, _, cz = coarse_xy.shape
    cells_x, cells_y, cells_z = out.shape
    mx, my, mz = cells_x // 2, cells_y // 2, cells_z // 2
    cx, cy = cells_x // 4, cells_y // 4
    half = before.shape[0]
    crs_pad[...] = jnp.zeros_like(crs_pad)
    crs_pad[:, 0 : coarse_xy.shape[1], :] = coarse_xy[...]
    for source, at in ((before, 0), (after, cy + 8)):
        msg[...] = source[...].astype(F32)
        crs_pad[0:half, at : at + 5, :] += unpair(msg[:, 0:5, :], cz)
        crs_pad[half:rows_c, at : at + 5, :] += unpair(msg[0 : rows_c - half, 8:13, :], cz)
    gather_rows(crs_pad, rows_c, 8, 2, cz, crs_lhs)
    convolve(crs_lhs, coarse_w, rows_c - 8, crs_acc)
    rows = rows_c - 8
    pot = crs_acc[...].reshape(rows, 8, WIDE)
    for b in range(8):
        crs_pot[:, pl.ds(b, 2, stride=8), :] = pot[:, 0:2, b * cz : (b + 1) * cz]
    pot = crs_pot[...]
    keep = inside(pot.shape, 0, -2, cx, gx, nx) & inside(pot.shape, 1, -2, cy, gy, ny)
    pot = jnp.where(keep, pot, 0.0)
    n = cx + 2
    odd = prolong_odd(*(pot[s : s + n] for s in range(4)))
    even = jnp.concatenate([pot[2 : 1 + n], jnp.zeros_like(pot[:1])], axis=0) if n + 2 > rows else pot[2 : 2 + n]
    wide[:, 0] = odd
    wide[:, 1] = even
    wide_y = cy + 2
    v = wide[...].reshape((2 * n,) + pot.shape[1:])
    mid_tot[...] = jnp.zeros_like(mid_tot)
    odd = prolong_odd(*(v[:, s : s + wide_y] for s in range(4)))
    even = v[:, 2 : 1 + wide_y]
    matrix = transfer_matrix(mz, cz, True)
    mid_tot[:, pl.ds(0, wide_y, stride=2), 0:cz] = odd
    mid_tot[:, pl.ds(1, wide_y - 1, stride=2), 0:cz] = even
    total = dot_last(mid_tot[:, :, 0:cz], matrix)
    rows = mx + 3
    pot = mid_acc[...].reshape(rows, 8, WIDE)
    for b in range(4):
        mid_tot[0:rows, pl.ds(b, 3, stride=4), :] = pot[:, 0:3, b * mz : (b + 1) * mz]
    total = mid_tot[0:rows] + total[0:rows]
    keep = inside(total.shape, 0, -1, mx, gx, nx) & inside(total.shape, 1, -1, my, gy, ny)
    mid_tot[0:rows] = jnp.where(keep, total, 0.0)
    matrix = transfer_matrix(cells_z, mz, True)
    pot = fine_acc[...].reshape(cells_x, 8, WIDE)
    for a in (0, 1):
        if a == 0:
            u = mid_tot[0:rows, 1 : 1 + my, :]
        else:
            u = prolong_odd(*(mid_tot[0:rows, s : s + my, :] for s in range(4)))
        u = dot_last(u, matrix)
        odd = prolong_odd(*(u[s : s + mx] for s in range(4)))
        both = jnp.stack([u[1 : 1 + mx], odd], axis=1).reshape(cells_x, my, cells_z)
        out[:, pl.ds(a, my, stride=2), :] = pot[:, :, a * HALF : a * HALF + cells_z] + both


def whole():
    return pl.BlockSpec(memory_space=pltpu.VMEM)


def call(kernel, outs, ins, scratch, flops=10**8):
    return pl.pallas_call(
        kernel,
        out_shape=[jax.ShapeDtypeStruct(s, d) for s, d in outs],
        in_specs=[whole()] * len(ins),
        out_specs=[whole()] * len(outs),
        scratch_shapes=[pltpu.VMEM(s, d) for s, d in scratch],
        compiler_params=pltpu.CompilerParams(vmem_limit_bytes=VMEM_LIMIT),
        cost_estimate=pl.CostEstimate(flops=flops, bytes_accessed=10**6, transcendentals=0),
    )(*ins)


def exchange(up, down, axis, step, size):
    forward = [(i, i + step) for i in range(size - step)]
    backward = [(j, i) for i, j in forward]
    return lax.ppermute(up, axis, forward), lax.ppermute(down, axis, backward)


def local(counts, charges, kernel_fine, kernel_mid, kernel_coarse):
    nx, ny = counts
    cells_x, cells_y, cells_z = charges.shape
    mx, mz, cx, cz = cells_x // 2, cells_z // 2, cells_x // 4, cells_z // 4
    frame = cells_y
    fine_w = bands(kernel_fine, cells_z, 5)
    mid_w = bands(kernel_mid, mz, 3)
    coarse_w = bands(kernel_coarse, cz, 2)
    message = ((20, frame, cells_z), BF16)
    up, down, mid_own, coarse_own = call(
        functools.partial(spread_kernel, counts),
        [message, message, ((mx + 3, frame, mz), F32), ((cx + 5, frame, cz), F32)],
        [charges],
        [((mx + 3, frame + 24, mz), F32), ((mx + 3, frame + 24, mz), F32), ((cx + 5, frame, mz), F32)],
    )
    before, after = exchange(up, down, "gx", 1, nx)
    message = ((cells_x + 8, frame, cells_z), BF16)
    fine_x, mid_x, coarse_x, up, down = call(
        join_x_kernel,
        [
            ((cells_x + 8, cells_y, cells_z), F32),
            ((mx + 11, frame, mz), F32),
            ((cx + 13, frame, cz), F32),
            message,
            message,
        ],
        [charges, mid_own, coarse_own, before, after],
        [((cells_x + 8, frame, cells_z), F32)],
    )
    before, after = exchange(up, down, "gy", 1, ny)
    half = (cx + 14) // 2
    message = ((half, frame, cells_z), BF16)
    fine_xy, mid_xy, coarse_xy, up, down = call(
        join_y_kernel,
        [
            ((cells_x + 8, cells_y + 8, cells_z), F32),
            ((mx + 11, frame + 8, mz), F32),
            ((cx + 13, frame + 8, cz), F32),
            message,
            message,
        ],
        [fine_x, mid_x, coarse_x, before, after],
        [
            ((cells_x + 8, frame, cells_z), F32),
            ((cells_x + 8, frame, cells_z), F32),
            ((half, frame, cells_z), F32),
            ((cx + 13, frame + 8, cz), F32),
        ],
    )
    before, after = exchange(up, down, "gy", 2, ny)
    fine_acc, mid_acc = call(
        conv_kernel,
        [((cells_x * 8, WIDE), F32), (((mx + 3) * 8, WIDE), F32)],
        [fine_xy, mid_xy, fine_w, mid_w],
        [
            ((mx + 11, frame + 32, mz), F32),
            ((2, (cells_x + 8) * 8, 5 * WIDE), BF16),
            ((2, (mx + 12) * 8, 3 * WIDE), BF16),
        ],
        flops=10**10,
    )
    (out,) = call(
        functools.partial(finish_kernel, counts),
        [(charges.shape, F32)],
        [coarse_xy, before, after, coarse_w, fine_acc, mid_acc],
        [
            ((cx + 13, 80, cz), F32),
            ((2, (cx + 14) * 8, 2 * WIDE), BF16),
            (((cx + 5) * 8, WIDE), F32),
            ((half, frame, cells_z), F32),
            ((cx + 5, 16, cz), F32),
            ((cx + 2, 2, 16, cz), F32),
            ((mx + 4, 16, mz), F32),
        ],
    )
    return out


def solution(mesh):
    counts = (mesh.shape["gx"], mesh.shape["gy"])
    placed = (P("gx", "gy", None), P(), P(), P())
    return jax.shard_map(
        functools.partial(local, counts),
        mesh=mesh,
        in_specs=placed,
        out_specs=P("gx", "gy", None),
        check_vma=False,
    )
```

```python
import functools

import jax
import jax.numpy as jnp
from jax import lax
from jax.experimental import pallas as pl
from jax.experimental.pallas import tpu as pltpu
from jax.sharding import PartitionSpec as P

F32 = jnp.float32
BF16 = jnp.bfloat16
WIDE = 256
HALF = 128
VMEM_LIMIT = 14 * 1024 * 1024


def split_pair(v):
    high = v.astype(BF16).astype(F32)
    low = (v - high).astype(BF16).astype(F32)
    return high, low


def pair_lanes(v):
    return jnp.concatenate(split_pair(v), axis=-1)


def exact_dot(v, matrix):
    high, low = split_pair(v)
    return jnp.dot(high.astype(BF16), matrix, preferred_element_type=F32) + jnp.dot(
        low.astype(BF16), matrix, preferred_element_type=F32
    )


def transfer_matrix(fine, coarse, transpose):
    shape = (coarse, fine) if transpose else (fine, coarse)
    fine_at = lax.broadcasted_iota(jnp.int32, shape, 1 if transpose else 0)
    coarse_at = lax.broadcasted_iota(jnp.int32, shape, 0 if transpose else 1)
    d = fine_at - 2 * coarse_at
    one = jnp.where(d == 0, F32(1.0), F32(0.0))
    near = jnp.where((d == 1) | (d == -1), F32(0.5625), F32(0.0))
    far = jnp.where((d == 3) | (d == -3), F32(-0.0625), F32(0.0))
    return (one + near + far).astype(BF16)


def dot_last(v, matrix):
    lead = v.shape[:-1]
    return exact_dot(v.reshape(-1, v.shape[-1]), matrix).reshape(lead + (matrix.shape[1],))


def rows_at(v, first, low, count):
    begin, end = low - first, low - first + count
    inner = v[max(begin, 0) : min(end, v.shape[0])]
    parts = []
    if begin < 0:
        parts.append(jnp.zeros((-begin,) + v.shape[1:], v.dtype))
    parts.append(inner)
    if end > v.shape[0]:
        parts.append(jnp.zeros((end - v.shape[0],) + v.shape[1:], v.dtype))
    return jnp.concatenate(parts, axis=0) if len(parts) > 1 else inner


def weigh_restrict(even, odd0, odd_m1, odd_p1, odd_m2):
    return even + 0.5625 * (odd0 + odd_m1) - 0.0625 * (odd_p1 + odd_m2)


def restrict_rows(even, even_at, odd, odd_at, low, count):
    return weigh_restrict(
        rows_at(even, even_at, low, count),
        *(rows_at(odd, odd_at, low + s, count) for s in (0, -1, 1, -2)),
    )


def pairs_of_rows(v):
    v = v.reshape((v.shape[0] // 2, 2) + v.shape[1:])
    return v[:, 0], v[:, 1]


def inside(shape, axis, first, cells, index, count):
    at = lax.broadcasted_iota(jnp.int32, shape, axis) + first
    return ((at >= 0) | (index > 0)) & ((at < cells) | (index < count - 1))


def spread_kernel(counts, *refs):
    outside, (up, down, mid_own, coarse_own) = refs[0:4], refs[4:8]
    lines, (even_pad, odd_pad, crs, charges), raws, sems = refs[8:11], refs[11:15], refs[15:18], refs[18]
    copies = [
        pltpu.make_async_copy(source, target, sems.at[i])
        for i, (source, target) in enumerate(zip(outside, (charges,) + raws))
    ]
    for copy in copies:
        copy.start()
    even_pad[...] = jnp.zeros_like(even_pad)
    odd_pad[...] = jnp.zeros_like(odd_pad)
    for line in lines:
        line[...] = jnp.zeros_like(line)
    copies[0].wait()
    gx, gy = lax.axis_index("gx"), lax.axis_index("gy")
    nx, ny = counts
    cells_x, cells_y, cells_z = charges.shape
    mx, my, mz = cells_x // 2, cells_y // 2, cells_z // 2
    cx, cy, cz = cells_x // 4, cells_y // 4, cells_z // 4
    frame = mid_own.shape[1]
    even, odd = pairs_of_rows(charges[...])
    mid = restrict_rows(even, 0, odd, 0, -1, mx + 3)
    mid = dot_last(mid, transfer_matrix(cells_z, mz, False))
    mid_own[...] = mid
    even_pad[:, 8 : 8 + my] = mid_own[:, pl.ds(0, my, stride=2), :]
    odd_pad[:, 8 : 8 + my] = mid_own[:, pl.ds(1, my, stride=2), :]
    mid = weigh_restrict(
        even_pad[:, 7 : 7 + frame],
        *(odd_pad[:, 7 + s : 7 + s + frame] for s in (0, -1, 1, -2)),
    )
    keep = inside(mid.shape, 0, -1, mx, gx, nx) & inside(mid.shape, 1, -1, my, gy, ny)
    mid = jnp.where(keep, mid, 0.0)
    mid_own[...] = mid
    odd, even = pairs_of_rows(jnp.concatenate([mid, jnp.zeros_like(mid[:1])], axis=0))
    crs[...] = restrict_rows(even, 0, odd, -1, -2, cx + 5)
    n = cx + 5
    odd_pad[:n, 8 : 8 + frame // 2] = crs[:, pl.ds(0, frame // 2, stride=2), :]
    even_pad[:n, 8 : 8 + frame // 2] = crs[:, pl.ds(1, frame // 2, stride=2), :]
    coarse = weigh_restrict(
        even_pad[:n, 6 : 6 + frame],
        *(odd_pad[:n, 7 + s : 7 + s + frame] for s in (0, -1, 1, -2)),
    )
    coarse = dot_last(coarse, transfer_matrix(mz, cz, False))
    keep = inside(coarse.shape, 0, -2, cx, gx, nx) & inside(coarse.shape, 1, -2, cy, gy, ny)
    coarse = jnp.where(keep, coarse, 0.0)
    coarse_own[...] = coarse
    for out, fine_at, mid_at, coarse_at in ((up, cells_x - 4, mx - 4, cx - 4), (down, 0, 0, 0)):
        out[0:4] = charges[fine_at : fine_at + 4].astype(BF16)
        out[4:8] = two_halves(mid[mid_at : mid_at + 7]).astype(BF16)
        out[8:13] = two_halves(pair_lanes(coarse[coarse_at : coarse_at + 9])).astype(BF16)
    for copy, line, raw in zip(copies[1:], lines, raws):
        copy.wait()
        line[:, 0:9, 0:9] = raw[...].astype(F32)


def two_halves(v):
    half = (v.shape[0] + 1) // 2
    return jnp.concatenate([v[:half], rows_at(v, 0, half, half)], axis=-1)


def unpair(v, width):
    return v[..., :width] + v[..., width : 2 * width]


def from_halves(v, count):
    lanes = v.shape[-1] // 2
    return jnp.concatenate([v[..., :lanes], v[: count - v.shape[0], :, lanes:]], axis=0)


def fine_parts(rows):
    q = rows // 4
    return [(slice(0, q), q * r, q * r + q, 4 * r, 0) for r in range(4)]


def quarters(rows, at, lanes):
    q = -(-rows // 4)
    parts = []
    for r in range(4):
        first, last = q * r, min(q * r + q, rows)
        parts.append((slice(at, at + last - first), first, last, 8 * (r // 2), lanes * (r % 2)))
    return parts


def join_x_kernel(charges, mid_own, coarse_own, before, after, fine_x, mid_x, coarse_x, up, down, buf):
    cells_x, cells_y, _ = charges.shape
    mx, cx = cells_x // 2, cells_x // 4
    mz, cz = mid_own.shape[2], coarse_own.shape[2]
    my = cells_y // 2
    fine_x[0:4] = before[0:4].astype(F32)
    fine_x[4 : 4 + cells_x] = charges[...].astype(BF16).astype(F32)
    fine_x[4 + cells_x : 8 + cells_x] = after[0:4].astype(F32)
    low, high = (from_halves(m[4:8].astype(F32), 7) for m in (before, after))
    mid = (
        rows_at(mid_own[...], -1, -5, mx + 11)
        + rows_at(low, -5, -5, mx + 11)
        + rows_at(high, mx - 1, -5, mx + 11)
    )
    mid_x[...] = mid
    low, high = (from_halves(m[8:13].astype(F32), 9) for m in (before, after))
    coarse = (
        rows_at(coarse_own[...], -2, -6, cx + 13)
        + rows_at(unpair(low, cz), -6, -6, cx + 13)
        + rows_at(unpair(high, cz), cx - 2, -6, cx + 13)
    )
    coarse_x[...] = coarse
    buf[...] = jnp.zeros_like(buf)
    for out, fine_at, mid_at in ((up, cells_y - 4, my - 4), (down, 0, 0)):
        for part, first, last, top, left in fine_parts(cells_x + 8):
            buf[part, top : top + 4, left:] = fine_x[first:last, fine_at : fine_at + 4, :]
        at = (cells_x + 8) // 4
        for part, first, last, top, left in quarters(mx + 11, at, mz):
            buf[part, top : top + 7, left : left + mz] = mid_x[first:last, mid_at : mid_at + 7, :]
        at += -(-(mx + 11) // 4)
        buf[at:, 0:9, :] = two_halves(pair_lanes(coarse_x[:, 0:9, :]))
        out[...] = buf[...].astype(BF16)


def join_y_kernel(
    fine_x, mid_x, coarse_x, before, after, fine_xy, mid_xy, coarse_xy, up, down, low, high, buf, side
):
    cells_y = fine_x.shape[1]
    my, cy = cells_y // 2, cells_y // 4
    rows_m, rows_c = mid_x.shape[0], coarse_x.shape[0]
    mz, cz = mid_x.shape[2], coarse_x.shape[2]
    low[...] = before[...].astype(F32)
    high[...] = after[...].astype(F32)
    fine_xy[:, 4 : 4 + cells_y, :] = fine_x[...]
    for part, first, last, top, _ in fine_parts(fine_x.shape[0]):
        fine_xy[first:last, 0:4, :] = low[part, top : top + 4, :]
        fine_xy[first:last, 4 + cells_y : 8 + cells_y, :] = high[part, top : top + 4, :]
    mid_xy[...] = jnp.zeros_like(mid_xy)
    mid_xy[:, 4 : 7 + my, :] = mid_x[:, 0 : my + 3, :]
    at = fine_x.shape[0] // 4
    for part, first, last, top, left in quarters(rows_m, at, mz):
        mid_xy[first:last, 0:7, :] += low[part, top : top + 7, left : left + mz]
        mid_xy[first:last, 4 + my : 11 + my, :] += high[part, top : top + 7, left : left + mz]
    at += -(-rows_m // 4)
    from_low = unpair(from_halves(low[at:, 0:9, :], rows_c), cz)
    from_high = unpair(from_halves(high[at:, 0:9, :], rows_c), cz)
    side[...] = jnp.zeros_like(side)
    side[:, 4 : 9 + cy, :] = coarse_x[:, 0 : cy + 5, :]
    coarse_xy[...] = side[...]
    coarse_xy[:, 0:9, :] += from_low
    buf[...] = jnp.zeros_like(buf)

    def pack(rows, out):
        rows = pair_lanes(rows)
        for part, first, last, top, left in quarters(rows_c, 0, 2 * cz):
            buf[part, top : top + 5, left : left + 2 * cz] = rows[first:last]
        out[...] = buf[...].astype(BF16)

    pack(coarse_xy[:, 4 + cy : 9 + cy, :], up)
    coarse_xy[:, 4 + cy : 13 + cy, :] += from_high
    side[:, 4 + cy : 13 + cy, :] += from_high
    pack(side[:, 4:9, :], down)


def bands_kernel(levels, *refs):
    n = len(levels)
    (turned,) = refs[2 * n :]
    tap = lax.broadcasted_iota(jnp.int32, (HALF, HALF), 0)
    place = lax.broadcasted_iota(jnp.int32, (HALF, HALF), 1)
    reverse = ((tap <= 8) & (place == jnp.where(tap <= 4, 4 - tap, HALF + 4 - tap))).astype(F32).astype(BF16)
    for (depth, groups), lines, out in zip(levels, refs[:n], refs[n : 2 * n]):
        per = HALF // depth
        flat = lines[...].reshape(9 * 16, HALF).astype(BF16)
        values = jnp.dot(flat, reverse, preferred_element_type=F32)
        if per == 1:
            turned[0] = pltpu.roll(values.reshape(9, 16, HALF), 0, 2, stride=16, stride_axis=1)
            turned[1, :, 0:8, :] = jnp.broadcast_to(jnp.sum(turned[0, :, 0:8, :], axis=1, keepdims=True), (9, 8, HALF))
        else:
            for j in range(per):
                turned[j] = (pltpu.roll(values, j * depth, 1) if j else values).reshape(9, 16, HALF)
        apart = lax.rem(tap, depth) - lax.rem(place, depth)
        band = (apart <= 4) & (apart >= -4)

        def one_dx(dx, carry, per=per, depth=depth, groups=groups, out=out, band=band):
            def turn(line, by):
                return pltpu.roll(jnp.broadcast_to(line, (8, HALF)), by, 1, stride=1, stride_axis=0)

            def line_at(first):
                parts = [turned[j, dx, first - j : first - j + 1, :] for j in range(per) if 0 <= first - j <= 8]
                return functools.reduce(jnp.add, parts) if parts else None

            if per == 1:
                joint = [turn(turned[1, dx, 0:1, :], 8 * r) for r in range(16)]
                last = [turn(turned[0, dx, 8:9, :], 8 * r) for r in range(16)]

            def rows_of(offset):
                for a in range(per):
                    line = None if per == 1 else line_at(per * offset + a)
                    for g in range(depth // 8):
                        if per == 1:
                            full = last[g] if offset == 8 else joint[(g - 2 * offset) % 16]
                        else:
                            full = jnp.zeros((8, HALF), F32) if line is None else turn(line, 8 * g)
                        at = a * depth + 8 * g
                        yield jnp.where(band[at : at + 8], full, 0.0)

            zero = jnp.zeros((HALF, HALF), BF16)
            for offset in range(-1, 2 * groups):
                block = zero
                if 0 <= per * offset <= 8:
                    block = jnp.concatenate(list(rows_of(offset)), axis=0).astype(BF16)
                for group in range(groups):
                    for a in (0, 1):
                        b = 2 * group + a - offset
                        if b in (0, 1):
                            at = group * WIDE + a * HALF
                            out[dx, at : at + HALF, b * HALF : (b + 1) * HALF] = block
            return carry

        lax.fori_loop(0, 9, one_dx, 0)


def bands(stencils, levels):
    most = max([2] + [HALF // depth for depth, _ in levels])
    return call(
        functools.partial(bands_kernel, levels),
        [((9, groups * WIDE, WIDE), BF16) for _, groups in levels],
        list(stencils),
        [((most, 9, 16, HALF), F32)],
        flops=10**9,
    )


def gather_rows(field, rows, per, groups, depth, lhs):
    for parity in (0, 1):
        count = rows - parity
        for group in range(groups):
            for a in range(per):
                lane = group * WIDE + a * depth
                part = field[parity:rows, pl.ds(a + per * group, 8, stride=per), :]
                lhs[parity, 0 : count * 8, lane : lane + depth] = part.reshape(count * 8, depth).astype(BF16)


def gather_staged(field, rows, per, groups, depth, stage, lhs):
    count = field.shape[1] // per
    stage[...] = jnp.zeros_like(stage)
    for a in range(per):
        stage[:, 0:count, a * depth : (a + 1) * depth] = field[:, pl.ds(a, count, stride=per), :]
    for parity in (0, 1):
        n = (rows - parity) * 8
        for group in range(groups):
            part = stage[parity:rows, group : group + 8, :].reshape(n, WIDE)
            lhs[parity, 0:n, group * WIDE : (group + 1) * WIDE] = part.astype(BF16)


def convolve(lhs, weights, out_rows, acc):
    n = out_rows * 8
    for dx in range(9):
        start = 16 * (dx // 2)
        part = jnp.dot(lhs[dx % 2, start : start + n, :], weights[dx], preferred_element_type=F32)
        acc[...] = part if dx == 0 else acc[...] + part


def conv_kernel(fine_xy, mid_xy, fine_w, mid_w, fine_acc, mid_acc, stage, fine_lhs, mid_lhs):
    rows = fine_xy.shape[0]
    gather_rows(fine_xy, rows, 2, 5, fine_xy.shape[2], fine_lhs)
    convolve(fine_lhs, fine_w, rows - 8, fine_acc)
    rows = mid_xy.shape[0]
    gather_staged(mid_xy, rows, 4, 3, mid_xy.shape[2], stage, mid_lhs)
    convolve(mid_lhs, mid_w, rows - 8, mid_acc)


def prolong_odd(a, b, c, d):
    return 0.5625 * (b + c) - 0.0625 * (a + d)


def finish_kernel(
    counts, coarse_xy, before, after, coarse_w, fine_acc, mid_acc, out,
    crs_pad, stage, crs_lhs, crs_acc, msg, crs_pot, wide, mid_tot,
):
    gx, gy = lax.axis_index("gx"), lax.axis_index("gy")
    nx, ny = counts
    rows_c, _, cz = coarse_xy.shape
    cells_x, cells_y, cells_z = out.shape
    mx, my, mz = cells_x // 2, cells_y // 2, cells_z // 2
    cx, cy = cells_x // 4, cells_y // 4
    crs_pad[...] = coarse_xy[...]
    for source, at in ((before, 0), (after, cy + 8)):
        msg[...] = source[...].astype(F32)
        for part, first, last, top, left in quarters(rows_c, 0, 2 * cz):
            crs_pad[first:last, at : at + 5, :] += unpair(msg[part, top : top + 5, left : left + 2 * cz], cz)
    gather_staged(crs_pad, rows_c, 8, 2, cz, stage, crs_lhs)
    convolve(crs_lhs, coarse_w, rows_c - 8, crs_acc)
    rows = rows_c - 8
    pot = crs_acc[...].reshape(rows, 8, WIDE)
    for b in range(8):
        crs_pot[:, pl.ds(b, 2, stride=8), :] = pot[:, 0:2, b * cz : (b + 1) * cz]
    pot = crs_pot[...]
    keep = inside(pot.shape, 0, -2, cx, gx, nx) & inside(pot.shape, 1, -2, cy, gy, ny)
    pot = jnp.where(keep, pot, 0.0)
    n = cx + 2
    odd = prolong_odd(*(pot[s : s + n] for s in range(4)))
    even = jnp.concatenate([pot[2 : 1 + n], jnp.zeros_like(pot[:1])], axis=0) if n + 2 > rows else pot[2 : 2 + n]
    wide[:, 0] = odd
    wide[:, 1] = even
    wide_y = cy + 2
    v = wide[...].reshape((2 * n,) + pot.shape[1:])
    mid_tot[...] = jnp.zeros_like(mid_tot)
    odd = prolong_odd(*(v[:, s : s + wide_y] for s in range(4)))
    even = v[:, 2 : 1 + wide_y]
    matrix = transfer_matrix(mz, cz, True)
    mid_tot[:, pl.ds(0, wide_y, stride=2), 0:cz] = odd
    mid_tot[:, pl.ds(1, wide_y - 1, stride=2), 0:cz] = even
    total = dot_last(mid_tot[:, :, 0:cz], matrix)
    rows = mx + 3
    pot = mid_acc[...].reshape(rows, 8, WIDE)
    for b in range(4):
        mid_tot[0:rows, pl.ds(b, 3, stride=4), :] = pot[:, 0:3, b * mz : (b + 1) * mz]
    total = mid_tot[0:rows] + total[0:rows]
    keep = inside(total.shape, 0, -1, mx, gx, nx) & inside(total.shape, 1, -1, my, gy, ny)
    mid_tot[0:rows] = jnp.where(keep, total, 0.0)
    matrix = transfer_matrix(cells_z, mz, True)
    pot = fine_acc[...].reshape(cells_x, 8, WIDE)
    for a in (0, 1):
        if a == 0:
            u = mid_tot[0:rows, 1 : 1 + my, :]
        else:
            u = prolong_odd(*(mid_tot[0:rows, s : s + my, :] for s in range(4)))
        u = dot_last(u, matrix)
        odd = prolong_odd(*(u[s : s + mx] for s in range(4)))
        both = jnp.stack([u[1 : 1 + mx], odd], axis=1).reshape(cells_x, my, cells_z)
        out[:, pl.ds(a, my, stride=2), :] = pot[:, :, a * HALF : a * HALF + cells_z] + both


def whole():
    return pl.BlockSpec(memory_space=pltpu.VMEM)


def call(kernel, outs, ins, scratch, flops=10**8, vmem_out=True, after=(), space=pltpu.VMEM, sems=0, limit=VMEM_LIMIT):
    n = len(ins)

    def body(*refs):
        kernel(*refs[:n], *refs[n + len(after) :])

    return pl.pallas_call(
        body,
        out_shape=[pltpu.VMEM(s, d) for s, d in outs] if vmem_out else [jax.ShapeDtypeStruct(s, d) for s, d in outs],
        in_specs=[pl.BlockSpec(memory_space=space)] * n + [pl.BlockSpec(memory_space=pl.ANY)] * len(after),
        out_specs=[whole()] * len(outs),
        scratch_shapes=[pltpu.VMEM(s, d) for s, d in scratch] + [pltpu.SemaphoreType.DMA((sems,))] * (sems > 0),
        compiler_params=pltpu.CompilerParams(vmem_limit_bytes=limit),
        cost_estimate=pl.CostEstimate(flops=flops, bytes_accessed=10**6, transcendentals=0),
    )(*ins, *after)


def exchange(up, down, axis, step, size):
    forward = [(i, i + step) for i in range(size - step)]
    backward = [(j, i) for i, j in forward]
    return lax.ppermute(up, axis, forward), lax.ppermute(down, axis, backward)


def local(counts, charges, kernel_fine, kernel_mid, kernel_coarse):
    nx, ny = counts
    cells_x, cells_y, cells_z = charges.shape
    mx, mz, cx, cz = cells_x // 2, cells_z // 2, cells_x // 4, cells_z // 4
    frame = cells_y
    message = ((13, frame, cells_z), BF16)
    line = ((9, 16, HALF), F32)
    up, down, mid_own, coarse_own, *lines = call(
        functools.partial(spread_kernel, counts),
        [message, message, ((mx + 3, frame, mz), F32), ((cx + 5, frame, cz), F32), line, line, line],
        [charges, kernel_fine, kernel_mid, kernel_coarse],
        [
            ((mx + 3, frame + 24, mz), F32),
            ((mx + 3, frame + 24, mz), F32),
            ((cx + 5, frame, mz), F32),
            (charges.shape, F32),
        ]
        + [((9, 9, 9), BF16)] * 3,
        space=pltpu.HBM,
        sems=4,
        limit=60 * 1024 * 1024,
    )
    before, after = exchange(up, down, "gx", 1, nx)
    levels = ((cells_z, 5), (mz, 3), (cz, 2))
    fine_w, mid_w, coarse_w = bands(lines, levels)
    rows = (cells_x + 8) // 4 + (mx + 14) // 4 + (cx + 14) // 2
    message = ((rows, frame, cells_z), BF16)
    fine_x, mid_x, coarse_x, up, down = call(
        join_x_kernel,
        [
            ((cells_x + 8, cells_y, cells_z), F32),
            ((mx + 11, frame, mz), F32),
            ((cx + 13, frame, cz), F32),
            message,
            message,
        ],
        [charges, mid_own, coarse_own, before, after],
        [((rows, frame, cells_z), F32)],
        after=(fine_w,),
    )
    before, after = exchange(up, down, "gy", 1, ny)
    half = (cx + 16) // 4
    message = ((half, frame, cells_z), BF16)
    fine_xy, mid_xy, coarse_xy, up, down = call(
        join_y_kernel,
        [
            ((cells_x + 8, cells_y + 8, cells_z), F32),
            ((mx + 11, frame + 8, mz), F32),
            ((cx + 13, frame + 8, cz), F32),
            message,
            message,
        ],
        [fine_x, mid_x, coarse_x, before, after],
        [
            ((rows, frame, cells_z), F32),
            ((rows, frame, cells_z), F32),
            ((half, frame, cells_z), F32),
            ((cx + 13, frame + 8, cz), F32),
        ],
    )
    before, after = exchange(up, down, "gy", 2, ny)
    fine_acc, mid_acc = call(
        conv_kernel,
        [((cells_x * 8, WIDE), F32), (((mx + 3) * 8, WIDE), F32)],
        [fine_xy, mid_xy, fine_w, mid_w],
        [
            ((mx + 11, 16, WIDE), F32),
            ((2, (cells_x + 8) * 8, 5 * WIDE), BF16),
            ((2, (mx + 12) * 8, 3 * WIDE), BF16),
        ],
        flops=10**10,
    )
    (out,) = call(
        functools.partial(finish_kernel, counts),
        [(charges.shape, F32)],
        [coarse_xy, before, after, coarse_w, fine_acc, mid_acc],
        [
            ((cx + 13, frame + 8, cz), F32),
            ((cx + 13, 16, WIDE), F32),
            ((2, (cx + 14) * 8, 2 * WIDE), BF16),
            (((cx + 5) * 8, WIDE), F32),
            ((half, frame, cells_z), F32),
            ((cx + 5, 16, cz), F32),
            ((cx + 2, 2, 16, cz), F32),
            ((mx + 4, 16, mz), F32),
        ],
        vmem_out=False,
    )
    return out


def solution(mesh):
    counts = (mesh.shape["gx"], mesh.shape["gy"])
    placed = (P("gx", "gy", None), P(), P(), P())
    return jax.shard_map(
        functools.partial(local, counts),
        mesh=mesh,
        in_specs=placed,
        out_specs=P("gx", "gy", None),
        check_vma=False,
    )
```

```python
import functools

import jax
import jax.numpy as jnp
from jax import lax
from jax.experimental import pallas as pl
from jax.experimental.pallas import tpu as pltpu
from jax.sharding import PartitionSpec as P

F32 = jnp.float32
BF16 = jnp.bfloat16
WIDE = 256
HALF = 128
VMEM_LIMIT = 14 * 1024 * 1024


def split_pair(v):
    high = v.astype(BF16).astype(F32)
    low = (v - high).astype(BF16).astype(F32)
    return high, low


def pair_lanes(v):
    return jnp.concatenate(split_pair(v), axis=-1)


def exact_dot(v, matrix):
    high, low = split_pair(v)
    return jnp.dot(high.astype(BF16), matrix, preferred_element_type=F32) + jnp.dot(
        low.astype(BF16), matrix, preferred_element_type=F32
    )


def transfer_matrix(fine, coarse, transpose):
    shape = (coarse, fine) if transpose else (fine, coarse)
    fine_at = lax.broadcasted_iota(jnp.int32, shape, 1 if transpose else 0)
    coarse_at = lax.broadcasted_iota(jnp.int32, shape, 0 if transpose else 1)
    d = fine_at - 2 * coarse_at
    one = jnp.where(d == 0, F32(1.0), F32(0.0))
    near = jnp.where((d == 1) | (d == -1), F32(0.5625), F32(0.0))
    far = jnp.where((d == 3) | (d == -3), F32(-0.0625), F32(0.0))
    return (one + near + far).astype(BF16)


def dot_last(v, matrix):
    lead = v.shape[:-1]
    return exact_dot(v.reshape(-1, v.shape[-1]), matrix).reshape(lead + (matrix.shape[1],))


def rows_at(v, first, low, count):
    begin, end = low - first, low - first + count
    inner = v[max(begin, 0) : min(end, v.shape[0])]
    parts = []
    if begin < 0:
        parts.append(jnp.zeros((-begin,) + v.shape[1:], v.dtype))
    parts.append(inner)
    if end > v.shape[0]:
        parts.append(jnp.zeros((end - v.shape[0],) + v.shape[1:], v.dtype))
    return jnp.concatenate(parts, axis=0) if len(parts) > 1 else inner


def weigh_restrict(even, odd0, odd_m1, odd_p1, odd_m2):
    return even + 0.5625 * (odd0 + odd_m1) - 0.0625 * (odd_p1 + odd_m2)


def restrict_rows(even, even_at, odd, odd_at, low, count):
    return weigh_restrict(
        rows_at(even, even_at, low, count),
        *(rows_at(odd, odd_at, low + s, count) for s in (0, -1, 1, -2)),
    )


def pairs_of_rows(v):
    v = v.reshape((v.shape[0] // 2, 2) + v.shape[1:])
    return v[:, 0], v[:, 1]


def inside(shape, axis, first, cells, index, count):
    at = lax.broadcasted_iota(jnp.int32, shape, axis) + first
    return ((at >= 0) | (index > 0)) & ((at < cells) | (index < count - 1))


def spread_kernel(counts, *refs):
    outside, (message, fine_own, mid_own, coarse_own, lines) = refs[0:4], refs[4:9]
    (even_pad, odd_pad, crs, charges), raws, sems = refs[9:13], refs[13:16], refs[16]
    copies = [
        pltpu.make_async_copy(source, target, sems.at[i])
        for i, (source, target) in enumerate(zip(outside, (charges,) + raws))
    ]
    for copy in copies:
        copy.start()
    even_pad[...] = jnp.zeros_like(even_pad)
    odd_pad[...] = jnp.zeros_like(odd_pad)
    lines[...] = jnp.zeros_like(lines)
    copies[0].wait()
    fine_own[...] = charges[...].astype(BF16)
    gx, gy = lax.axis_index("gx"), lax.axis_index("gy")
    nx, ny = counts
    cells_x, cells_y, cells_z = charges.shape
    mx, my, mz = cells_x // 2, cells_y // 2, cells_z // 2
    cx, cy, cz = cells_x // 4, cells_y // 4, cells_z // 4
    frame = mid_own.shape[1]
    even, odd = pairs_of_rows(charges[...])
    mid = restrict_rows(even, 0, odd, 0, -1, mx + 3)
    mid = dot_last(mid, transfer_matrix(cells_z, mz, False))
    mid_own[...] = mid
    even_pad[:, 8 : 8 + my] = mid_own[:, pl.ds(0, my, stride=2), :]
    odd_pad[:, 8 : 8 + my] = mid_own[:, pl.ds(1, my, stride=2), :]
    mid = weigh_restrict(
        even_pad[:, 7 : 7 + frame],
        *(odd_pad[:, 7 + s : 7 + s + frame] for s in (0, -1, 1, -2)),
    )
    keep = inside(mid.shape, 0, -1, mx, gx, nx) & inside(mid.shape, 1, -1, my, gy, ny)
    mid = jnp.where(keep, mid, 0.0)
    mid_own[...] = mid
    odd, even = pairs_of_rows(jnp.concatenate([mid, jnp.zeros_like(mid[:1])], axis=0))
    crs[...] = restrict_rows(even, 0, odd, -1, -2, cx + 5)
    n = cx + 5
    odd_pad[:n, 8 : 8 + frame // 2] = crs[:, pl.ds(0, frame // 2, stride=2), :]
    even_pad[:n, 8 : 8 + frame // 2] = crs[:, pl.ds(1, frame // 2, stride=2), :]
    coarse = weigh_restrict(
        even_pad[:n, 6 : 6 + frame],
        *(odd_pad[:n, 7 + s : 7 + s + frame] for s in (0, -1, 1, -2)),
    )
    coarse = dot_last(coarse, transfer_matrix(mz, cz, False))
    keep = inside(coarse.shape, 0, -2, cx, gx, nx) & inside(coarse.shape, 1, -2, cy, gy, ny)
    coarse = jnp.where(keep, coarse, 0.0)
    coarse_own[...] = coarse
    after, before = jnp.minimum(gx + 1, nx - 1), jnp.maximum(gx - 1, 0)
    for slot, fine_at, mid_at, coarse_at in ((after, cells_x - 4, mx - 4, cx - 4), (before, 0, 0, 0)):
        out = message.at[slot]
        out[0:4] = charges[fine_at : fine_at + 4].astype(BF16)
        out[4:8] = two_halves(mid[mid_at : mid_at + 7]).astype(BF16)
        out[8:13] = two_halves(pair_lanes(coarse[coarse_at : coarse_at + 9])).astype(BF16)
    for i, raw in enumerate(raws):
        copies[i + 1].wait()
        lines[9 * i : 9 * i + 9, 0:9, 0:9] = raw[...].astype(F32)


def two_halves(v):
    half = (v.shape[0] + 1) // 2
    return jnp.concatenate([v[:half], rows_at(v, 0, half, half)], axis=-1)


def unpair(v, width):
    return v[..., :width] + v[..., width : 2 * width]


def from_halves(v, count):
    lanes = v.shape[-1] // 2
    return jnp.concatenate([v[..., :lanes], v[: count - v.shape[0], :, lanes:]], axis=0)


def fine_parts(rows):
    q = rows // 4
    return [(slice(0, q), q * r, q * r + q, 4 * r, 0) for r in range(4)]


def quarters(rows, at, lanes):
    q = -(-rows // 4)
    parts = []
    for r in range(4):
        first, last = q * r, min(q * r + q, rows)
        parts.append((slice(at, at + last - first), first, last, 8 * (r // 2), lanes * (r % 2)))
    return parts


def join_x_kernel(nx, charges, mid_own, coarse_own, lines, message, fine_x, mid_x, coarse_x, lines_x, first_out, second_out, buf):
    gx = lax.axis_index("gx")
    lines_x[...] = lines[...]
    before = jnp.where(gx > 0, message[jnp.maximum(gx - 1, 0)].astype(F32), 0.0)
    after = jnp.where(gx < nx - 1, message[jnp.minimum(gx + 1, nx - 1)].astype(F32), 0.0)
    cells_x, cells_y, _ = charges.shape
    mx, cx = cells_x // 2, cells_x // 4
    mz, cz = mid_own.shape[2], coarse_own.shape[2]
    my = cells_y // 2
    rows_x = cells_x + 8
    own = slice(4, 4 + cells_y)
    for edge in (0, 4 + cells_y):
        fine_x[:, edge : edge + 4, :] = jnp.zeros((rows_x, 4, charges.shape[2]), F32)
    fine_x[0:4, own, :] = before[0:4]
    fine_x[4 : 4 + cells_x, own, :] = charges[...].astype(F32)
    fine_x[4 + cells_x : rows_x, own, :] = after[0:4]
    low, high = (from_halves(m[4:8], 7) for m in (before, after))
    mid = (
        rows_at(mid_own[...], -1, -5, mx + 11)
        + rows_at(low, -5, -5, mx + 11)
        + rows_at(high, mx - 1, -5, mx + 11)
    )
    mid_x[...] = mid
    low, high = (from_halves(m[8:13], 9) for m in (before, after))
    coarse = (
        rows_at(coarse_own[...], -2, -6, cx + 13)
        + rows_at(unpair(low, cz), -6, -6, cx + 13)
        + rows_at(unpair(high, cz), cx - 2, -6, cx + 13)
    )
    coarse_x[...] = coarse
    buf[...] = jnp.zeros_like(buf)

    def pack(out, fine_at, mid_at):
        for part, first, last, top, left in fine_parts(cells_x + 8):
            buf[part, top : top + 4, left:] = fine_x[first:last, fine_at : fine_at + 4, :]
        at = (cells_x + 8) // 4
        for part, first, last, top, left in quarters(mx + 11, at, mz):
            buf[part, top : top + 7, left : left + mz] = mid_x[first:last, mid_at : mid_at + 7, :]
        at += -(-(mx + 11) // 4)
        buf[at:, 0:9, :] = two_halves(pair_lanes(coarse_x[:, 0:9, :]))
        out[...] = buf[...].astype(BF16)

    flag = up_first(1, 1)

    @pl.when(flag)
    def _():
        pack(first_out, cells_y, my - 4)
        pack(second_out, 4, 0)

    @pl.when(jnp.logical_not(flag))
    def _():
        pack(first_out, 4, 0)
        pack(second_out, cells_y, my - 4)


def join_y_kernel(at, mid_x, coarse_x, first_in, second_in, mid_xy, coarse_xy, first_out, second_out, low, high, buf, side):
    my, cy = mid_x.shape[1] // 2, mid_x.shape[1] // 4
    rows_m, rows_c = mid_x.shape[0], coarse_x.shape[0]
    mz, cz = mid_x.shape[2], coarse_x.shape[2]
    low[...], high[...] = by_order(up_first(1, 1), first_in[...].astype(F32), second_in[...].astype(F32))
    mid_xy[...] = jnp.zeros_like(mid_xy)
    mid_xy[:, 4 : 7 + my, :] = mid_x[:, 0 : my + 3, :]
    for part, first, last, top, left in quarters(rows_m, at, mz):
        mid_xy[first:last, 0:7, :] += low[part, top : top + 7, left : left + mz]
        mid_xy[first:last, 4 + my : 11 + my, :] += high[part, top : top + 7, left : left + mz]
    at += -(-rows_m // 4)
    from_low = unpair(from_halves(low[at:, 0:9, :], rows_c), cz)
    from_high = unpair(from_halves(high[at:, 0:9, :], rows_c), cz)
    side[...] = jnp.zeros_like(side)
    side[:, 4 : 9 + cy, :] = coarse_x[:, 0 : cy + 5, :]
    coarse_xy[...] = side[...]
    coarse_xy[:, 0:9, :] += from_low
    buf[...] = jnp.zeros_like(buf)

    def pack(rows, out):
        rows = pair_lanes(rows)
        for part, first, last, top, left in quarters(rows_c, 0, 2 * cz):
            buf[part, top : top + 5, left : left + 2 * cz] = rows[first:last]
        out[...] = buf[...].astype(BF16)

    up = coarse_xy[:, 4 + cy : 9 + cy, :]
    coarse_xy[:, 4 + cy : 13 + cy, :] += from_high
    side[:, 4 + cy : 13 + cy, :] += from_high
    down = side[:, 4:9, :]
    flag = up_first(2, 0)
    pack(jnp.where(flag, up, down), first_out)
    pack(jnp.where(flag, down, up), second_out)


def bands_kernel(begin, levels, lines, *refs):
    outs, joint, last, turned = refs[:-3], refs[-3], refs[-2], refs[-1]
    tap = lax.broadcasted_iota(jnp.int32, (HALF, HALF), 0)
    place = lax.broadcasted_iota(jnp.int32, (HALF, HALF), 1)
    reverse = ((tap <= 8) & (place == jnp.where(tap <= 4, 4 - tap, HALF + 4 - tap))).astype(F32).astype(BF16)
    n = len(levels)
    flat = lines[9 * begin : 9 * (begin + n)].reshape(n * 9 * 16, HALF).astype(BF16)
    values = jnp.dot(flat, reverse, preferred_element_type=F32).reshape(n * 9, 16, HALF)
    turned[...] = pltpu.roll(values, 0, 2, stride=16, stride_axis=1)
    joint[...] = jnp.broadcast_to(jnp.sum(turned[:, 0:8, :], axis=1, keepdims=True), joint.shape)
    ninth = [turned[9 * i : 9 * i + 9, 8:9, :] for i in range(n)]
    ninth = functools.reduce(jnp.add, [pltpu.roll(v, 16 * i, 2) if i else v for i, v in enumerate(ninth)])
    last[...] = jnp.broadcast_to(ninth, last.shape)
    lane = lax.broadcasted_iota(jnp.int32, (8, HALF), 1)

    def one_dx(dx, carry):
        def turns(line):
            return [pltpu.roll(line, 8 * r, 1, stride=1, stride_axis=0) for r in range(16)]

        ninths = turns(last[dx])
        for level, ((depth, groups), out) in enumerate(zip(levels, outs)):
            per, steps = HALF // depth, depth // 8
            eights = turns(joint[9 * level + dx])
            for offset in range(2 * groups - 1):
                rows = []
                for a in range(per):
                    for g in range(steps):
                        full = jnp.zeros((8, HALF), F32)
                        for b in range(per):
                            line = per * offset + a - b
                            at = steps * b + g
                            if 0 <= line <= 8:
                                part = ninths[(at - 2 * level) % 16] if line == 8 else eights[(at - 2 * line) % 16]
                                full = part if per == 1 else jnp.where(lane // depth == b, part, full)
                        apart = lax.rem(lane, depth) - 8 * g - lax.broadcasted_iota(jnp.int32, (8, HALF), 0)
                        rows.append(jnp.where((apart <= 4) & (apart >= -4), full, 0.0))
                out[dx, offset] = jnp.concatenate(rows, axis=0).astype(BF16)
        return carry

    lax.fori_loop(0, 9, one_dx, 0)


def bands(lines, begin, levels, after=()):
    n = len(levels) * 9
    return call(
        functools.partial(bands_kernel, begin, levels),
        [((9, 2 * groups - 1, HALF, HALF), BF16) for _, groups in levels],
        [lines],
        [((n, 8, HALF), F32), ((9, 8, HALF), F32), ((n, 16, HALF), F32)],
        flops=10**9,
        after=after,
    )


def weights_of(blocks, dx):
    count = blocks.shape[1]
    zero = jnp.zeros((HALF, HALF), BF16)

    def block(offset):
        return blocks[dx, offset] if 0 <= offset < count else zero

    halves = range(count + 1)
    return jnp.concatenate([jnp.concatenate([block(h), block(h - 1)], axis=1) for h in halves], axis=0)


def gather_rows(field, rows, per, groups, depth, lhs):
    for parity in (0, 1):
        count = rows - parity
        for group in range(groups):
            for a in range(per):
                lane = group * WIDE + a * depth
                part = field[parity:rows, pl.ds(a + per * group, 8, stride=per), :]
                lhs[parity, 0 : count * 8, lane : lane + depth] = part.reshape(count * 8, depth).astype(BF16)


def gather_staged(field, rows, per, groups, depth, stage, lhs):
    count = field.shape[1] // per
    stage[...] = jnp.zeros_like(stage)
    for a in range(per):
        stage[:, 0:count, a * depth : (a + 1) * depth] = field[:, pl.ds(a, count, stride=per), :]
    for parity in (0, 1):
        n = (rows - parity) * 8
        for group in range(groups):
            part = stage[parity:rows, group : group + 8, :].reshape(n, WIDE)
            lhs[parity, 0:n, group * WIDE : (group + 1) * WIDE] = part.astype(BF16)


def convolve(lhs, weights, out_rows, acc):
    n = out_rows * 8
    for dx in range(9):
        start = 16 * (dx // 2)
        part = jnp.dot(lhs[dx % 2, start : start + n, :], weights_of(weights, dx), preferred_element_type=F32)
        acc[...] = part if dx == 0 else acc[...] + part


def own_kernel(fine_x, weights, acc, lhs):
    rows = fine_x.shape[0]
    gather_rows(fine_x, rows, 2, 5, fine_x.shape[2], lhs)
    convolve(lhs, weights, rows - 8, acc)


def group_weights(blocks, dx, group):
    return weights_of(blocks, dx)[group * WIDE : (group + 1) * WIDE]


def rim_kernel(first_in, second_in, mid_xy, own, fine_w, mid_w, fine_acc, mid_acc, rim, stage_f, lhs_f, stage, mid_lhs, sums):
    cells_x = own.shape[0] // 8
    quarter = cells_x // 4
    tiles = rim.shape[1]
    rim[0], rim[1] = by_order(up_first(1, 1), *(v[0:tiles].astype(F32) for v in (first_in, second_in)))
    for side in (0, 1):
        for q in range(4):
            for r in range(4):
                first, last = max(quarter * q, tiles * r), min(quarter * q + quarter + 8, tiles * r + tiles)
                if first < last:
                    to = slice(first - quarter * q, last - quarter * q)
                    source_rows = slice(first - tiles * r, last - tiles * r)
                    for a in (0, 1):
                        part = rim[side, source_rows, pl.ds(4 * r + a, 2, stride=2), :]
                        stage_f[side, to, 2 * q : 2 * q + 2, a * HALF : (a + 1) * HALF] = part
        for parity in (0, 1):
            n = quarter + 8 - parity
            lhs_f[side, parity, 0 : 8 * n, :] = stage_f[side, parity : parity + n].reshape(8 * n, WIDE).astype(BF16)
    n = quarter * 8
    for dx in range(9):
        start = 16 * (dx // 2)
        for i, (side, group) in enumerate(((0, 0), (0, 1), (1, 3), (1, 4))):
            rows = lhs_f[side, dx % 2, start : start + n, :]
            part = jnp.dot(rows, group_weights(fine_w, dx, group), preferred_element_type=F32)
            sums[i] = part if dx == 0 else sums[i] + part
    rows = mid_xy.shape[0]
    gather_staged(mid_xy, rows, 4, 3, mid_xy.shape[2], stage, mid_lhs)
    convolve(mid_lhs, mid_w, rows - 8, mid_acc)
    fine_acc[...] = own[...].reshape(fine_acc.shape)
    near, far, far_right, near_right = (sums[i].reshape(quarter, 8, WIDE) for i in range(4))
    odd = lax.rem(lax.broadcasted_iota(jnp.int32, near.shape, 1), 2) == 1
    stage_f[0, 0:quarter] = near + jnp.where(odd, 0.0, pltpu.roll(far, 7, 1))
    stage_f[1, 0:quarter] = near_right + jnp.where(odd, pltpu.roll(far_right, 1, 1), 0.0)
    for q in range(4):
        at = slice(quarter * q, quarter * q + quarter)
        fine_acc[at, 0:2, :] += stage_f[0, 0:quarter, 2 * q : 2 * q + 2, :]
        fine_acc[at, 6:8, :] += stage_f[1, 0:quarter, 2 * q : 2 * q + 2, :]


def prolong_odd(a, b, c, d):
    return 0.5625 * (b + c) - 0.0625 * (a + d)


def finish_kernel(
    counts, coarse_xy, first_in, second_in, coarse_w, fine_acc, mid_acc, out,
    crs_pad, stage, crs_lhs, crs_acc, msg, crs_pot, wide, mid_tot,
):
    gx, gy = lax.axis_index("gx"), lax.axis_index("gy")
    nx, ny = counts
    rows_c, _, cz = coarse_xy.shape
    cells_x, cells_y, cells_z = out.shape
    mx, my, mz = cells_x // 2, cells_y // 2, cells_z // 2
    cx, cy = cells_x // 4, cells_y // 4
    crs_pad[...] = coarse_xy[...]
    received = by_order(up_first(2, 0), *(v[...].astype(F32) for v in (first_in, second_in)))
    for source, at in zip(received, (0, cy + 8)):
        msg[...] = source
        for part, first, last, top, left in quarters(rows_c, 0, 2 * cz):
            crs_pad[first:last, at : at + 5, :] += unpair(msg[part, top : top + 5, left : left + 2 * cz], cz)
    gather_staged(crs_pad, rows_c, 8, 2, cz, stage, crs_lhs)
    convolve(crs_lhs, coarse_w, rows_c - 8, crs_acc)
    rows = rows_c - 8
    pot = crs_acc[...].reshape(rows, 8, WIDE)
    for b in range(8):
        crs_pot[:, pl.ds(b, 2, stride=8), :] = pot[:, 0:2, b * cz : (b + 1) * cz]
    pot = crs_pot[...]
    keep = inside(pot.shape, 0, -2, cx, gx, nx) & inside(pot.shape, 1, -2, cy, gy, ny)
    pot = jnp.where(keep, pot, 0.0)
    n = cx + 2
    odd = prolong_odd(*(pot[s : s + n] for s in range(4)))
    even = jnp.concatenate([pot[2 : 1 + n], jnp.zeros_like(pot[:1])], axis=0) if n + 2 > rows else pot[2 : 2 + n]
    wide[:, 0] = odd
    wide[:, 1] = even
    wide_y = cy + 2
    v = wide[...].reshape((2 * n,) + pot.shape[1:])
    mid_tot[...] = jnp.zeros_like(mid_tot)
    odd = prolong_odd(*(v[:, s : s + wide_y] for s in range(4)))
    even = v[:, 2 : 1 + wide_y]
    matrix = transfer_matrix(mz, cz, True)
    mid_tot[:, pl.ds(0, wide_y, stride=2), 0:cz] = odd
    mid_tot[:, pl.ds(1, wide_y - 1, stride=2), 0:cz] = even
    total = dot_last(mid_tot[:, :, 0:cz], matrix)
    rows = mx + 3
    pot = mid_acc[...].reshape(rows, 8, WIDE)
    for b in range(4):
        mid_tot[0:rows, pl.ds(b, 3, stride=4), :] = pot[:, 0:3, b * mz : (b + 1) * mz]
    total = mid_tot[0:rows] + total[0:rows]
    keep = inside(total.shape, 0, -1, mx, gx, nx) & inside(total.shape, 1, -1, my, gy, ny)
    mid_tot[0:rows] = jnp.where(keep, total, 0.0)
    matrix = transfer_matrix(cells_z, mz, True)
    pot = fine_acc[...]
    for a in (0, 1):
        if a == 0:
            u = mid_tot[0:rows, 1 : 1 + my, :]
        else:
            u = prolong_odd(*(mid_tot[0:rows, s : s + my, :] for s in range(4)))
        u = dot_last(u, matrix)
        odd = prolong_odd(*(u[s : s + mx] for s in range(4)))
        both = jnp.stack([u[1 : 1 + mx], odd], axis=1).reshape(cells_x, my, cells_z)
        out[:, pl.ds(a, my, stride=2), :] = pot[:, :, a * HALF : a * HALF + cells_z] + both


def whole():
    return pl.BlockSpec(memory_space=pltpu.VMEM)


def call(kernel, outs, ins, scratch, flops=10**8, vmem_out=True, after=(), space=pltpu.VMEM, sems=0, limit=VMEM_LIMIT):
    n = len(ins)

    def body(*refs):
        kernel(*refs[:n], *refs[n + len(after) :])

    return pl.pallas_call(
        body,
        out_shape=[pltpu.VMEM(s, d) for s, d in outs] if vmem_out else [jax.ShapeDtypeStruct(s, d) for s, d in outs],
        in_specs=[pl.BlockSpec(memory_space=space)] * n + [pl.BlockSpec(memory_space=pl.ANY)] * len(after),
        out_specs=[whole()] * len(outs),
        scratch_shapes=[pltpu.VMEM(s, d) for s, d in scratch] + [pltpu.SemaphoreType.DMA((sems,))] * (sems > 0),
        compiler_params=pltpu.CompilerParams(vmem_limit_bytes=limit),
        cost_estimate=pl.CostEstimate(flops=flops, bytes_accessed=10**6, transcendentals=0),
    )(*ins, *after)


def swap(first, second, axis, step, size, start):
    received = []
    for message, group in ((first, start), (second, 1 - start)):
        lower = [i for i in range(size - step) if (i // step) % 2 == group]
        pairs = [(i, i + step) for i in lower] + [(i + step, i) for i in lower]
        received.append(lax.ppermute(message, axis, pairs))
    return received


def up_first(step, start):
    return lax.rem(lax.axis_index("gy") // step, 2) == start


def by_order(flag, first, second):
    return jnp.where(flag, second, first), jnp.where(flag, first, second)


def local(counts, charges, kernel_fine, kernel_mid, kernel_coarse):
    nx, ny = counts
    cells_x, cells_y, cells_z = charges.shape
    mx, mz, cx, cz = cells_x // 2, cells_z // 2, cells_x // 4, cells_z // 4
    frame = cells_y
    lines = ((27, 16, HALF), F32)
    message, fine_own, mid_own, coarse_own, lines = call(
        functools.partial(spread_kernel, counts),
        [((nx, 13, frame, cells_z), BF16), (charges.shape, BF16), ((mx + 3, frame, mz), F32), ((cx + 5, frame, cz), F32), lines],
        [charges, kernel_fine, kernel_mid, kernel_coarse],
        [
            ((mx + 3, frame + 24, mz), F32),
            ((mx + 3, frame + 24, mz), F32),
            ((cx + 5, frame, mz), F32),
            (charges.shape, F32),
        ]
        + [((9, 9, 9), BF16)] * 3,
        space=pltpu.HBM,
        sems=4,
        limit=60 * 1024 * 1024,
    )
    message = lax.all_to_all(message, "gx", 0, 0)
    rows = (cells_x + 8) // 4 + (mx + 14) // 4 + (cx + 14) // 2
    packed = ((rows, frame, cells_z), BF16)
    fine_x, mid_x, coarse_x, lines, first, second = call(
        functools.partial(join_x_kernel, nx),
        [
            ((cells_x + 8, cells_y + 8, cells_z), F32),
            ((mx + 11, frame, mz), F32),
            ((cx + 13, frame, cz), F32),
            (lines.shape, F32),
            packed,
            packed,
        ],
        [fine_own, mid_own, coarse_own, lines, message],
        [((rows, frame, cells_z), F32)],
    )
    first, second = swap(first, second, "gy", 1, ny, 1)
    (fine_w,) = bands(lines, 0, ((cells_z, 5),))
    (own_acc,) = call(
        own_kernel,
        [((cells_x * 8, WIDE), F32)],
        [fine_x, fine_w],
        [((2, (cells_x + 8) * 8, 5 * WIDE), BF16)],
        flops=10**9,
    )
    half = (cx + 16) // 4
    message = ((half, frame, cells_z), BF16)
    mid_xy, coarse_xy, last_first, last_second = call(
        functools.partial(join_y_kernel, (cells_x + 8) // 4),
        [
            ((mx + 11, frame + 8, mz), F32),
            ((cx + 13, frame + 8, cz), F32),
            message,
            message,
        ],
        [mid_x, coarse_x, first, second],
        [
            ((rows, frame, cells_z), F32),
            ((rows, frame, cells_z), F32),
            ((half, frame, cells_z), F32),
            ((cx + 13, frame + 8, cz), F32),
        ],
        after=(own_acc,),
    )
    last_first, last_second = swap(last_first, last_second, "gy", 2, ny, 0)
    quarter = cells_x // 4
    mid_w, coarse_w = bands(lines, 1, ((mz, 3), (cz, 2)), (mid_xy,))
    fine_acc, mid_acc = call(
        rim_kernel,
        [((cells_x, 8, WIDE), F32), (((mx + 3) * 8, WIDE), F32)],
        [first, second, mid_xy, own_acc, fine_w, mid_w],
        [
            ((2, (cells_x + 8) // 4, frame, cells_z), F32),
            ((2, quarter + 8, 8, WIDE), F32),
            ((2, 2, (quarter + 8) * 8, WIDE), BF16),
            ((mx + 11, 16, WIDE), F32),
            ((2, (mx + 12) * 8, 3 * WIDE), BF16),
            ((4, quarter * 8, WIDE), F32),
        ],
        flops=10**9,
    )
    (out,) = call(
        functools.partial(finish_kernel, counts),
        [(charges.shape, F32)],
        [coarse_xy, last_first, last_second, coarse_w, fine_acc, mid_acc],
        [
            ((cx + 13, frame + 8, cz), F32),
            ((cx + 13, 16, WIDE), F32),
            ((2, (cx + 14) * 8, 2 * WIDE), BF16),
            (((cx + 5) * 8, WIDE), F32),
            ((half, frame, cells_z), F32),
            ((cx + 5, 16, cz), F32),
            ((cx + 2, 2, 16, cz), F32),
            ((mx + 4, 16, mz), F32),
        ],
        vmem_out=False,
    )
    return out


def solution(mesh):
    counts = (mesh.shape["gx"], mesh.shape["gy"])
    placed = (P("gx", "gy", None), P(), P(), P())
    return jax.shard_map(
        functools.partial(local, counts),
        mesh=mesh,
        in_specs=placed,
        out_specs=P("gx", "gy", None),
        check_vma=False,
    )
```

```python
import functools

import jax
import jax.numpy as jnp
from jax import lax
from jax.experimental import pallas as pl
from jax.experimental.pallas import tpu as pltpu
from jax.sharding import PartitionSpec as P

F32 = jnp.float32
BF16 = jnp.bfloat16
WIDE = 256
HALF = 128
VMEM_LIMIT = 14 * 1024 * 1024


def split_pair(v):
    high = v.astype(BF16).astype(F32)
    low = (v - high).astype(BF16).astype(F32)
    return high, low


def pair_lanes(v):
    return jnp.concatenate(split_pair(v), axis=-1)


def exact_dot(v, matrix):
    high, low = split_pair(v)
    return jnp.dot(high.astype(BF16), matrix, preferred_element_type=F32) + jnp.dot(
        low.astype(BF16), matrix, preferred_element_type=F32
    )


def transfer_matrix(fine, coarse, transpose):
    shape = (coarse, fine) if transpose else (fine, coarse)
    fine_at = lax.broadcasted_iota(jnp.int32, shape, 1 if transpose else 0)
    coarse_at = lax.broadcasted_iota(jnp.int32, shape, 0 if transpose else 1)
    d = fine_at - 2 * coarse_at
    one = jnp.where(d == 0, F32(1.0), F32(0.0))
    near = jnp.where((d == 1) | (d == -1), F32(0.5625), F32(0.0))
    far = jnp.where((d == 3) | (d == -3), F32(-0.0625), F32(0.0))
    return (one + near + far).astype(BF16)


def dot_last(v, matrix):
    lead = v.shape[:-1]
    return exact_dot(v.reshape(-1, v.shape[-1]), matrix).reshape(lead + (matrix.shape[1],))


def rows_at(v, first, low, count):
    begin, end = low - first, low - first + count
    inner = v[max(begin, 0) : min(end, v.shape[0])]
    parts = []
    if begin < 0:
        parts.append(jnp.zeros((-begin,) + v.shape[1:], v.dtype))
    parts.append(inner)
    if end > v.shape[0]:
        parts.append(jnp.zeros((end - v.shape[0],) + v.shape[1:], v.dtype))
    return jnp.concatenate(parts, axis=0) if len(parts) > 1 else inner


def weigh_restrict(even, odd0, odd_m1, odd_p1, odd_m2):
    return even + 0.5625 * (odd0 + odd_m1) - 0.0625 * (odd_p1 + odd_m2)


def restrict_rows(even, even_at, odd, odd_at, low, count):
    return weigh_restrict(
        rows_at(even, even_at, low, count),
        *(rows_at(odd, odd_at, low + s, count) for s in (0, -1, 1, -2)),
    )


def pairs_of_rows(v):
    v = v.reshape((v.shape[0] // 2, 2) + v.shape[1:])
    return v[:, 0], v[:, 1]


def inside(shape, axis, first, cells, index, count):
    at = lax.broadcasted_iota(jnp.int32, shape, axis) + first
    return ((at >= 0) | (index > 0)) & ((at < cells) | (index < count - 1))


def spread_kernel(counts, *refs):
    outside, (first_out, second_out, fine_own, mid_own, coarse_own, lines) = refs[0:4], refs[4:10]
    (even_pad, odd_pad, crs, charges), raws, sems = refs[10:14], refs[14:17], refs[17]
    copies = [
        pltpu.make_async_copy(source, target, sems.at[i])
        for i, (source, target) in enumerate(zip(outside, (charges,) + raws))
    ]
    for copy in copies:
        copy.start()
    even_pad[...] = jnp.zeros_like(even_pad)
    odd_pad[...] = jnp.zeros_like(odd_pad)
    lines[...] = jnp.zeros_like(lines)
    copies[0].wait()
    fine_own[...] = charges[...].astype(BF16)
    gx, gy = lax.axis_index("gx"), lax.axis_index("gy")
    nx, ny = counts
    cells_x, cells_y, cells_z = charges.shape
    mx, my, mz = cells_x // 2, cells_y // 2, cells_z // 2
    cx, cy, cz = cells_x // 4, cells_y // 4, cells_z // 4
    frame = mid_own.shape[1]
    even, odd = pairs_of_rows(charges[...])
    mid = restrict_rows(even, 0, odd, 0, -1, mx + 3)
    mid = dot_last(mid, transfer_matrix(cells_z, mz, False))
    mid_own[...] = mid
    even_pad[:, 8 : 8 + my] = mid_own[:, pl.ds(0, my, stride=2), :]
    odd_pad[:, 8 : 8 + my] = mid_own[:, pl.ds(1, my, stride=2), :]
    mid = weigh_restrict(
        even_pad[:, 7 : 7 + frame],
        *(odd_pad[:, 7 + s : 7 + s + frame] for s in (0, -1, 1, -2)),
    )
    keep = inside(mid.shape, 0, -1, mx, gx, nx) & inside(mid.shape, 1, -1, my, gy, ny)
    mid = jnp.where(keep, mid, 0.0)
    mid_own[...] = mid
    odd, even = pairs_of_rows(jnp.concatenate([mid, jnp.zeros_like(mid[:1])], axis=0))
    crs[...] = restrict_rows(even, 0, odd, -1, -2, cx + 5)
    n = cx + 5
    odd_pad[:n, 8 : 8 + frame // 2] = crs[:, pl.ds(0, frame // 2, stride=2), :]
    even_pad[:n, 8 : 8 + frame // 2] = crs[:, pl.ds(1, frame // 2, stride=2), :]
    coarse = weigh_restrict(
        even_pad[:n, 6 : 6 + frame],
        *(odd_pad[:n, 7 + s : 7 + s + frame] for s in (0, -1, 1, -2)),
    )
    coarse = dot_last(coarse, transfer_matrix(mz, cz, False))
    keep = inside(coarse.shape, 0, -2, cx, gx, nx) & inside(coarse.shape, 1, -2, cy, gy, ny)
    coarse = jnp.where(keep, coarse, 0.0)
    coarse_own[...] = coarse
    def pack(out, fine_at, mid_at, coarse_at):
        out[0:4] = charges[fine_at : fine_at + 4].astype(BF16)
        out[4:8] = two_halves(mid_own[mid_at : mid_at + 7]).astype(BF16)
        out[8:13] = two_halves(pair_lanes(coarse_own[coarse_at : coarse_at + 9])).astype(BF16)

    flag = up_first("gx", 1, 1)

    @pl.when(flag)
    def _():
        pack(first_out, cells_x - 4, mx - 4, cx - 4)
        pack(second_out, 0, 0, 0)

    @pl.when(jnp.logical_not(flag))
    def _():
        pack(first_out, 0, 0, 0)
        pack(second_out, cells_x - 4, mx - 4, cx - 4)

    for i, raw in enumerate(raws):
        copies[i + 1].wait()
        lines[9 * i : 9 * i + 9, 0:9, 0:9] = raw[...].astype(F32)


def two_halves(v):
    half = (v.shape[0] + 1) // 2
    return jnp.concatenate([v[:half], rows_at(v, 0, half, half)], axis=-1)


def unpair(v, width):
    return v[..., :width] + v[..., width : 2 * width]


def from_halves(v, count):
    lanes = v.shape[-1] // 2
    return jnp.concatenate([v[..., :lanes], v[: count - v.shape[0], :, lanes:]], axis=0)


def fine_parts(rows):
    q = rows // 4
    return [(slice(0, q), q * r, q * r + q, 4 * r, 0) for r in range(4)]


def quarters(rows, at, lanes):
    q = -(-rows // 4)
    parts = []
    for r in range(4):
        first, last = q * r, min(q * r + q, rows)
        parts.append((slice(at, at + last - first), first, last, 8 * (r // 2), lanes * (r % 2)))
    return parts


def join_x_kernel(charges, mid_own, coarse_own, first_in, second_in, fine_x, mid_x, coarse_x, first_out, second_out, buf):
    before, after = by_order(up_first("gx", 1, 1), *(v[...].astype(F32) for v in (first_in, second_in)))
    cells_x, cells_y, _ = charges.shape
    mx, cx = cells_x // 2, cells_x // 4
    mz, cz = mid_own.shape[2], coarse_own.shape[2]
    my = cells_y // 2
    rows_x = cells_x + 8
    own = slice(4, 4 + cells_y)
    for edge in (0, 4 + cells_y):
        fine_x[:, edge : edge + 4, :] = jnp.zeros((rows_x, 4, charges.shape[2]), F32)
    fine_x[0:4, own, :] = before[0:4]
    fine_x[4 : 4 + cells_x, own, :] = charges[...].astype(F32)
    fine_x[4 + cells_x : rows_x, own, :] = after[0:4]
    low, high = (from_halves(m[4:8], 7) for m in (before, after))
    mid = (
        rows_at(mid_own[...], -1, -5, mx + 11)
        + rows_at(low, -5, -5, mx + 11)
        + rows_at(high, mx - 1, -5, mx + 11)
    )
    mid_x[...] = mid
    low, high = (from_halves(m[8:13], 9) for m in (before, after))
    coarse = (
        rows_at(coarse_own[...], -2, -6, cx + 13)
        + rows_at(unpair(low, cz), -6, -6, cx + 13)
        + rows_at(unpair(high, cz), cx - 2, -6, cx + 13)
    )
    coarse_x[...] = coarse
    buf[...] = jnp.zeros_like(buf)

    def pack(out, fine_at, mid_at):
        for part, first, last, top, left in fine_parts(cells_x + 8):
            buf[part, top : top + 4, left:] = fine_x[first:last, fine_at : fine_at + 4, :]
        at = (cells_x + 8) // 4
        for part, first, last, top, left in quarters(mx + 11, at, mz):
            buf[part, top : top + 7, left : left + mz] = mid_x[first:last, mid_at : mid_at + 7, :]
        at += -(-(mx + 11) // 4)
        buf[at:, 0:9, :] = two_halves(pair_lanes(coarse_x[:, 0:9, :]))
        out[...] = buf[...].astype(BF16)

    flag = up_first("gy", 1, 1)

    @pl.when(flag)
    def _():
        pack(first_out, cells_y, my - 4)
        pack(second_out, 4, 0)

    @pl.when(jnp.logical_not(flag))
    def _():
        pack(first_out, 4, 0)
        pack(second_out, cells_y, my - 4)


def join_y_kernel(at, mid_x, coarse_x, first_in, second_in, mid_xy, coarse_xy, first_out, second_out, low, high, buf, side):
    my, cy = mid_x.shape[1] // 2, mid_x.shape[1] // 4
    rows_m, rows_c = mid_x.shape[0], coarse_x.shape[0]
    mz, cz = mid_x.shape[2], coarse_x.shape[2]
    low[...], high[...] = by_order(up_first("gy", 1, 1), first_in[...].astype(F32), second_in[...].astype(F32))
    mid_xy[...] = jnp.zeros_like(mid_xy)
    mid_xy[:, 4 : 7 + my, :] = mid_x[:, 0 : my + 3, :]
    for part, first, last, top, left in quarters(rows_m, at, mz):
        mid_xy[first:last, 0:7, :] += low[part, top : top + 7, left : left + mz]
        mid_xy[first:last, 4 + my : 11 + my, :] += high[part, top : top + 7, left : left + mz]
    at += -(-rows_m // 4)
    from_low = unpair(from_halves(low[at:, 0:9, :], rows_c), cz)
    from_high = unpair(from_halves(high[at:, 0:9, :], rows_c), cz)
    side[...] = jnp.zeros_like(side)
    side[:, 4 : 9 + cy, :] = coarse_x[:, 0 : cy + 5, :]
    coarse_xy[...] = side[...]
    coarse_xy[:, 0:9, :] += from_low
    buf[...] = jnp.zeros_like(buf)

    def pack(rows, out):
        rows = pair_lanes(rows)
        for part, first, last, top, left in quarters(rows_c, 0, 2 * cz):
            buf[part, top : top + 5, left : left + 2 * cz] = rows[first:last]
        out[...] = buf[...].astype(BF16)

    up = coarse_xy[:, 4 + cy : 9 + cy, :]
    coarse_xy[:, 4 + cy : 13 + cy, :] += from_high
    side[:, 4 + cy : 13 + cy, :] += from_high
    down = side[:, 4:9, :]
    flag = up_first("gy", 2, 0)
    pack(jnp.where(flag, up, down), first_out)
    pack(jnp.where(flag, down, up), second_out)


def bands_kernel(begin, levels, lines, *refs):
    outs, joint, last, turned = refs[:-3], refs[-3], refs[-2], refs[-1]
    tap = lax.broadcasted_iota(jnp.int32, (HALF, HALF), 0)
    place = lax.broadcasted_iota(jnp.int32, (HALF, HALF), 1)
    reverse = ((tap <= 8) & (place == jnp.where(tap <= 4, 4 - tap, HALF + 4 - tap))).astype(F32).astype(BF16)
    n = len(levels)
    flat = lines[9 * begin : 9 * (begin + n)].reshape(n * 9 * 16, HALF).astype(BF16)
    values = jnp.dot(flat, reverse, preferred_element_type=F32).reshape(n * 9, 16, HALF)
    turned[...] = pltpu.roll(values, 0, 2, stride=16, stride_axis=1)
    joint[...] = jnp.broadcast_to(jnp.sum(turned[:, 0:8, :], axis=1, keepdims=True), joint.shape)
    ninth = [turned[9 * i : 9 * i + 9, 8:9, :] for i in range(n)]
    ninth = functools.reduce(jnp.add, [pltpu.roll(v, 16 * i, 2) if i else v for i, v in enumerate(ninth)])
    last[...] = jnp.broadcast_to(ninth, last.shape)
    lane = lax.broadcasted_iota(jnp.int32, (8, HALF), 1)

    def one_dx(dx, carry):
        def turns(line):
            return [pltpu.roll(line, 8 * r, 1, stride=1, stride_axis=0) for r in range(16)]

        ninths = turns(last[dx])
        for level, ((depth, groups), out) in enumerate(zip(levels, outs)):
            per, steps = HALF // depth, depth // 8
            eights = turns(joint[9 * level + dx])
            for offset in range(2 * groups - 1):
                rows = []
                for a in range(per):
                    for g in range(steps):
                        full = jnp.zeros((8, HALF), F32)
                        for b in range(per):
                            line = per * offset + a - b
                            at = steps * b + g
                            if 0 <= line <= 8:
                                part = ninths[(at - 2 * level) % 16] if line == 8 else eights[(at - 2 * line) % 16]
                                full = part if per == 1 else jnp.where(lane // depth == b, part, full)
                        apart = lax.rem(lane, depth) - 8 * g - lax.broadcasted_iota(jnp.int32, (8, HALF), 0)
                        rows.append(jnp.where((apart <= 4) & (apart >= -4), full, 0.0))
                out[dx, offset] = jnp.concatenate(rows, axis=0).astype(BF16)
        return carry

    lax.fori_loop(0, 9, one_dx, 0)


def bands(lines, begin, levels, after=()):
    n = len(levels) * 9
    return call(
        functools.partial(bands_kernel, begin, levels),
        [((9, 2 * groups - 1, HALF, HALF), BF16) for _, groups in levels],
        [lines],
        [((n, 8, HALF), F32), ((9, 8, HALF), F32), ((n, 16, HALF), F32)],
        flops=10**9,
        after=after,
    )


def weights_of(blocks, dx):
    count = blocks.shape[1]
    zero = jnp.zeros((HALF, HALF), BF16)

    def block(offset):
        return blocks[dx, offset] if 0 <= offset < count else zero

    halves = range(count + 1)
    return jnp.concatenate([jnp.concatenate([block(h), block(h - 1)], axis=1) for h in halves], axis=0)


def gather_rows(field, rows, per, groups, depth, lhs):
    for parity in (0, 1):
        count = rows - parity
        for group in range(groups):
            for a in range(per):
                lane = group * WIDE + a * depth
                part = field[parity:rows, pl.ds(a + per * group, 8, stride=per), :]
                lhs[parity, 0 : count * 8, lane : lane + depth] = part.reshape(count * 8, depth).astype(BF16)


def gather_staged(field, rows, per, groups, depth, stage, lhs):
    count = field.shape[1] // per
    stage[...] = jnp.zeros_like(stage)
    for a in range(per):
        stage[:, 0:count, a * depth : (a + 1) * depth] = field[:, pl.ds(a, count, stride=per), :]
    for parity in (0, 1):
        n = (rows - parity) * 8
        for group in range(groups):
            part = stage[parity:rows, group : group + 8, :].reshape(n, WIDE)
            lhs[parity, 0:n, group * WIDE : (group + 1) * WIDE] = part.astype(BF16)


def convolve(lhs, weights, out_rows, acc):
    n = out_rows * 8
    for dx in range(9):
        start = 16 * (dx // 2)
        part = jnp.dot(lhs[dx % 2, start : start + n, :], weights_of(weights, dx), preferred_element_type=F32)
        acc[...] = part if dx == 0 else acc[...] + part


def own_kernel(fine_x, weights, acc, lhs):
    rows = fine_x.shape[0]
    gather_rows(fine_x, rows, 2, 5, fine_x.shape[2], lhs)
    convolve(lhs, weights, rows - 8, acc)


def group_weights(blocks, dx, group):
    return weights_of(blocks, dx)[group * WIDE : (group + 1) * WIDE]


def rim_kernel(first_in, second_in, mid_xy, own, fine_w, mid_w, fine_acc, mid_acc, rim, stage_f, lhs_f, stage, mid_lhs, sums):
    cells_x = own.shape[0] // 8
    quarter = cells_x // 4
    tiles = rim.shape[1]
    rim[0], rim[1] = by_order(up_first("gy", 1, 1), *(v[0:tiles].astype(F32) for v in (first_in, second_in)))
    for side in (0, 1):
        for q in range(4):
            for r in range(4):
                first, last = max(quarter * q, tiles * r), min(quarter * q + quarter + 8, tiles * r + tiles)
                if first < last:
                    to = slice(first - quarter * q, last - quarter * q)
                    source_rows = slice(first - tiles * r, last - tiles * r)
                    for a in (0, 1):
                        part = rim[side, source_rows, pl.ds(4 * r + a, 2, stride=2), :]
                        stage_f[side, to, 2 * q : 2 * q + 2, a * HALF : (a + 1) * HALF] = part
        for parity in (0, 1):
            n = quarter + 8 - parity
            lhs_f[side, parity, 0 : 8 * n, :] = stage_f[side, parity : parity + n].reshape(8 * n, WIDE).astype(BF16)
    n = quarter * 8
    for dx in range(9):
        start = 16 * (dx // 2)
        for i, (side, group) in enumerate(((0, 0), (0, 1), (1, 3), (1, 4))):
            rows = lhs_f[side, dx % 2, start : start + n, :]
            part = jnp.dot(rows, group_weights(fine_w, dx, group), preferred_element_type=F32)
            sums[i] = part if dx == 0 else sums[i] + part
    rows = mid_xy.shape[0]
    gather_staged(mid_xy, rows, 4, 3, mid_xy.shape[2], stage, mid_lhs)
    convolve(mid_lhs, mid_w, rows - 8, mid_acc)
    fine_acc[...] = own[...].reshape(fine_acc.shape)
    near, far, far_right, near_right = (sums[i].reshape(quarter, 8, WIDE) for i in range(4))
    odd = lax.rem(lax.broadcasted_iota(jnp.int32, near.shape, 1), 2) == 1
    stage_f[0, 0:quarter] = near + jnp.where(odd, 0.0, pltpu.roll(far, 7, 1))
    stage_f[1, 0:quarter] = near_right + jnp.where(odd, pltpu.roll(far_right, 1, 1), 0.0)
    for q in range(4):
        at = slice(quarter * q, quarter * q + quarter)
        fine_acc[at, 0:2, :] += stage_f[0, 0:quarter, 2 * q : 2 * q + 2, :]
        fine_acc[at, 6:8, :] += stage_f[1, 0:quarter, 2 * q : 2 * q + 2, :]


def prolong_odd(a, b, c, d):
    return 0.5625 * (b + c) - 0.0625 * (a + d)


def finish_kernel(
    counts, coarse_xy, first_in, second_in, coarse_w, fine_acc, mid_acc, out,
    crs_pad, stage, crs_lhs, crs_acc, msg, crs_pot, wide, mid_tot,
):
    gx, gy = lax.axis_index("gx"), lax.axis_index("gy")
    nx, ny = counts
    rows_c, _, cz = coarse_xy.shape
    cells_x, cells_y, cells_z = out.shape
    mx, my, mz = cells_x // 2, cells_y // 2, cells_z // 2
    cx, cy = cells_x // 4, cells_y // 4
    crs_pad[...] = coarse_xy[...]
    received = by_order(up_first("gy", 2, 0), *(v[...].astype(F32) for v in (first_in, second_in)))
    for source, at in zip(received, (0, cy + 8)):
        msg[...] = source
        for part, first, last, top, left in quarters(rows_c, 0, 2 * cz):
            crs_pad[first:last, at : at + 5, :] += unpair(msg[part, top : top + 5, left : left + 2 * cz], cz)
    gather_staged(crs_pad, rows_c, 8, 2, cz, stage, crs_lhs)
    convolve(crs_lhs, coarse_w, rows_c - 8, crs_acc)
    rows = rows_c - 8
    pot = crs_acc[...].reshape(rows, 8, WIDE)
    for b in range(8):
        crs_pot[:, pl.ds(b, 2, stride=8), :] = pot[:, 0:2, b * cz : (b + 1) * cz]
    pot = crs_pot[...]
    keep = inside(pot.shape, 0, -2, cx, gx, nx) & inside(pot.shape, 1, -2, cy, gy, ny)
    pot = jnp.where(keep, pot, 0.0)
    n = cx + 2
    odd = prolong_odd(*(pot[s : s + n] for s in range(4)))
    even = jnp.concatenate([pot[2 : 1 + n], jnp.zeros_like(pot[:1])], axis=0) if n + 2 > rows else pot[2 : 2 + n]
    wide[:, 0] = odd
    wide[:, 1] = even
    wide_y = cy + 2
    v = wide[...].reshape((2 * n,) + pot.shape[1:])
    mid_tot[...] = jnp.zeros_like(mid_tot)
    odd = prolong_odd(*(v[:, s : s + wide_y] for s in range(4)))
    even = v[:, 2 : 1 + wide_y]
    matrix = transfer_matrix(mz, cz, True)
    mid_tot[:, pl.ds(0, wide_y, stride=2), 0:cz] = odd
    mid_tot[:, pl.ds(1, wide_y - 1, stride=2), 0:cz] = even
    total = dot_last(mid_tot[:, :, 0:cz], matrix)
    rows = mx + 3
    pot = mid_acc[...].reshape(rows, 8, WIDE)
    for b in range(4):
        mid_tot[0:rows, pl.ds(b, 3, stride=4), :] = pot[:, 0:3, b * mz : (b + 1) * mz]
    total = mid_tot[0:rows] + total[0:rows]
    keep = inside(total.shape, 0, -1, mx, gx, nx) & inside(total.shape, 1, -1, my, gy, ny)
    mid_tot[0:rows] = jnp.where(keep, total, 0.0)
    matrix = transfer_matrix(cells_z, mz, True)
    pot = fine_acc[...]
    for a in (0, 1):
        if a == 0:
            u = mid_tot[0:rows, 1 : 1 + my, :]
        else:
            u = prolong_odd(*(mid_tot[0:rows, s : s + my, :] for s in range(4)))
        u = dot_last(u, matrix)
        odd = prolong_odd(*(u[s : s + mx] for s in range(4)))
        both = jnp.stack([u[1 : 1 + mx], odd], axis=1).reshape(cells_x, my, cells_z)
        out[:, pl.ds(a, my, stride=2), :] = pot[:, :, a * HALF : a * HALF + cells_z] + both


def whole():
    return pl.BlockSpec(memory_space=pltpu.VMEM)


def call(kernel, outs, ins, scratch, flops=10**8, vmem_out=True, after=(), space=pltpu.VMEM, sems=0, limit=VMEM_LIMIT):
    n = len(ins)

    def body(*refs):
        kernel(*refs[:n], *refs[n + len(after) :])

    return pl.pallas_call(
        body,
        out_shape=[pltpu.VMEM(s, d) for s, d in outs] if vmem_out else [jax.ShapeDtypeStruct(s, d) for s, d in outs],
        in_specs=[pl.BlockSpec(memory_space=space)] * n + [pl.BlockSpec(memory_space=pl.ANY)] * len(after),
        out_specs=[whole()] * len(outs),
        scratch_shapes=[pltpu.VMEM(s, d) for s, d in scratch] + [pltpu.SemaphoreType.DMA((sems,))] * (sems > 0),
        compiler_params=pltpu.CompilerParams(vmem_limit_bytes=limit),
        cost_estimate=pl.CostEstimate(flops=flops, bytes_accessed=10**6, transcendentals=0),
    )(*ins, *after)


def swap(first, second, axis, step, size, start):
    received = []
    for message, group in ((first, start), (second, 1 - start)):
        lower = [i for i in range(size - step) if (i // step) % 2 == group]
        pairs = [(i, i + step) for i in lower] + [(i + step, i) for i in lower]
        received.append(lax.ppermute(message, axis, pairs))
    return received


def up_first(axis, step, start):
    return lax.rem(lax.axis_index(axis) // step, 2) == start


def by_order(flag, first, second):
    return jnp.where(flag, second, first), jnp.where(flag, first, second)


def local(counts, charges, kernel_fine, kernel_mid, kernel_coarse):
    nx, ny = counts
    cells_x, cells_y, cells_z = charges.shape
    mx, mz, cx, cz = cells_x // 2, cells_z // 2, cells_x // 4, cells_z // 4
    frame = cells_y
    lines = ((27, 16, HALF), F32)
    message = ((13, frame, cells_z), BF16)
    first, second, fine_own, mid_own, coarse_own, lines = call(
        functools.partial(spread_kernel, counts),
        [message, message, (charges.shape, BF16), ((mx + 3, frame, mz), F32), ((cx + 5, frame, cz), F32), lines],
        [charges, kernel_fine, kernel_mid, kernel_coarse],
        [
            ((mx + 3, frame + 24, mz), F32),
            ((mx + 3, frame + 24, mz), F32),
            ((cx + 5, frame, mz), F32),
            (charges.shape, F32),
        ]
        + [((9, 9, 9), BF16)] * 3,
        space=pltpu.HBM,
        sems=4,
        limit=60 * 1024 * 1024,
    )
    first, second = swap(first, second, "gx", 1, nx, 1)
    fine_w, mid_w, coarse_w = bands(lines, 0, ((cells_z, 5), (mz, 3), (cz, 2)))
    rows = (cells_x + 8) // 4 + (mx + 14) // 4 + (cx + 14) // 2
    packed = ((rows, frame, cells_z), BF16)
    fine_x, mid_x, coarse_x, first, second = call(
        join_x_kernel,
        [
            ((cells_x + 8, cells_y + 8, cells_z), F32),
            ((mx + 11, frame, mz), F32),
            ((cx + 13, frame, cz), F32),
            packed,
            packed,
        ],
        [fine_own, mid_own, coarse_own, first, second],
        [((rows, frame, cells_z), F32)],
        after=(fine_w,),
    )
    first, second = swap(first, second, "gy", 1, ny, 1)
    (own_acc,) = call(
        own_kernel,
        [((cells_x * 8, WIDE), F32)],
        [fine_x, fine_w],
        [((2, (cells_x + 8) * 8, 5 * WIDE), BF16)],
        flops=10**9,
    )
    half = (cx + 16) // 4
    message = ((half, frame, cells_z), BF16)
    mid_xy, coarse_xy, last_first, last_second = call(
        functools.partial(join_y_kernel, (cells_x + 8) // 4),
        [
            ((mx + 11, frame + 8, mz), F32),
            ((cx + 13, frame + 8, cz), F32),
            message,
            message,
        ],
        [mid_x, coarse_x, first, second],
        [
            ((rows, frame, cells_z), F32),
            ((rows, frame, cells_z), F32),
            ((half, frame, cells_z), F32),
            ((cx + 13, frame + 8, cz), F32),
        ],
        after=(own_acc,),
    )
    last_first, last_second = swap(last_first, last_second, "gy", 2, ny, 0)
    quarter = cells_x // 4
    fine_acc, mid_acc = call(
        rim_kernel,
        [((cells_x, 8, WIDE), F32), (((mx + 3) * 8, WIDE), F32)],
        [first, second, mid_xy, own_acc, fine_w, mid_w],
        [
            ((2, (cells_x + 8) // 4, frame, cells_z), F32),
            ((2, quarter + 8, 8, WIDE), F32),
            ((2, 2, (quarter + 8) * 8, WIDE), BF16),
            ((mx + 11, 16, WIDE), F32),
            ((2, (mx + 12) * 8, 3 * WIDE), BF16),
            ((4, quarter * 8, WIDE), F32),
        ],
        flops=10**9,
    )
    (out,) = call(
        functools.partial(finish_kernel, counts),
        [(charges.shape, F32)],
        [coarse_xy, last_first, last_second, coarse_w, fine_acc, mid_acc],
        [
            ((cx + 13, frame + 8, cz), F32),
            ((cx + 13, 16, WIDE), F32),
            ((2, (cx + 14) * 8, 2 * WIDE), BF16),
            (((cx + 5) * 8, WIDE), F32),
            ((half, frame, cells_z), F32),
            ((cx + 5, 16, cz), F32),
            ((cx + 2, 2, 16, cz), F32),
            ((mx + 4, 16, mz), F32),
        ],
        vmem_out=False,
    )
    return out


def solution(mesh):
    counts = (mesh.shape["gx"], mesh.shape["gy"])
    placed = (P("gx", "gy", None), P(), P(), P())
    return jax.shard_map(
        functools.partial(local, counts),
        mesh=mesh,
        in_specs=placed,
        out_specs=P("gx", "gy", None),
        check_vma=False,
    )
```

```python
import functools

import jax
import jax.numpy as jnp
from jax import lax
from jax.experimental import pallas as pl
from jax.experimental.pallas import tpu as pltpu
from jax.sharding import PartitionSpec as P

F32 = jnp.float32
BF16 = jnp.bfloat16
WIDE = 256
HALF = 128
VMEM_LIMIT = 14 * 1024 * 1024


def split_pair(v):
    high = v.astype(BF16).astype(F32)
    low = (v - high).astype(BF16).astype(F32)
    return high, low


def pair_lanes(v):
    return jnp.concatenate(split_pair(v), axis=-1)


def exact_dot(v, matrix):
    high, low = split_pair(v)
    return jnp.dot(high.astype(BF16), matrix, preferred_element_type=F32) + jnp.dot(
        low.astype(BF16), matrix, preferred_element_type=F32
    )


def transfer_matrix(fine, coarse, transpose):
    shape = (coarse, fine) if transpose else (fine, coarse)
    fine_at = lax.broadcasted_iota(jnp.int32, shape, 1 if transpose else 0)
    coarse_at = lax.broadcasted_iota(jnp.int32, shape, 0 if transpose else 1)
    d = fine_at - 2 * coarse_at
    one = jnp.where(d == 0, F32(1.0), F32(0.0))
    near = jnp.where((d == 1) | (d == -1), F32(0.5625), F32(0.0))
    far = jnp.where((d == 3) | (d == -3), F32(-0.0625), F32(0.0))
    return (one + near + far).astype(BF16)


def dot_last(v, matrix):
    lead = v.shape[:-1]
    return exact_dot(v.reshape(-1, v.shape[-1]), matrix).reshape(lead + (matrix.shape[1],))


def rows_at(v, first, low, count):
    begin, end = low - first, low - first + count
    inner = v[max(begin, 0) : min(end, v.shape[0])]
    parts = []
    if begin < 0:
        parts.append(jnp.zeros((-begin,) + v.shape[1:], v.dtype))
    parts.append(inner)
    if end > v.shape[0]:
        parts.append(jnp.zeros((end - v.shape[0],) + v.shape[1:], v.dtype))
    return jnp.concatenate(parts, axis=0) if len(parts) > 1 else inner


def weigh_restrict(even, odd0, odd_m1, odd_p1, odd_m2):
    return even + 0.5625 * (odd0 + odd_m1) - 0.0625 * (odd_p1 + odd_m2)


def restrict_rows(even, even_at, odd, odd_at, low, count):
    return weigh_restrict(
        rows_at(even, even_at, low, count),
        *(rows_at(odd, odd_at, low + s, count) for s in (0, -1, 1, -2)),
    )


def pairs_of_rows(v):
    v = v.reshape((v.shape[0] // 2, 2) + v.shape[1:])
    return v[:, 0], v[:, 1]


def inside(shape, axis, first, cells, index, count):
    at = lax.broadcasted_iota(jnp.int32, shape, axis) + first
    return ((at >= 0) | (index > 0)) & ((at < cells) | (index < count - 1))


def spread_kernel(counts, *refs):
    outside, (first_out, second_out, fine_own, mid_own, coarse_own, lines) = refs[0:4], refs[4:10]
    (even_pad, odd_pad, crs, charges), raws, sems = refs[10:14], refs[14:17], refs[17]
    copies = [
        pltpu.make_async_copy(source, target, sems.at[i])
        for i, (source, target) in enumerate(zip(outside, (charges,) + raws))
    ]
    for copy in copies:
        copy.start()
    even_pad[...] = jnp.zeros_like(even_pad)
    odd_pad[...] = jnp.zeros_like(odd_pad)
    lines[...] = jnp.zeros_like(lines)
    copies[0].wait()
    fine_own[...] = charges[...].astype(BF16)
    gx, gy = lax.axis_index("gx"), lax.axis_index("gy")
    nx, ny = counts
    cells_x, cells_y, cells_z = charges.shape
    mx, my, mz = cells_x // 2, cells_y // 2, cells_z // 2
    cx, cy, cz = cells_x // 4, cells_y // 4, cells_z // 4
    frame = mid_own.shape[1]
    even, odd = pairs_of_rows(charges[...])
    mid = restrict_rows(even, 0, odd, 0, -1, mx + 3)
    mid = dot_last(mid, transfer_matrix(cells_z, mz, False))
    mid_own[...] = mid
    even_pad[:, 8 : 8 + my] = mid_own[:, pl.ds(0, my, stride=2), :]
    odd_pad[:, 8 : 8 + my] = mid_own[:, pl.ds(1, my, stride=2), :]
    mid = weigh_restrict(
        even_pad[:, 7 : 7 + frame],
        *(odd_pad[:, 7 + s : 7 + s + frame] for s in (0, -1, 1, -2)),
    )
    keep = inside(mid.shape, 0, -1, mx, gx, nx) & inside(mid.shape, 1, -1, my, gy, ny)
    mid = jnp.where(keep, mid, 0.0)
    mid_own[...] = mid
    odd, even = pairs_of_rows(jnp.concatenate([mid, jnp.zeros_like(mid[:1])], axis=0))
    crs[...] = restrict_rows(even, 0, odd, -1, -2, cx + 5)
    n = cx + 5
    odd_pad[:n, 8 : 8 + frame // 2] = crs[:, pl.ds(0, frame // 2, stride=2), :]
    even_pad[:n, 8 : 8 + frame // 2] = crs[:, pl.ds(1, frame // 2, stride=2), :]
    coarse = weigh_restrict(
        even_pad[:n, 6 : 6 + frame],
        *(odd_pad[:n, 7 + s : 7 + s + frame] for s in (0, -1, 1, -2)),
    )
    coarse = dot_last(coarse, transfer_matrix(mz, cz, False))
    keep = inside(coarse.shape, 0, -2, cx, gx, nx) & inside(coarse.shape, 1, -2, cy, gy, ny)
    coarse = jnp.where(keep, coarse, 0.0)
    coarse_own[...] = coarse
    def pack(out, fine_at, mid_at, coarse_at):
        out[0:4] = charges[fine_at : fine_at + 4].astype(BF16)
        out[4:8] = two_halves(mid_own[mid_at : mid_at + 7]).astype(BF16)
        out[8:13] = two_halves(pair_lanes(coarse_own[coarse_at : coarse_at + 9])).astype(BF16)

    flag = up_first("gx", 1, 1)

    @pl.when(flag)
    def _():
        pack(first_out, cells_x - 4, mx - 4, cx - 4)
        pack(second_out, 0, 0, 0)

    @pl.when(jnp.logical_not(flag))
    def _():
        pack(first_out, 0, 0, 0)
        pack(second_out, cells_x - 4, mx - 4, cx - 4)

    for i, raw in enumerate(raws):
        copies[i + 1].wait()
        lines[9 * i : 9 * i + 9, 0:9, 0:9] = raw[...].astype(F32)


def two_halves(v):
    half = (v.shape[0] + 1) // 2
    return jnp.concatenate([v[:half], rows_at(v, 0, half, half)], axis=-1)


def unpair(v, width):
    return v[..., :width] + v[..., width : 2 * width]


def from_halves(v, count):
    lanes = v.shape[-1] // 2
    return jnp.concatenate([v[..., :lanes], v[: count - v.shape[0], :, lanes:]], axis=0)


def fine_parts(rows):
    q = rows // 4
    return [(slice(0, q), q * r, q * r + q, 4 * r, 0) for r in range(4)]


def quarters(rows, at, lanes):
    q = -(-rows // 4)
    parts = []
    for r in range(4):
        first, last = q * r, min(q * r + q, rows)
        parts.append((slice(at, at + last - first), first, last, 8 * (r // 2), lanes * (r % 2)))
    return parts


def join_x_kernel(charges, mid_own, coarse_own, first_in, second_in, fine_x, mid_x, coarse_x, first_out, second_out, buf):
    before, after = by_order(up_first("gx", 1, 1), *(v[...].astype(F32) for v in (first_in, second_in)))
    cells_x, cells_y, _ = charges.shape
    mx, cx = cells_x // 2, cells_x // 4
    mz, cz = mid_own.shape[2], coarse_own.shape[2]
    my = cells_y // 2
    rows_x = cells_x + 8
    own = slice(4, 4 + cells_y)
    for edge in (0, 4 + cells_y):
        fine_x[:, edge : edge + 4, :] = jnp.zeros((rows_x, 4, charges.shape[2]), F32)
    fine_x[0:4, own, :] = before[0:4]
    fine_x[4 : 4 + cells_x, own, :] = charges[...].astype(F32)
    fine_x[4 + cells_x : rows_x, own, :] = after[0:4]
    low, high = (from_halves(m[4:8], 7) for m in (before, after))
    mid = (
        rows_at(mid_own[...], -1, -5, mx + 11)
        + rows_at(low, -5, -5, mx + 11)
        + rows_at(high, mx - 1, -5, mx + 11)
    )
    mid_x[...] = mid
    low, high = (from_halves(m[8:13], 9) for m in (before, after))
    coarse = (
        rows_at(coarse_own[...], -2, -6, cx + 13)
        + rows_at(unpair(low, cz), -6, -6, cx + 13)
        + rows_at(unpair(high, cz), cx - 2, -6, cx + 13)
    )
    coarse_x[...] = coarse
    buf[...] = jnp.zeros_like(buf)

    def pack(out, fine_at, mid_at):
        for part, first, last, top, left in fine_parts(cells_x + 8):
            buf[part, top : top + 4, left:] = fine_x[first:last, fine_at : fine_at + 4, :]
        at = (cells_x + 8) // 4
        for part, first, last, top, left in quarters(mx + 11, at, mz):
            buf[part, top : top + 7, left : left + mz] = mid_x[first:last, mid_at : mid_at + 7, :]
        at += -(-(mx + 11) // 4)
        buf[at:, 0:9, :] = two_halves(pair_lanes(coarse_x[:, 0:9, :]))
        out[...] = buf[...].astype(BF16)

    flag = up_first("gy", 1, 1)

    @pl.when(flag)
    def _():
        pack(first_out, cells_y, my - 4)
        pack(second_out, 4, 0)

    @pl.when(jnp.logical_not(flag))
    def _():
        pack(first_out, 4, 0)
        pack(second_out, cells_y, my - 4)


def join_y_kernel(at, mid_x, coarse_x, first_in, second_in, mid_xy, coarse_xy, first_out, second_out, low, high, buf, side):
    my, cy = mid_x.shape[1] // 2, mid_x.shape[1] // 4
    rows_m, rows_c = mid_x.shape[0], coarse_x.shape[0]
    mz, cz = mid_x.shape[2], coarse_x.shape[2]
    low[...], high[...] = by_order(up_first("gy", 1, 1), first_in[...].astype(F32), second_in[...].astype(F32))
    mid_xy[...] = jnp.zeros_like(mid_xy)
    mid_xy[:, 4 : 7 + my, :] = mid_x[:, 0 : my + 3, :]
    for part, first, last, top, left in quarters(rows_m, at, mz):
        mid_xy[first:last, 0:7, :] += low[part, top : top + 7, left : left + mz]
        mid_xy[first:last, 4 + my : 11 + my, :] += high[part, top : top + 7, left : left + mz]
    at += -(-rows_m // 4)
    from_low = unpair(from_halves(low[at:, 0:9, :], rows_c), cz)
    from_high = unpair(from_halves(high[at:, 0:9, :], rows_c), cz)
    side[...] = jnp.zeros_like(side)
    side[:, 4 : 9 + cy, :] = coarse_x[:, 0 : cy + 5, :]
    coarse_xy[...] = side[...]
    coarse_xy[:, 0:9, :] += from_low
    buf[...] = jnp.zeros_like(buf)

    def pack(rows, out):
        rows = pair_lanes(rows)
        for part, first, last, top, left in quarters(rows_c, 0, 2 * cz):
            buf[part, top : top + 5, left : left + 2 * cz] = rows[first:last]
        out[...] = buf[...].astype(BF16)

    up = coarse_xy[:, 4 + cy : 9 + cy, :]
    coarse_xy[:, 4 + cy : 13 + cy, :] += from_high
    side[:, 4 + cy : 13 + cy, :] += from_high
    down = side[:, 4:9, :]
    flag = up_first("gy", 2, 0)
    pack(jnp.where(flag, up, down), first_out)
    pack(jnp.where(flag, down, up), second_out)


def bands_kernel(begin, levels, lines, *refs):
    outs, joint, last, turned = refs[:-3], refs[-3], refs[-2], refs[-1]
    tap = lax.broadcasted_iota(jnp.int32, (HALF, HALF), 0)
    place = lax.broadcasted_iota(jnp.int32, (HALF, HALF), 1)
    reverse = ((tap <= 8) & (place == jnp.where(tap <= 4, 4 - tap, HALF + 4 - tap))).astype(F32).astype(BF16)
    n = len(levels)
    flat = lines[9 * begin : 9 * (begin + n)].reshape(n * 9 * 16, HALF).astype(BF16)
    values = jnp.dot(flat, reverse, preferred_element_type=F32).reshape(n * 9, 16, HALF)
    turned[...] = pltpu.roll(values, 0, 2, stride=16, stride_axis=1)
    joint[...] = jnp.broadcast_to(jnp.sum(turned[:, 0:8, :], axis=1, keepdims=True), joint.shape)
    ninth = [turned[9 * i : 9 * i + 9, 8:9, :] for i in range(n)]
    ninth = functools.reduce(jnp.add, [pltpu.roll(v, 16 * i, 2) if i else v for i, v in enumerate(ninth)])
    last[...] = jnp.broadcast_to(ninth, last.shape)
    lane = lax.broadcasted_iota(jnp.int32, (8, HALF), 1)

    def one_dx(dx, carry):
        def turns(line):
            return [pltpu.roll(line, 8 * r, 1, stride=1, stride_axis=0) for r in range(16)]

        ninths = turns(last[dx])
        for level, ((depth, groups), out) in enumerate(zip(levels, outs)):
            per, steps = HALF // depth, depth // 8
            eights = turns(joint[9 * level + dx])
            for offset in range(2 * groups - 1):
                rows = []
                for a in range(per):
                    for g in range(steps):
                        full = jnp.zeros((8, HALF), F32)
                        for b in range(per):
                            line = per * offset + a - b
                            at = steps * b + g
                            if 0 <= line <= 8:
                                part = ninths[(at - 2 * level) % 16] if line == 8 else eights[(at - 2 * line) % 16]
                                full = part if per == 1 else jnp.where(lane // depth == b, part, full)
                        apart = lax.rem(lane, depth) - 8 * g - lax.broadcasted_iota(jnp.int32, (8, HALF), 0)
                        rows.append(jnp.where((apart <= 4) & (apart >= -4), full, 0.0))
                out[dx, offset] = jnp.concatenate(rows, axis=0).astype(BF16)
        return carry

    lax.fori_loop(0, 9, one_dx, 0)


def bands(lines, begin, levels, after=()):
    n = len(levels) * 9
    return call(
        functools.partial(bands_kernel, begin, levels),
        [((9, 2 * groups - 1, HALF, HALF), BF16) for _, groups in levels],
        [lines],
        [((n, 8, HALF), F32), ((9, 8, HALF), F32), ((n, 16, HALF), F32)],
        flops=10**9,
        after=after,
    )


def weights_of(blocks, dx):
    count = blocks.shape[1]
    zero = jnp.zeros((HALF, HALF), BF16)

    def block(offset):
        return blocks[dx, offset] if 0 <= offset < count else zero

    halves = range(count + 1)
    return jnp.concatenate([jnp.concatenate([block(h), block(h - 1)], axis=1) for h in halves], axis=0)


def gather_rows(field, rows, per, groups, depth, lhs):
    for parity in (0, 1):
        count = rows - parity
        for group in range(groups):
            for a in range(per):
                lane = group * WIDE + a * depth
                part = field[parity:rows, pl.ds(a + per * group, 8, stride=per), :]
                lhs[parity, 0 : count * 8, lane : lane + depth] = part.reshape(count * 8, depth).astype(BF16)


def gather_staged(field, rows, per, groups, depth, stage, lhs):
    count = field.shape[1] // per
    stage[...] = jnp.zeros_like(stage)
    for a in range(per):
        stage[:, 0:count, a * depth : (a + 1) * depth] = field[:, pl.ds(a, count, stride=per), :]
    for parity in (0, 1):
        n = (rows - parity) * 8
        for group in range(groups):
            part = stage[parity:rows, group : group + 8, :].reshape(n, WIDE)
            lhs[parity, 0:n, group * WIDE : (group + 1) * WIDE] = part.astype(BF16)


def convolve(lhs, weights, out_rows, acc):
    n = out_rows * 8
    for dx in range(9):
        start = 16 * (dx // 2)
        part = jnp.dot(lhs[dx % 2, start : start + n, :], weights_of(weights, dx), preferred_element_type=F32)
        acc[...] = part if dx == 0 else acc[...] + part


def own_kernel(fine_x, weights, acc, lhs):
    rows = fine_x.shape[0]
    gather_rows(fine_x, rows, 2, 5, fine_x.shape[2], lhs)
    convolve(lhs, weights, rows - 8, acc)


def group_weights(blocks, dx, group):
    return weights_of(blocks, dx)[group * WIDE : (group + 1) * WIDE]


def rim_kernel(first_in, second_in, mid_xy, own, fine_w, mid_w, fine_acc, mid_acc, rim, stage_f, lhs_f, stage, mid_lhs, sums):
    cells_x = own.shape[0] // 8
    quarter = cells_x // 4
    tiles = rim.shape[1]
    rim[0], rim[1] = by_order(up_first("gy", 1, 1), *(v[0:tiles].astype(F32) for v in (first_in, second_in)))
    for side in (0, 1):
        for q in range(4):
            for r in range(4):
                first, last = max(quarter * q, tiles * r), min(quarter * q + quarter + 8, tiles * r + tiles)
                if first < last:
                    to = slice(first - quarter * q, last - quarter * q)
                    source_rows = slice(first - tiles * r, last - tiles * r)
                    for a in (0, 1):
                        part = rim[side, source_rows, pl.ds(4 * r + a, 2, stride=2), :]
                        stage_f[side, to, 2 * q : 2 * q + 2, a * HALF : (a + 1) * HALF] = part
        for parity in (0, 1):
            n = quarter + 8 - parity
            lhs_f[side, parity, 0 : 8 * n, :] = stage_f[side, parity : parity + n].reshape(8 * n, WIDE).astype(BF16)
    n = quarter * 8
    for dx in range(9):
        start = 16 * (dx // 2)
        for i, (side, group) in enumerate(((0, 0), (0, 1), (1, 3), (1, 4))):
            rows = lhs_f[side, dx % 2, start : start + n, :]
            part = jnp.dot(rows, group_weights(fine_w, dx, group), preferred_element_type=F32)
            sums[i] = part if dx == 0 else sums[i] + part
    rows = mid_xy.shape[0]
    gather_staged(mid_xy, rows, 4, 3, mid_xy.shape[2], stage, mid_lhs)
    convolve(mid_lhs, mid_w, rows - 8, mid_acc)
    fine_acc[...] = own[...].reshape(fine_acc.shape)
    near, far, far_right, near_right = (sums[i].reshape(quarter, 8, WIDE) for i in range(4))
    odd = lax.rem(lax.broadcasted_iota(jnp.int32, near.shape, 1), 2) == 1
    stage_f[0, 0:quarter] = near + jnp.where(odd, 0.0, pltpu.roll(far, 7, 1))
    stage_f[1, 0:quarter] = near_right + jnp.where(odd, pltpu.roll(far_right, 1, 1), 0.0)
    for q in range(4):
        at = slice(quarter * q, quarter * q + quarter)
        fine_acc[at, 0:2, :] += stage_f[0, 0:quarter, 2 * q : 2 * q + 2, :]
        fine_acc[at, 6:8, :] += stage_f[1, 0:quarter, 2 * q : 2 * q + 2, :]


def prolong_odd(a, b, c, d):
    return 0.5625 * (b + c) - 0.0625 * (a + d)


def finish_kernel(
    counts, coarse_xy, first_in, second_in, coarse_w, fine_acc, mid_acc, out,
    crs_pad, stage, packed, crs_lhs, msg, crs_pot, wide, mid_tot,
):
    gx, gy = lax.axis_index("gx"), lax.axis_index("gy")
    nx, ny = counts
    rows_c, _, cz = coarse_xy.shape
    cells_x, cells_y, cells_z = out.shape
    mx, my, mz = cells_x // 2, cells_y // 2, cells_z // 2
    cx, cy = cells_x // 4, cells_y // 4
    crs_pad[...] = coarse_xy[...]
    received = by_order(up_first("gy", 2, 0), *(v[...].astype(F32) for v in (first_in, second_in)))
    for source, at in zip(received, (0, cy + 8)):
        msg[...] = source
        for part, first, last, top, left in quarters(rows_c, 0, 2 * cz):
            crs_pad[first:last, at : at + 5, :] += unpair(msg[part, top : top + 5, left : left + 2 * cz], cz)
    rows = rows_c - 8
    part = crs_lhs.shape[0] // 8
    per = HALF // cz
    stage[...] = jnp.zeros_like(stage)
    for a in range(per):
        stage[0:rows_c, 0:5, a * cz : (a + 1) * cz] = crs_pad[:, pl.ds(a, 5, stride=per), :]
    for q in range(2):
        for group in range(3):
            moved = stage[part * q : part * q + part + 8, group : group + 4, :]
            packed[:, 4 * q : 4 * q + 4, group * HALF : (group + 1) * HALF] = moved
    for dx in range(9):
        lhs = packed[dx : dx + part].reshape(part * 8, 3 * HALF)
        crs_lhs[:, dx * 3 * HALF : (dx + 1) * 3 * HALF] = lhs.astype(BF16)
    weights = coarse_w[...].reshape(9 * 3 * HALF, HALF)
    pot = jnp.dot(crs_lhs[...], weights, preferred_element_type=F32).reshape(part, 8, HALF)
    for q in range(2):
        for b in range(per):
            moved = pot[:, 4 * q : 4 * q + 3, b * cz : (b + 1) * cz]
            crs_pot[part * q : part * q + part, pl.ds(b, 3, stride=per), :] = moved
    pot = crs_pot[0:rows]
    keep = inside(pot.shape, 0, -2, cx, gx, nx) & inside(pot.shape, 1, -2, cy, gy, ny)
    pot = jnp.where(keep, pot, 0.0)
    n = cx + 2
    odd = prolong_odd(*(pot[s : s + n] for s in range(4)))
    even = jnp.concatenate([pot[2 : 1 + n], jnp.zeros_like(pot[:1])], axis=0) if n + 2 > rows else pot[2 : 2 + n]
    wide[:, 0] = odd
    wide[:, 1] = even
    wide_y = cy + 2
    v = wide[...].reshape((2 * n,) + pot.shape[1:])
    mid_tot[...] = jnp.zeros_like(mid_tot)
    odd = prolong_odd(*(v[:, s : s + wide_y] for s in range(4)))
    even = v[:, 2 : 1 + wide_y]
    matrix = transfer_matrix(mz, cz, True)
    mid_tot[:, pl.ds(0, wide_y, stride=2), 0:cz] = odd
    mid_tot[:, pl.ds(1, wide_y - 1, stride=2), 0:cz] = even
    total = dot_last(mid_tot[:, :, 0:cz], matrix)
    rows = mx + 3
    pot = mid_acc[...].reshape(rows, 8, WIDE)
    for b in range(4):
        mid_tot[0:rows, pl.ds(b, 3, stride=4), :] = pot[:, 0:3, b * mz : (b + 1) * mz]
    total = mid_tot[0:rows] + total[0:rows]
    keep = inside(total.shape, 0, -1, mx, gx, nx) & inside(total.shape, 1, -1, my, gy, ny)
    mid_tot[0:rows] = jnp.where(keep, total, 0.0)
    matrix = transfer_matrix(cells_z, mz, True)
    pot = fine_acc[...]
    for a in (0, 1):
        if a == 0:
            u = mid_tot[0:rows, 1 : 1 + my, :]
        else:
            u = prolong_odd(*(mid_tot[0:rows, s : s + my, :] for s in range(4)))
        u = dot_last(u, matrix)
        odd = prolong_odd(*(u[s : s + mx] for s in range(4)))
        both = jnp.stack([u[1 : 1 + mx], odd], axis=1).reshape(cells_x, my, cells_z)
        out[:, pl.ds(a, my, stride=2), :] = pot[:, :, a * HALF : a * HALF + cells_z] + both


def whole():
    return pl.BlockSpec(memory_space=pltpu.VMEM)


def call(kernel, outs, ins, scratch, flops=10**8, vmem_out=True, after=(), space=pltpu.VMEM, sems=0, limit=VMEM_LIMIT):
    n = len(ins)

    def body(*refs):
        kernel(*refs[:n], *refs[n + len(after) :])

    return pl.pallas_call(
        body,
        out_shape=[pltpu.VMEM(s, d) for s, d in outs] if vmem_out else [jax.ShapeDtypeStruct(s, d) for s, d in outs],
        in_specs=[pl.BlockSpec(memory_space=space)] * n + [pl.BlockSpec(memory_space=pl.ANY)] * len(after),
        out_specs=[whole()] * len(outs),
        scratch_shapes=[pltpu.VMEM(s, d) for s, d in scratch] + [pltpu.SemaphoreType.DMA((sems,))] * (sems > 0),
        compiler_params=pltpu.CompilerParams(vmem_limit_bytes=limit),
        cost_estimate=pl.CostEstimate(flops=flops, bytes_accessed=10**6, transcendentals=0),
    )(*ins, *after)


def swap(first, second, axis, step, size, start):
    received = []
    for message, group in ((first, start), (second, 1 - start)):
        lower = [i for i in range(size - step) if (i // step) % 2 == group]
        pairs = [(i, i + step) for i in lower] + [(i + step, i) for i in lower]
        received.append(lax.ppermute(message, axis, pairs))
    return received


def up_first(axis, step, start):
    return lax.rem(lax.axis_index(axis) // step, 2) == start


def by_order(flag, first, second):
    return jnp.where(flag, second, first), jnp.where(flag, first, second)


def local(counts, charges, kernel_fine, kernel_mid, kernel_coarse):
    nx, ny = counts
    cells_x, cells_y, cells_z = charges.shape
    mx, mz, cx, cz = cells_x // 2, cells_z // 2, cells_x // 4, cells_z // 4
    frame = cells_y
    lines = ((27, 16, HALF), F32)
    message = ((13, frame, cells_z), BF16)
    first, second, fine_own, mid_own, coarse_own, lines = call(
        functools.partial(spread_kernel, counts),
        [message, message, (charges.shape, BF16), ((mx + 3, frame, mz), F32), ((cx + 5, frame, cz), F32), lines],
        [charges, kernel_fine, kernel_mid, kernel_coarse],
        [
            ((mx + 3, frame + 24, mz), F32),
            ((mx + 3, frame + 24, mz), F32),
            ((cx + 5, frame, mz), F32),
            (charges.shape, F32),
        ]
        + [((9, 9, 9), BF16)] * 3,
        space=pltpu.HBM,
        sems=4,
        limit=60 * 1024 * 1024,
    )
    first, second = swap(first, second, "gx", 1, nx, 1)
    fine_w, mid_w, coarse_w = bands(lines, 0, ((cells_z, 5), (mz, 3), (cz, 2)))
    rows = (cells_x + 8) // 4 + (mx + 14) // 4 + (cx + 14) // 2
    packed = ((rows, frame, cells_z), BF16)
    fine_x, mid_x, coarse_x, first, second = call(
        join_x_kernel,
        [
            ((cells_x + 8, cells_y + 8, cells_z), F32),
            ((mx + 11, frame, mz), F32),
            ((cx + 13, frame, cz), F32),
            packed,
            packed,
        ],
        [fine_own, mid_own, coarse_own, first, second],
        [((rows, frame, cells_z), F32)],
        after=(fine_w,),
    )
    first, second = swap(first, second, "gy", 1, ny, 1)
    (own_acc,) = call(
        own_kernel,
        [((cells_x * 8, WIDE), F32)],
        [fine_x, fine_w],
        [((2, (cells_x + 8) * 8, 5 * WIDE), BF16)],
        flops=10**9,
    )
    half = (cx + 16) // 4
    message = ((half, frame, cells_z), BF16)
    mid_xy, coarse_xy, last_first, last_second = call(
        functools.partial(join_y_kernel, (cells_x + 8) // 4),
        [
            ((mx + 11, frame + 8, mz), F32),
            ((cx + 13, frame + 8, cz), F32),
            message,
            message,
        ],
        [mid_x, coarse_x, first, second],
        [
            ((rows, frame, cells_z), F32),
            ((rows, frame, cells_z), F32),
            ((half, frame, cells_z), F32),
            ((cx + 13, frame + 8, cz), F32),
        ],
        after=(own_acc,),
    )
    last_first, last_second = swap(last_first, last_second, "gy", 2, ny, 0)
    quarter = cells_x // 4
    fine_acc, mid_acc = call(
        rim_kernel,
        [((cells_x, 8, WIDE), F32), (((mx + 3) * 8, WIDE), F32)],
        [first, second, mid_xy, own_acc, fine_w, mid_w],
        [
            ((2, (cells_x + 8) // 4, frame, cells_z), F32),
            ((2, quarter + 8, 8, WIDE), F32),
            ((2, 2, (quarter + 8) * 8, WIDE), BF16),
            ((mx + 11, 16, WIDE), F32),
            ((2, (mx + 12) * 8, 3 * WIDE), BF16),
            ((4, quarter * 8, WIDE), F32),
        ],
        flops=10**9,
    )
    part = (cx + 6) // 2
    (out,) = call(
        functools.partial(finish_kernel, counts),
        [(charges.shape, F32)],
        [coarse_xy, last_first, last_second, coarse_w, fine_acc, mid_acc],
        [
            ((cx + 13, frame + 8, cz), F32),
            ((2 * part + 8, 8, HALF), F32),
            ((part + 8, 8, 3 * HALF), F32),
            ((part * 8, 9 * 3 * HALF), BF16),
            ((half, frame, cells_z), F32),
            ((2 * part, 16, cz), F32),
            ((cx + 2, 2, 16, cz), F32),
            ((mx + 4, 16, mz), F32),
        ],
        vmem_out=False,
    )
    return out


def solution(mesh):
    counts = (mesh.shape["gx"], mesh.shape["gy"])
    placed = (P("gx", "gy", None), P(), P(), P())
    return jax.shard_map(
        functools.partial(local, counts),
        mesh=mesh,
        in_specs=placed,
        out_specs=P("gx", "gy", None),
        check_vma=False,
    )
```

```python
import functools

import jax
import jax.numpy as jnp
from jax import lax
from jax.experimental import pallas as pl
from jax.experimental.pallas import tpu as pltpu
from jax.sharding import PartitionSpec as P

F32 = jnp.float32
BF16 = jnp.bfloat16
WIDE = 256
HALF = 128
VMEM_LIMIT = 14 * 1024 * 1024


def split_pair(v):
    high = v.astype(BF16).astype(F32)
    low = (v - high).astype(BF16).astype(F32)
    return high, low


def pair_lanes(v):
    return jnp.concatenate(split_pair(v), axis=-1)


def exact_dot(v, matrix):
    high, low = split_pair(v)
    return jnp.dot(high.astype(BF16), matrix, preferred_element_type=F32) + jnp.dot(
        low.astype(BF16), matrix, preferred_element_type=F32
    )


def transfer_matrix(fine, coarse, transpose):
    shape = (coarse, fine) if transpose else (fine, coarse)
    fine_at = lax.broadcasted_iota(jnp.int32, shape, 1 if transpose else 0)
    coarse_at = lax.broadcasted_iota(jnp.int32, shape, 0 if transpose else 1)
    d = fine_at - 2 * coarse_at
    one = jnp.where(d == 0, F32(1.0), F32(0.0))
    near = jnp.where((d == 1) | (d == -1), F32(0.5625), F32(0.0))
    far = jnp.where((d == 3) | (d == -3), F32(-0.0625), F32(0.0))
    return (one + near + far).astype(BF16)


def dot_last(v, matrix):
    lead = v.shape[:-1]
    return exact_dot(v.reshape(-1, v.shape[-1]), matrix).reshape(lead + (matrix.shape[1],))


def rows_at(v, first, low, count):
    begin, end = low - first, low - first + count
    inner = v[max(begin, 0) : min(end, v.shape[0])]
    parts = []
    if begin < 0:
        parts.append(jnp.zeros((-begin,) + v.shape[1:], v.dtype))
    parts.append(inner)
    if end > v.shape[0]:
        parts.append(jnp.zeros((end - v.shape[0],) + v.shape[1:], v.dtype))
    return jnp.concatenate(parts, axis=0) if len(parts) > 1 else inner


def weigh_restrict(even, odd0, odd_m1, odd_p1, odd_m2):
    return even + 0.5625 * (odd0 + odd_m1) - 0.0625 * (odd_p1 + odd_m2)


def restrict_rows(even, even_at, odd, odd_at, low, count):
    return weigh_restrict(
        rows_at(even, even_at, low, count),
        *(rows_at(odd, odd_at, low + s, count) for s in (0, -1, 1, -2)),
    )


def pairs_of_rows(v):
    v = v.reshape((v.shape[0] // 2, 2) + v.shape[1:])
    return v[:, 0], v[:, 1]


def inside(shape, axis, first, cells, index, count):
    at = lax.broadcasted_iota(jnp.int32, shape, axis) + first
    return ((at >= 0) | (index > 0)) & ((at < cells) | (index < count - 1))


def x_slots(count, rows):
    half = (count + 1) // 2
    y = slice(0, rows)
    return [
        (slice(0, half), rows, 0, slice(0, half), 0, y),
        (slice(half, count), rows, HALF // 2, slice(0, count - half), 0, y),
    ]


def x_pair_slots(used, rows, frame):
    top, rest = frame - used, rows - (frame - used)
    slots = [(slice(8, 9), rows, HALF // 2, slice(3, 4), 0, slice(0, rows))]
    for half in (0, 1):
        left = half * HALF // 2
        slots.append((slice(4 * half, 4 * half + 4), top, left, slice(0, 4), used, slice(0, top)))
        for g in range(4):
            x = 4 * half + g
            slots.append((slice(x, x + 1), rest, left, slice(4, 5), rest * g, slice(top, rows)))
    return slots


def spread_kernel(counts, *refs):
    outside, (first_out, second_out, fine_own, mid_own, coarse_own, lines) = refs[0:4], refs[4:10]
    (even_pad, odd_pad, crs, charges, msg), raws, sems = refs[10:15], refs[15:18], refs[18]
    copies = [
        pltpu.make_async_copy(source, target, sems.at[i])
        for i, (source, target) in enumerate(zip(outside, (charges,) + raws))
    ]
    for copy in copies:
        copy.start()
    even_pad[...] = jnp.zeros_like(even_pad)
    odd_pad[...] = jnp.zeros_like(odd_pad)
    lines[...] = jnp.zeros_like(lines)
    msg[...] = jnp.zeros_like(msg)
    copies[0].wait()
    fine_own[...] = charges[...].astype(BF16)
    gx, gy = lax.axis_index("gx"), lax.axis_index("gy")
    nx, ny = counts
    cells_x, cells_y, cells_z = charges.shape
    mx, my, mz = cells_x // 2, cells_y // 2, cells_z // 2
    cx, cy, cz = cells_x // 4, cells_y // 4, cells_z // 4
    frame = mid_own.shape[1]
    even, odd = pairs_of_rows(charges[...])
    mid = restrict_rows(even, 0, odd, 0, -1, mx + 3)
    mid = dot_last(mid, transfer_matrix(cells_z, mz, False))
    mid_own[...] = mid
    even_pad[:, 8 : 8 + my] = mid_own[:, pl.ds(0, my, stride=2), :]
    odd_pad[:, 8 : 8 + my] = mid_own[:, pl.ds(1, my, stride=2), :]
    mid = weigh_restrict(
        even_pad[:, 7 : 7 + frame],
        *(odd_pad[:, 7 + s : 7 + s + frame] for s in (0, -1, 1, -2)),
    )
    keep = inside(mid.shape, 0, -1, mx, gx, nx) & inside(mid.shape, 1, -1, my, gy, ny)
    mid = jnp.where(keep, mid, 0.0)
    mid_own[...] = mid
    odd, even = pairs_of_rows(jnp.concatenate([mid, jnp.zeros_like(mid[:1])], axis=0))
    crs[...] = restrict_rows(even, 0, odd, -1, -2, cx + 5)
    n = cx + 5
    odd_pad[:n, 8 : 8 + frame // 2] = crs[:, pl.ds(0, frame // 2, stride=2), :]
    even_pad[:n, 8 : 8 + frame // 2] = crs[:, pl.ds(1, frame // 2, stride=2), :]
    coarse = weigh_restrict(
        even_pad[:n, 6 : 6 + frame],
        *(odd_pad[:n, 7 + s : 7 + s + frame] for s in (0, -1, 1, -2)),
    )
    coarse = dot_last(coarse, transfer_matrix(mz, cz, False))
    keep = inside(coarse.shape, 0, -2, cx, gx, nx) & inside(coarse.shape, 1, -2, cy, gy, ny)
    coarse = jnp.where(keep, coarse, 0.0)
    coarse_own[...] = coarse
    def pack(out, fine_at, mid_at, coarse_at):
        out[0:4] = charges[fine_at : fine_at + 4].astype(BF16)
        for part, rows, left, tile, top, y in x_slots(7, my + 3):
            value = mid_own[mid_at + part.start : mid_at + part.stop, y, :]
            msg[tile, top : top + rows, left : left + mz] = value
        for part, rows, left, tile, top, y in x_pair_slots(my + 3, cy + 5, frame):
            value = coarse_own[coarse_at + part.start : coarse_at + part.stop, y, :]
            msg[tile, top : top + rows, left : left + 2 * cz] = pair_lanes(value)
        out[4:9] = msg[...].astype(BF16)

    flag = up_first("gx", 1, 1)

    @pl.when(flag)
    def _():
        pack(first_out, cells_x - 4, mx - 4, cx - 4)
        pack(second_out, 0, 0, 0)

    @pl.when(jnp.logical_not(flag))
    def _():
        pack(first_out, 0, 0, 0)
        pack(second_out, cells_x - 4, mx - 4, cx - 4)

    for i, raw in enumerate(raws):
        copies[i + 1].wait()
        lines[9 * i : 9 * i + 9, 0:9, 0:9] = raw[...].astype(F32)


def two_halves(v):
    half = (v.shape[0] + 1) // 2
    return jnp.concatenate([v[:half], rows_at(v, 0, half, half)], axis=-1)


def unpair(v, width):
    return v[..., :width] + v[..., width : 2 * width]


def from_halves(v, count):
    lanes = v.shape[-1] // 2
    return jnp.concatenate([v[..., :lanes], v[: count - v.shape[0], :, lanes:]], axis=0)


def fine_parts(rows):
    q = rows // 4
    return [(slice(0, q), q * r, q * r + q, 4 * r, 0) for r in range(4)]


def quarters(rows, at, lanes):
    q = -(-rows // 4)
    parts = []
    for r in range(4):
        first, last = q * r, min(q * r + q, rows)
        parts.append((slice(at, at + last - first), first, last, 8 * (r // 2), lanes * (r % 2)))
    return parts


def ninth_rows(rows, count, at, lanes):
    parts = []
    for part, first, last, top, left in quarters(rows, at, lanes):
        last = min(last, count)
        if first < last:
            parts.append((slice(part.start, part.start + last - first), first, last, top + 7, left))
    return parts


def join_x_kernel(charges, mid_own, coarse_own, first_in, second_in, fine_x, mid_x, coarse_x, first_out, second_out, buf, got):
    before, after = by_order(up_first("gx", 1, 1), *(v[...].astype(F32) for v in (first_in, second_in)))
    cells_x, cells_y, _ = charges.shape
    mx, cx = cells_x // 2, cells_x // 4
    mz, cz = mid_own.shape[2], coarse_own.shape[2]
    my = cells_y // 2
    rows_x = cells_x + 8
    own = slice(4, 4 + cells_y)
    for edge in (0, 4 + cells_y):
        fine_x[:, edge : edge + 4, :] = jnp.zeros((rows_x, 4, charges.shape[2]), F32)
    fine_x[0:4, own, :] = before[0:4]
    fine_x[4 : 4 + cells_x, own, :] = charges[...].astype(F32)
    fine_x[4 + cells_x : rows_x, own, :] = after[0:4]
    got[0], got[1] = before[4:9], after[4:9]
    mid_x[...] = rows_at(mid_own[...], -1, -5, mx + 11)
    coarse_x[...] = rows_at(coarse_own[...], -2, -6, cx + 13)
    for side, mid_at, coarse_at in ((0, 0, 0), (1, mx + 4, cx + 4)):
        for part, rows, left, tile, top, y in x_slots(7, my + 3):
            at = slice(mid_at + part.start, mid_at + part.stop)
            mid_x[at, y, :] += got[side, tile, top : top + rows, left : left + mz]
        for part, rows, left, tile, top, y in x_pair_slots(my + 3, cells_y // 4 + 5, cells_y):
            at = slice(coarse_at + part.start, coarse_at + part.stop)
            coarse_x[at, y, :] += unpair(got[side, tile, top : top + rows, left : left + 2 * cz], cz)
    buf[...] = jnp.zeros_like(buf)

    def pack(out, fine_at, mid_at):
        for part, first, last, top, left in fine_parts(cells_x + 8):
            buf[part, top : top + 4, left:] = fine_x[first:last, fine_at : fine_at + 4, :]
        at = (cells_x + 8) // 4
        for part, first, last, top, left in quarters(mx + 11, at, mz):
            buf[part, top : top + 7, left : left + mz] = mid_x[first:last, mid_at : mid_at + 7, :]
        packed = pair_lanes(coarse_x[:, 0:9, :])
        for part, first, last, top, left in ninth_rows(mx + 11, cx + 13, at, 2 * cz):
            buf[part, top : top + 1, left : left + 2 * cz] = packed[first:last, 8:9, :]
        at += -(-(mx + 11) // 4)
        for part, first, last, top, left in quarters(cx + 13, at, 2 * cz):
            buf[part, top : top + 8, left : left + 2 * cz] = packed[first:last, 0:8, :]
        out[...] = buf[...].astype(BF16)

    flag = up_first("gy", 1, 1)

    @pl.when(flag)
    def _():
        pack(first_out, cells_y, my - 4)
        pack(second_out, 4, 0)

    @pl.when(jnp.logical_not(flag))
    def _():
        pack(first_out, 4, 0)
        pack(second_out, cells_y, my - 4)


def join_y_kernel(at, mid_x, coarse_x, first_in, second_in, mid_xy, coarse_xy, first_out, second_out, low, high, buf, side, from_low, from_high):
    my, cy = mid_x.shape[1] // 2, mid_x.shape[1] // 4
    rows_m, rows_c = mid_x.shape[0], coarse_x.shape[0]
    mz, cz = mid_x.shape[2], coarse_x.shape[2]
    low[...], high[...] = by_order(up_first("gy", 1, 1), first_in[...].astype(F32), second_in[...].astype(F32))
    mid_xy[...] = jnp.zeros_like(mid_xy)
    mid_xy[:, 4 : 7 + my, :] = mid_x[:, 0 : my + 3, :]
    for part, first, last, top, left in quarters(rows_m, at, mz):
        mid_xy[first:last, 0:7, :] += low[part, top : top + 7, left : left + mz]
        mid_xy[first:last, 4 + my : 11 + my, :] += high[part, top : top + 7, left : left + mz]
    ninths = ninth_rows(rows_m, rows_c, at, 2 * cz)
    at += -(-rows_m // 4)
    for source, target in ((low, from_low), (high, from_high)):
        for part, first, last, top, left in ninths:
            target[first:last, 8:9, :] = unpair(source[part, top : top + 1, left : left + 2 * cz], cz)
        for part, first, last, top, left in quarters(rows_c, at, 2 * cz):
            target[first:last, 0:8, :] = unpair(source[part, top : top + 8, left : left + 2 * cz], cz)
    side[...] = jnp.zeros_like(side)
    side[:, 4 : 9 + cy, :] = coarse_x[:, 0 : cy + 5, :]
    coarse_xy[...] = side[...]
    coarse_xy[:, 0:9, :] += from_low[:, 0:9, :]
    buf[...] = jnp.zeros_like(buf)

    def pack(rows, out):
        rows = pair_lanes(rows)
        for part, first, last, top, left in quarters(rows_c, 0, 2 * cz):
            buf[part, top : top + 5, left : left + 2 * cz] = rows[first:last]
        out[...] = buf[...].astype(BF16)

    up = coarse_xy[:, 4 + cy : 9 + cy, :]
    coarse_xy[:, 4 + cy : 13 + cy, :] += from_high[:, 0:9, :]
    side[:, 4 + cy : 13 + cy, :] += from_high[:, 0:9, :]
    down = side[:, 4:9, :]
    flag = up_first("gy", 2, 0)
    pack(jnp.where(flag, up, down), first_out)
    pack(jnp.where(flag, down, up), second_out)


def bands_kernel(begin, levels, lines, *refs):
    outs, joint, last, turned = refs[:-3], refs[-3], refs[-2], refs[-1]
    tap = lax.broadcasted_iota(jnp.int32, (HALF, HALF), 0)
    place = lax.broadcasted_iota(jnp.int32, (HALF, HALF), 1)
    reverse = ((tap <= 8) & (place == jnp.where(tap <= 4, 4 - tap, HALF + 4 - tap))).astype(F32).astype(BF16)
    n = len(levels)
    flat = lines[9 * begin : 9 * (begin + n)].reshape(n * 9 * 16, HALF).astype(BF16)
    values = jnp.dot(flat, reverse, preferred_element_type=F32).reshape(n * 9, 16, HALF)
    turned[...] = pltpu.roll(values, 0, 2, stride=16, stride_axis=1)
    joint[...] = jnp.broadcast_to(jnp.sum(turned[:, 0:8, :], axis=1, keepdims=True), joint.shape)
    ninth = [turned[9 * i : 9 * i + 9, 8:9, :] for i in range(n)]
    ninth = functools.reduce(jnp.add, [pltpu.roll(v, 16 * i, 2) if i else v for i, v in enumerate(ninth)])
    last[...] = jnp.broadcast_to(ninth, last.shape)
    lane = lax.broadcasted_iota(jnp.int32, (8, HALF), 1)

    def one_dx(dx, carry):
        def turns(line):
            return [pltpu.roll(line, 8 * r, 1, stride=1, stride_axis=0) for r in range(16)]

        ninths = turns(last[dx])
        for level, ((depth, groups), out) in enumerate(zip(levels, outs)):
            per, steps = HALF // depth, depth // 8
            eights = turns(joint[9 * level + dx])
            for offset in range(2 * groups - 1):
                rows = []
                for a in range(per):
                    for g in range(steps):
                        full = jnp.zeros((8, HALF), F32)
                        for b in range(per):
                            line = per * offset + a - b
                            at = steps * b + g
                            if 0 <= line <= 8:
                                part = ninths[(at - 2 * level) % 16] if line == 8 else eights[(at - 2 * line) % 16]
                                full = part if per == 1 else jnp.where(lane // depth == b, part, full)
                        apart = lax.rem(lane, depth) - 8 * g - lax.broadcasted_iota(jnp.int32, (8, HALF), 0)
                        rows.append(jnp.where((apart <= 4) & (apart >= -4), full, 0.0))
                out[dx, offset] = jnp.concatenate(rows, axis=0).astype(BF16)
        return carry

    lax.fori_loop(0, 9, one_dx, 0)


def bands(lines, begin, levels, after=()):
    n = len(levels) * 9
    return call(
        functools.partial(bands_kernel, begin, levels),
        [((9, 2 * groups - 1, HALF, HALF), BF16) for _, groups in levels],
        [lines],
        [((n, 8, HALF), F32), ((9, 8, HALF), F32), ((n, 16, HALF), F32)],
        flops=10**9,
        after=after,
    )


def weights_of(blocks, dx):
    count = blocks.shape[1]
    zero = jnp.zeros((HALF, HALF), BF16)

    def block(offset):
        return blocks[dx, offset] if 0 <= offset < count else zero

    halves = range(count + 1)
    return jnp.concatenate([jnp.concatenate([block(h), block(h - 1)], axis=1) for h in halves], axis=0)


def gather_rows(field, rows, per, groups, depth, lhs):
    for parity in (0, 1):
        count = rows - parity
        for group in range(groups):
            for a in range(per):
                lane = group * WIDE + a * depth
                part = field[parity:rows, pl.ds(a + per * group, 8, stride=per), :]
                lhs[parity, 0 : count * 8, lane : lane + depth] = part.reshape(count * 8, depth).astype(BF16)


def gather_staged(field, rows, per, groups, depth, stage, lhs):
    count = field.shape[1] // per
    stage[...] = jnp.zeros_like(stage)
    for a in range(per):
        stage[:, 0:count, a * depth : (a + 1) * depth] = field[:, pl.ds(a, count, stride=per), :]
    for parity in (0, 1):
        n = (rows - parity) * 8
        for group in range(groups):
            part = stage[parity:rows, group : group + 8, :].reshape(n, WIDE)
            lhs[parity, 0:n, group * WIDE : (group + 1) * WIDE] = part.astype(BF16)


def convolve(lhs, weights, out_rows, acc):
    n = out_rows * 8
    for dx in range(9):
        start = 16 * (dx // 2)
        part = jnp.dot(lhs[dx % 2, start : start + n, :], weights_of(weights, dx), preferred_element_type=F32)
        acc[...] = part if dx == 0 else acc[...] + part


def own_kernel(fine_x, weights, acc, lhs):
    rows = fine_x.shape[0]
    gather_rows(fine_x, rows, 2, 5, fine_x.shape[2], lhs)
    convolve(lhs, weights, rows - 8, acc)


def group_weights(blocks, dx, group):
    return weights_of(blocks, dx)[group * WIDE : (group + 1) * WIDE]


def rim_kernel(first_in, second_in, mid_xy, own, fine_w, mid_w, fine_acc, mid_acc, rim, stage_f, lhs_f, stage, mid_lhs, sums):
    cells_x = own.shape[0] // 8
    quarter = cells_x // 4
    tiles = rim.shape[1]
    rim[0], rim[1] = by_order(up_first("gy", 1, 1), *(v[0:tiles].astype(F32) for v in (first_in, second_in)))
    for side in (0, 1):
        for q in range(4):
            for r in range(4):
                first, last = max(quarter * q, tiles * r), min(quarter * q + quarter + 8, tiles * r + tiles)
                if first < last:
                    to = slice(first - quarter * q, last - quarter * q)
                    source_rows = slice(first - tiles * r, last - tiles * r)
                    for a in (0, 1):
                        part = rim[side, source_rows, pl.ds(4 * r + a, 2, stride=2), :]
                        stage_f[side, to, 2 * q : 2 * q + 2, a * HALF : (a + 1) * HALF] = part
        for parity in (0, 1):
            n = quarter + 8 - parity
            lhs_f[side, parity, 0 : 8 * n, :] = stage_f[side, parity : parity + n].reshape(8 * n, WIDE).astype(BF16)
    n = quarter * 8
    for dx in range(9):
        start = 16 * (dx // 2)
        for i, (side, group) in enumerate(((0, 0), (0, 1), (1, 3), (1, 4))):
            rows = lhs_f[side, dx % 2, start : start + n, :]
            part = jnp.dot(rows, group_weights(fine_w, dx, group), preferred_element_type=F32)
            sums[i] = part if dx == 0 else sums[i] + part
    rows = mid_xy.shape[0]
    gather_staged(mid_xy, rows, 4, 3, mid_xy.shape[2], stage, mid_lhs)
    convolve(mid_lhs, mid_w, rows - 8, mid_acc)
    fine_acc[...] = own[...].reshape(fine_acc.shape)
    near, far, far_right, near_right = (sums[i].reshape(quarter, 8, WIDE) for i in range(4))
    odd = lax.rem(lax.broadcasted_iota(jnp.int32, near.shape, 1), 2) == 1
    stage_f[0, 0:quarter] = near + jnp.where(odd, 0.0, pltpu.roll(far, 7, 1))
    stage_f[1, 0:quarter] = near_right + jnp.where(odd, pltpu.roll(far_right, 1, 1), 0.0)
    for q in range(4):
        at = slice(quarter * q, quarter * q + quarter)
        fine_acc[at, 0:2, :] += stage_f[0, 0:quarter, 2 * q : 2 * q + 2, :]
        fine_acc[at, 6:8, :] += stage_f[1, 0:quarter, 2 * q : 2 * q + 2, :]


def prolong_odd(a, b, c, d):
    return 0.5625 * (b + c) - 0.0625 * (a + d)


def finish_kernel(
    counts, coarse_xy, first_in, second_in, coarse_w, fine_acc, mid_acc, out,
    crs_pad, stage, packed, crs_lhs, msg, crs_pot, wide, mid_tot,
):
    gx, gy = lax.axis_index("gx"), lax.axis_index("gy")
    nx, ny = counts
    rows_c, _, cz = coarse_xy.shape
    cells_x, cells_y, cells_z = out.shape
    mx, my, mz = cells_x // 2, cells_y // 2, cells_z // 2
    cx, cy = cells_x // 4, cells_y // 4
    crs_pad[...] = coarse_xy[...]
    received = by_order(up_first("gy", 2, 0), *(v[...].astype(F32) for v in (first_in, second_in)))
    for source, at in zip(received, (0, cy + 8)):
        msg[...] = source
        for part, first, last, top, left in quarters(rows_c, 0, 2 * cz):
            crs_pad[first:last, at : at + 5, :] += unpair(msg[part, top : top + 5, left : left + 2 * cz], cz)
    rows = rows_c - 8
    part = crs_lhs.shape[0] // 8
    per = HALF // cz
    stage[...] = jnp.zeros_like(stage)
    for a in range(per):
        stage[0:rows_c, 0:5, a * cz : (a + 1) * cz] = crs_pad[:, pl.ds(a, 5, stride=per), :]
    for q in range(2):
        for group in range(3):
            moved = stage[part * q : part * q + part + 8, group : group + 4, :]
            packed[:, 4 * q : 4 * q + 4, group * HALF : (group + 1) * HALF] = moved
    for dx in range(9):
        lhs = packed[dx : dx + part].reshape(part * 8, 3 * HALF)
        crs_lhs[:, dx * 3 * HALF : (dx + 1) * 3 * HALF] = lhs.astype(BF16)
    weights = coarse_w[...].reshape(9 * 3 * HALF, HALF)
    pot = jnp.dot(crs_lhs[...], weights, preferred_element_type=F32).reshape(part, 8, HALF)
    for q in range(2):
        for b in range(per):
            moved = pot[:, 4 * q : 4 * q + 3, b * cz : (b + 1) * cz]
            crs_pot[part * q : part * q + part, pl.ds(b, 3, stride=per), :] = moved
    pot = crs_pot[0:rows]
    keep = inside(pot.shape, 0, -2, cx, gx, nx) & inside(pot.shape, 1, -2, cy, gy, ny)
    pot = jnp.where(keep, pot, 0.0)
    n = cx + 2
    odd = prolong_odd(*(pot[s : s + n] for s in range(4)))
    even = jnp.concatenate([pot[2 : 1 + n], jnp.zeros_like(pot[:1])], axis=0) if n + 2 > rows else pot[2 : 2 + n]
    wide[:, 0] = odd
    wide[:, 1] = even
    wide_y = cy + 2
    v = wide[...].reshape((2 * n,) + pot.shape[1:])
    mid_tot[...] = jnp.zeros_like(mid_tot)
    odd = prolong_odd(*(v[:, s : s + wide_y] for s in range(4)))
    even = v[:, 2 : 1 + wide_y]
    matrix = transfer_matrix(mz, cz, True)
    mid_tot[:, pl.ds(0, wide_y, stride=2), 0:cz] = odd
    mid_tot[:, pl.ds(1, wide_y - 1, stride=2), 0:cz] = even
    total = dot_last(mid_tot[:, :, 0:cz], matrix)
    rows = mx + 3
    pot = mid_acc[...].reshape(rows, 8, WIDE)
    for b in range(4):
        mid_tot[0:rows, pl.ds(b, 3, stride=4), :] = pot[:, 0:3, b * mz : (b + 1) * mz]
    total = mid_tot[0:rows] + total[0:rows]
    keep = inside(total.shape, 0, -1, mx, gx, nx) & inside(total.shape, 1, -1, my, gy, ny)
    mid_tot[0:rows] = jnp.where(keep, total, 0.0)
    matrix = transfer_matrix(cells_z, mz, True)
    pot = fine_acc[...]
    for a in (0, 1):
        if a == 0:
            u = mid_tot[0:rows, 1 : 1 + my, :]
        else:
            u = prolong_odd(*(mid_tot[0:rows, s : s + my, :] for s in range(4)))
        u = dot_last(u, matrix)
        odd = prolong_odd(*(u[s : s + mx] for s in range(4)))
        both = jnp.stack([u[1 : 1 + mx], odd], axis=1).reshape(cells_x, my, cells_z)
        out[:, pl.ds(a, my, stride=2), :] = pot[:, :, a * HALF : a * HALF + cells_z] + both


def whole():
    return pl.BlockSpec(memory_space=pltpu.VMEM)


def call(kernel, outs, ins, scratch, flops=10**8, vmem_out=True, after=(), space=pltpu.VMEM, sems=0, limit=VMEM_LIMIT):
    n = len(ins)

    def body(*refs):
        kernel(*refs[:n], *refs[n + len(after) :])

    return pl.pallas_call(
        body,
        out_shape=[pltpu.VMEM(s, d) for s, d in outs] if vmem_out else [jax.ShapeDtypeStruct(s, d) for s, d in outs],
        in_specs=[pl.BlockSpec(memory_space=space)] * n + [pl.BlockSpec(memory_space=pl.ANY)] * len(after),
        out_specs=[whole()] * len(outs),
        scratch_shapes=[pltpu.VMEM(s, d) for s, d in scratch] + [pltpu.SemaphoreType.DMA((sems,))] * (sems > 0),
        compiler_params=pltpu.CompilerParams(vmem_limit_bytes=limit),
        cost_estimate=pl.CostEstimate(flops=flops, bytes_accessed=10**6, transcendentals=0),
    )(*ins, *after)


def swap(first, second, axis, step, size, start):
    received = []
    for message, group in ((first, start), (second, 1 - start)):
        lower = [i for i in range(size - step) if (i // step) % 2 == group]
        pairs = [(i, i + step) for i in lower] + [(i + step, i) for i in lower]
        received.append(lax.ppermute(message, axis, pairs))
    return received


def up_first(axis, step, start):
    return lax.rem(lax.axis_index(axis) // step, 2) == start


def by_order(flag, first, second):
    return jnp.where(flag, second, first), jnp.where(flag, first, second)


def local(counts, charges, kernel_fine, kernel_mid, kernel_coarse):
    nx, ny = counts
    cells_x, cells_y, cells_z = charges.shape
    mx, mz, cx, cz = cells_x // 2, cells_z // 2, cells_x // 4, cells_z // 4
    frame = cells_y
    lines = ((27, 16, HALF), F32)
    message = ((9, frame, cells_z), BF16)
    first, second, fine_own, mid_own, coarse_own, lines = call(
        functools.partial(spread_kernel, counts),
        [message, message, (charges.shape, BF16), ((mx + 3, frame, mz), F32), ((cx + 5, frame, cz), F32), lines],
        [charges, kernel_fine, kernel_mid, kernel_coarse],
        [
            ((mx + 3, frame + 24, mz), F32),
            ((mx + 3, frame + 24, mz), F32),
            ((cx + 5, frame, mz), F32),
            (charges.shape, F32),
            ((5, frame, cells_z), F32),
        ]
        + [((9, 9, 9), BF16)] * 3,
        space=pltpu.HBM,
        sems=4,
        limit=60 * 1024 * 1024,
    )
    first, second = swap(first, second, "gx", 1, nx, 1)
    fine_w, mid_w, coarse_w = bands(lines, 0, ((cells_z, 5), (mz, 3), (cz, 2)))
    rows = (cells_x + 8) // 4 + (mx + 14) // 4 + (cx + 16) // 4
    packed = ((rows, frame, cells_z), BF16)
    fine_x, mid_x, coarse_x, first, second = call(
        join_x_kernel,
        [
            ((cells_x + 8, cells_y + 8, cells_z), F32),
            ((mx + 11, frame, mz), F32),
            ((cx + 13, frame, cz), F32),
            packed,
            packed,
        ],
        [fine_own, mid_own, coarse_own, first, second],
        [((rows, frame, cells_z), F32), ((2, 5, frame, cells_z), F32)],
        after=(fine_w,),
    )
    first, second = swap(first, second, "gy", 1, ny, 1)
    (own_acc,) = call(
        own_kernel,
        [((cells_x * 8, WIDE), F32)],
        [fine_x, fine_w],
        [((2, (cells_x + 8) * 8, 5 * WIDE), BF16)],
        flops=10**9,
    )
    half = (cx + 16) // 4
    message = ((half, frame, cells_z), BF16)
    mid_xy, coarse_xy, last_first, last_second = call(
        functools.partial(join_y_kernel, (cells_x + 8) // 4),
        [
            ((mx + 11, frame + 8, mz), F32),
            ((cx + 13, frame + 8, cz), F32),
            message,
            message,
        ],
        [mid_x, coarse_x, first, second],
        [
            ((rows, frame, cells_z), F32),
            ((rows, frame, cells_z), F32),
            ((half, frame, cells_z), F32),
            ((cx + 13, frame + 8, cz), F32),
            ((cx + 13, frame, cz), F32),
            ((cx + 13, frame, cz), F32),
        ],
        after=(own_acc,),
    )
    last_first, last_second = swap(last_first, last_second, "gy", 2, ny, 0)
    quarter = cells_x // 4
    fine_acc, mid_acc = call(
        rim_kernel,
        [((cells_x, 8, WIDE), F32), (((mx + 3) * 8, WIDE), F32)],
        [first, second, mid_xy, own_acc, fine_w, mid_w],
        [
            ((2, (cells_x + 8) // 4, frame, cells_z), F32),
            ((2, quarter + 8, 8, WIDE), F32),
            ((2, 2, (quarter + 8) * 8, WIDE), BF16),
            ((mx + 11, 16, WIDE), F32),
            ((2, (mx + 12) * 8, 3 * WIDE), BF16),
            ((4, quarter * 8, WIDE), F32),
        ],
        flops=10**9,
    )
    part = (cx + 6) // 2
    (out,) = call(
        functools.partial(finish_kernel, counts),
        [(charges.shape, F32)],
        [coarse_xy, last_first, last_second, coarse_w, fine_acc, mid_acc],
        [
            ((cx + 13, frame + 8, cz), F32),
            ((2 * part + 8, 8, HALF), F32),
            ((part + 8, 8, 3 * HALF), F32),
            ((part * 8, 9 * 3 * HALF), BF16),
            ((half, frame, cells_z), F32),
            ((2 * part, 16, cz), F32),
            ((cx + 2, 2, 16, cz), F32),
            ((mx + 4, 16, mz), F32),
        ],
        vmem_out=False,
    )
    return out


def solution(mesh):
    counts = (mesh.shape["gx"], mesh.shape["gy"])
    placed = (P("gx", "gy", None), P(), P(), P())
    return jax.shard_map(
        functools.partial(local, counts),
        mesh=mesh,
        in_specs=placed,
        out_specs=P("gx", "gy", None),
        check_vma=False,
    )
```

```python
import functools

import jax
import jax.numpy as jnp
from jax import lax
from jax.experimental import pallas as pl
from jax.experimental.pallas import tpu as pltpu
from jax.sharding import PartitionSpec as P

F32 = jnp.float32
BF16 = jnp.bfloat16
WIDE = 256
HALF = 128
VMEM_LIMIT = 14 * 1024 * 1024


def split_pair(v):
    high = v.astype(BF16).astype(F32)
    low = (v - high).astype(BF16).astype(F32)
    return high, low


def pair_lanes(v):
    return jnp.concatenate(split_pair(v), axis=-1)


def exact_dot(v, matrix):
    pair = pair_lanes(v).astype(BF16)
    return jnp.dot(pair, jnp.concatenate([matrix, matrix], axis=0), preferred_element_type=F32)


def transfer_matrix(fine, coarse, transpose):
    shape = (coarse, fine) if transpose else (fine, coarse)
    fine_at = lax.broadcasted_iota(jnp.int32, shape, 1 if transpose else 0)
    coarse_at = lax.broadcasted_iota(jnp.int32, shape, 0 if transpose else 1)
    d = fine_at - 2 * coarse_at
    one = jnp.where(d == 0, F32(1.0), F32(0.0))
    near = jnp.where((d == 1) | (d == -1), F32(0.5625), F32(0.0))
    far = jnp.where((d == 3) | (d == -3), F32(-0.0625), F32(0.0))
    return (one + near + far).astype(BF16)


def dot_last(v, matrix):
    lead = v.shape[:-1]
    return exact_dot(v.reshape(-1, v.shape[-1]), matrix).reshape(lead + (matrix.shape[1],))


def rows_at(v, first, low, count):
    begin, end = low - first, low - first + count
    inner = v[max(begin, 0) : min(end, v.shape[0])]
    parts = []
    if begin < 0:
        parts.append(jnp.zeros((-begin,) + v.shape[1:], v.dtype))
    parts.append(inner)
    if end > v.shape[0]:
        parts.append(jnp.zeros((end - v.shape[0],) + v.shape[1:], v.dtype))
    return jnp.concatenate(parts, axis=0) if len(parts) > 1 else inner


def weigh_restrict(even, odd0, odd_m1, odd_p1, odd_m2):
    return even + 0.5625 * (odd0 + odd_m1) - 0.0625 * (odd_p1 + odd_m2)


def restrict_rows(even, even_at, odd, odd_at, low, count):
    return weigh_restrict(
        rows_at(even, even_at, low, count),
        *(rows_at(odd, odd_at, low + s, count) for s in (0, -1, 1, -2)),
    )


def pairs_of_rows(v):
    v = v.reshape((v.shape[0] // 2, 2) + v.shape[1:])
    return v[:, 0], v[:, 1]


def inside(shape, axis, first, cells, index, count):
    at = lax.broadcasted_iota(jnp.int32, shape, axis) + first
    return ((at >= 0) | (index > 0)) & ((at < cells) | (index < count - 1))


def x_slots(count, rows):
    half = (count + 1) // 2
    y = slice(0, rows)
    return [
        (slice(0, half), rows, 0, slice(0, half), 0, y),
        (slice(half, count), rows, HALF // 2, slice(0, count - half), 0, y),
    ]


def x_pair_slots(used, rows, frame):
    top, rest = frame - used, rows - (frame - used)
    slots = [(slice(8, 9), rows, HALF // 2, slice(3, 4), 0, slice(0, rows))]
    for half in (0, 1):
        left = half * HALF // 2
        slots.append((slice(4 * half, 4 * half + 4), top, left, slice(0, 4), used, slice(0, top)))
        for g in range(4):
            x = 4 * half + g
            slots.append((slice(x, x + 1), rest, left, slice(4, 5), rest * g, slice(top, rows)))
    return slots


def spread_kernel(counts, *refs):
    outside, (first_out, second_out, fine_own, mid_own, coarse_own, lines) = refs[0:4], refs[4:10]
    (even_pad, odd_pad, crs, charges, msg), raws, sems = refs[10:15], refs[15:18], refs[18]
    copies = [
        pltpu.make_async_copy(source, target, sems.at[i])
        for i, (source, target) in enumerate(zip(outside, (charges,) + raws))
    ]
    for copy in copies:
        copy.start()
    even_pad[...] = jnp.zeros_like(even_pad)
    odd_pad[...] = jnp.zeros_like(odd_pad)
    lines[...] = jnp.zeros_like(lines)
    msg[...] = jnp.zeros_like(msg)
    copies[0].wait()
    fine_own[...] = charges[...].astype(BF16)
    gx, gy = lax.axis_index("gx"), lax.axis_index("gy")
    nx, ny = counts
    cells_x, cells_y, cells_z = charges.shape
    mx, my, mz = cells_x // 2, cells_y // 2, cells_z // 2
    cx, cy, cz = cells_x // 4, cells_y // 4, cells_z // 4
    frame = mid_own.shape[1]
    even, odd = pairs_of_rows(charges[...])
    mid = restrict_rows(even, 0, odd, 0, -1, mx + 3)
    mid = dot_last(mid, transfer_matrix(cells_z, mz, False))
    mid_own[...] = mid
    even_pad[:, 8 : 8 + my] = mid_own[:, pl.ds(0, my, stride=2), :]
    odd_pad[:, 8 : 8 + my] = mid_own[:, pl.ds(1, my, stride=2), :]
    mid = weigh_restrict(
        even_pad[:, 7 : 7 + frame],
        *(odd_pad[:, 7 + s : 7 + s + frame] for s in (0, -1, 1, -2)),
    )
    keep = inside(mid.shape, 0, -1, mx, gx, nx) & inside(mid.shape, 1, -1, my, gy, ny)
    mid = jnp.where(keep, mid, 0.0)
    mid_own[...] = mid
    odd, even = pairs_of_rows(jnp.concatenate([mid, jnp.zeros_like(mid[:1])], axis=0))
    crs[...] = restrict_rows(even, 0, odd, -1, -2, cx + 5)
    n = cx + 5
    odd_pad[:n, 8 : 8 + frame // 2] = crs[:, pl.ds(0, frame // 2, stride=2), :]
    even_pad[:n, 8 : 8 + frame // 2] = crs[:, pl.ds(1, frame // 2, stride=2), :]
    coarse = weigh_restrict(
        even_pad[:n, 6 : 6 + frame],
        *(odd_pad[:n, 7 + s : 7 + s + frame] for s in (0, -1, 1, -2)),
    )
    coarse = dot_last(coarse, transfer_matrix(mz, cz, False))
    keep = inside(coarse.shape, 0, -2, cx, gx, nx) & inside(coarse.shape, 1, -2, cy, gy, ny)
    coarse = jnp.where(keep, coarse, 0.0)
    coarse_own[...] = coarse
    def pack(out, fine_at, mid_at, coarse_at):
        out[0:4] = charges[fine_at : fine_at + 4].astype(BF16)
        for part, rows, left, tile, top, y in x_slots(7, my + 3):
            value = mid_own[mid_at + part.start : mid_at + part.stop, y, :]
            msg[tile, top : top + rows, left : left + mz] = value
        for part, rows, left, tile, top, y in x_pair_slots(my + 3, cy + 5, frame):
            value = coarse_own[coarse_at + part.start : coarse_at + part.stop, y, :]
            msg[tile, top : top + rows, left : left + 2 * cz] = pair_lanes(value)
        out[4:9] = msg[...].astype(BF16)

    flag = up_first("gx", 1, 1)

    @pl.when(flag)
    def _():
        pack(first_out, cells_x - 4, mx - 4, cx - 4)
        pack(second_out, 0, 0, 0)

    @pl.when(jnp.logical_not(flag))
    def _():
        pack(first_out, 0, 0, 0)
        pack(second_out, cells_x - 4, mx - 4, cx - 4)

    for i, raw in enumerate(raws):
        copies[i + 1].wait()
        lines[9 * i : 9 * i + 9, 0:9, 0:9] = raw[...].astype(F32)


def two_halves(v):
    half = (v.shape[0] + 1) // 2
    return jnp.concatenate([v[:half], rows_at(v, 0, half, half)], axis=-1)


def unpair(v, width):
    return v[..., :width] + v[..., width : 2 * width]


def from_halves(v, count):
    lanes = v.shape[-1] // 2
    return jnp.concatenate([v[..., :lanes], v[: count - v.shape[0], :, lanes:]], axis=0)


def fine_parts(rows):
    q = rows // 4
    return [(slice(0, q), q * r, q * r + q, 4 * r, 0) for r in range(4)]


def quarters(rows, at, lanes):
    q = -(-rows // 4)
    parts = []
    for r in range(4):
        first, last = q * r, min(q * r + q, rows)
        parts.append((slice(at, at + last - first), first, last, 8 * (r // 2), lanes * (r % 2)))
    return parts


def ninth_rows(rows, count, at, lanes):
    parts = []
    for part, first, last, top, left in quarters(rows, at, lanes):
        last = min(last, count)
        if first < last:
            parts.append((slice(part.start, part.start + last - first), first, last, top + 7, left))
    return parts


def join_x_kernel(charges, mid_own, coarse_own, first_in, second_in, fine_x, mid_x, coarse_x, first_out, second_out, buf, got):
    before, after = by_order(up_first("gx", 1, 1), *(v[...].astype(F32) for v in (first_in, second_in)))
    cells_x, cells_y, _ = charges.shape
    mx, cx = cells_x // 2, cells_x // 4
    mz, cz = mid_own.shape[2], coarse_own.shape[2]
    my = cells_y // 2
    rows_x = cells_x + 8
    own = slice(4, 4 + cells_y)
    for edge in (0, 4 + cells_y):
        fine_x[:, edge : edge + 4, :] = jnp.zeros((rows_x, 4, charges.shape[2]), F32)
    fine_x[0:4, own, :] = before[0:4]
    fine_x[4 : 4 + cells_x, own, :] = charges[...].astype(F32)
    fine_x[4 + cells_x : rows_x, own, :] = after[0:4]
    got[0], got[1] = before[4:9], after[4:9]
    mid_x[...] = rows_at(mid_own[...], -1, -5, mx + 11)
    coarse_x[...] = rows_at(coarse_own[...], -2, -6, cx + 13)
    for side, mid_at, coarse_at in ((0, 0, 0), (1, mx + 4, cx + 4)):
        for part, rows, left, tile, top, y in x_slots(7, my + 3):
            at = slice(mid_at + part.start, mid_at + part.stop)
            mid_x[at, y, :] += got[side, tile, top : top + rows, left : left + mz]
        for part, rows, left, tile, top, y in x_pair_slots(my + 3, cells_y // 4 + 5, cells_y):
            at = slice(coarse_at + part.start, coarse_at + part.stop)
            coarse_x[at, y, :] += unpair(got[side, tile, top : top + rows, left : left + 2 * cz], cz)
    buf[...] = jnp.zeros_like(buf)

    def pack(out, fine_at, mid_at):
        for part, first, last, top, left in fine_parts(cells_x + 8):
            buf[part, top : top + 4, left:] = fine_x[first:last, fine_at : fine_at + 4, :]
        at = (cells_x + 8) // 4
        for part, first, last, top, left in quarters(mx + 11, at, mz):
            buf[part, top : top + 7, left : left + mz] = mid_x[first:last, mid_at : mid_at + 7, :]
        packed = pair_lanes(coarse_x[:, 0:9, :])
        for part, first, last, top, left in ninth_rows(mx + 11, cx + 13, at, 2 * cz):
            buf[part, top : top + 1, left : left + 2 * cz] = packed[first:last, 8:9, :]
        at += -(-(mx + 11) // 4)
        for part, first, last, top, left in quarters(cx + 13, at, 2 * cz):
            buf[part, top : top + 8, left : left + 2 * cz] = packed[first:last, 0:8, :]
        out[...] = buf[...].astype(BF16)

    flag = up_first("gy", 1, 1)

    @pl.when(flag)
    def _():
        pack(first_out, cells_y, my - 4)
        pack(second_out, 4, 0)

    @pl.when(jnp.logical_not(flag))
    def _():
        pack(first_out, 4, 0)
        pack(second_out, cells_y, my - 4)


def join_y_kernel(
    at, rows_m, coarse_x, first_in, second_in, coarse_xy, first_out, second_out,
    low, high, buf, side, from_low, from_high,
):
    cy = coarse_x.shape[1] // 4
    rows_c, cz = coarse_x.shape[0], coarse_x.shape[2]
    flag = up_first("gy", 1, 1)
    low[at:], high[at:] = by_order(flag, first_in[at:].astype(F32), second_in[at:].astype(F32))
    ninths = ninth_rows(rows_m, rows_c, at, 2 * cz)
    at += -(-rows_m // 4)
    for source, target in ((low, from_low), (high, from_high)):
        for part, first, last, top, left in ninths:
            target[first:last, 8:9, :] = unpair(source[part, top : top + 1, left : left + 2 * cz], cz)
        for part, first, last, top, left in quarters(rows_c, at, 2 * cz):
            target[first:last, 0:8, :] = unpair(source[part, top : top + 8, left : left + 2 * cz], cz)
    side[...] = jnp.zeros_like(side)
    side[:, 4 : 9 + cy, :] = coarse_x[:, 0 : cy + 5, :]
    coarse_xy[...] = side[...]
    coarse_xy[:, 0:9, :] += from_low[:, 0:9, :]
    buf[...] = jnp.zeros_like(buf)

    def pack(rows, out):
        rows = pair_lanes(rows)
        for part, first, last, top, left in quarters(rows_c, 0, 2 * cz):
            buf[part, top : top + 5, left : left + 2 * cz] = rows[first:last]
        out[...] = buf[...].astype(BF16)

    up = coarse_xy[:, 4 + cy : 9 + cy, :]
    coarse_xy[:, 4 + cy : 13 + cy, :] += from_high[:, 0:9, :]
    side[:, 4 + cy : 13 + cy, :] += from_high[:, 0:9, :]
    down = side[:, 4:9, :]
    flag = up_first("gy", 2, 0)
    pack(jnp.where(flag, up, down), first_out)
    pack(jnp.where(flag, down, up), second_out)


def bands_kernel(begin, levels, lines, *refs):
    outs, joint, last, turned = refs[:-3], refs[-3], refs[-2], refs[-1]
    tap = lax.broadcasted_iota(jnp.int32, (HALF, HALF), 0)
    place = lax.broadcasted_iota(jnp.int32, (HALF, HALF), 1)
    reverse = ((tap <= 8) & (place == jnp.where(tap <= 4, 4 - tap, HALF + 4 - tap))).astype(F32).astype(BF16)
    n = len(levels)
    flat = lines[9 * begin : 9 * (begin + n)].reshape(n * 9 * 16, HALF).astype(BF16)
    values = jnp.dot(flat, reverse, preferred_element_type=F32).reshape(n * 9, 16, HALF)
    turned[...] = pltpu.roll(values, 0, 2, stride=16, stride_axis=1)
    joint[...] = jnp.broadcast_to(jnp.sum(turned[:, 0:8, :], axis=1, keepdims=True), joint.shape)
    ninth = [turned[9 * i : 9 * i + 9, 8:9, :] for i in range(n)]
    ninth = functools.reduce(jnp.add, [pltpu.roll(v, 16 * i, 2) if i else v for i, v in enumerate(ninth)])
    last[...] = jnp.broadcast_to(ninth, last.shape)
    lane = lax.broadcasted_iota(jnp.int32, (8, HALF), 1)

    def one_dx(dx, carry):
        def turns(line):
            return [pltpu.roll(line, 8 * r, 1, stride=1, stride_axis=0) for r in range(16)]

        ninths = turns(last[dx])
        for level, ((depth, groups), out) in enumerate(zip(levels, outs)):
            per, steps = HALF // depth, depth // 8
            eights = turns(joint[9 * level + dx])
            for offset in range(2 * groups - 1):
                rows = []
                for a in range(per):
                    for g in range(steps):
                        full = jnp.zeros((8, HALF), F32)
                        for b in range(per):
                            line = per * offset + a - b
                            at = steps * b + g
                            if 0 <= line <= 8:
                                part = ninths[(at - 2 * level) % 16] if line == 8 else eights[(at - 2 * line) % 16]
                                full = part if per == 1 else jnp.where(lane // depth == b, part, full)
                        apart = lax.rem(lane, depth) - 8 * g - lax.broadcasted_iota(jnp.int32, (8, HALF), 0)
                        rows.append(jnp.where((apart <= 4) & (apart >= -4), full, 0.0))
                out[dx, offset] = jnp.concatenate(rows, axis=0).astype(BF16)
        return carry

    lax.fori_loop(0, 9, one_dx, 0)


def bands(lines, begin, levels, after=()):
    n = len(levels) * 9
    return call(
        functools.partial(bands_kernel, begin, levels),
        [((9, 2 * groups - 1, HALF, HALF), BF16) for _, groups in levels],
        [lines],
        [((n, 8, HALF), F32), ((9, 8, HALF), F32), ((n, 16, HALF), F32)],
        flops=10**9,
        after=after,
    )


def weights_of(blocks, dx):
    count = blocks.shape[1]
    zero = jnp.zeros((HALF, HALF), BF16)

    def block(offset):
        return blocks[dx, offset] if 0 <= offset < count else zero

    halves = range(count + 1)
    return jnp.concatenate([jnp.concatenate([block(h), block(h - 1)], axis=1) for h in halves], axis=0)


def gather_rows(field, rows, per, groups, depth, lhs):
    for parity in (0, 1):
        count = rows - parity
        for group in range(groups):
            for a in range(per):
                lane = group * WIDE + a * depth
                part = field[parity:rows, pl.ds(a + per * group, 8, stride=per), :]
                lhs[parity, 0 : count * 8, lane : lane + depth] = part.reshape(count * 8, depth).astype(BF16)


def gather_staged(field, rows, per, groups, depth, stage, lhs):
    count = field.shape[1] // per
    stage[...] = jnp.zeros_like(stage)
    for a in range(per):
        stage[:, 0:count, a * depth : (a + 1) * depth] = field[:, pl.ds(a, count, stride=per), :]
    for parity in (0, 1):
        n = (rows - parity) * 8
        for group in range(groups):
            part = stage[parity:rows, group : group + 8, :].reshape(n, WIDE)
            lhs[parity, 0:n, group * WIDE : (group + 1) * WIDE] = part.astype(BF16)


def convolve(lhs, weights, out_rows, acc):
    n = out_rows * 8
    for dx in range(9):
        start = 16 * (dx // 2)
        part = jnp.dot(lhs[dx % 2, start : start + n, :], weights_of(weights, dx), preferred_element_type=F32)
        acc[...] = part if dx == 0 else acc[...] + part


def own_kernel(fine_x, weights, acc, lhs):
    rows = fine_x.shape[0]
    gather_rows(fine_x, rows, 2, 5, fine_x.shape[2], lhs)
    convolve(lhs, weights, rows - 8, acc)


def group_weights(blocks, dx, group):
    return weights_of(blocks, dx)[group * WIDE : (group + 1) * WIDE]


def join_mid(first_in, second_in, mid_x, mid_xy, got):
    my, mz = mid_x.shape[1] // 2, mid_x.shape[2]
    count = got.shape[1]
    at = first_in.shape[0] - count
    got[0], got[1] = by_order(up_first("gy", 1, 1), *(v[at:].astype(F32) for v in (first_in, second_in)))
    mid_xy[...] = jnp.zeros_like(mid_xy)
    mid_xy[:, 4 : 7 + my, :] = mid_x[:, 0 : my + 3, :]
    for part, first, last, top, left in quarters(mid_x.shape[0], 0, mz):
        mid_xy[first:last, 0:7, :] += got[0, part, top : top + 7, left : left + mz]
        mid_xy[first:last, 4 + my : 11 + my, :] += got[1, part, top : top + 7, left : left + mz]


def rim_kernel(
    first_in, second_in, mid_x, own, fine_w, mid_w, fine_acc, mid_acc,
    rim, stage_f, lhs_f, stage, mid_lhs, sums, mid_xy, got,
):
    cells_x = own.shape[0] // 8
    quarter = cells_x // 4
    tiles = rim.shape[1]
    rim[0], rim[1] = by_order(up_first("gy", 1, 1), *(v[0:tiles].astype(F32) for v in (first_in, second_in)))
    for side in (0, 1):
        for q in range(4):
            for r in range(4):
                first, last = max(quarter * q, tiles * r), min(quarter * q + quarter + 8, tiles * r + tiles)
                if first < last:
                    to = slice(first - quarter * q, last - quarter * q)
                    source_rows = slice(first - tiles * r, last - tiles * r)
                    for a in (0, 1):
                        part = rim[side, source_rows, pl.ds(4 * r + a, 2, stride=2), :]
                        stage_f[side, to, 2 * q : 2 * q + 2, a * HALF : (a + 1) * HALF] = part
        for parity in (0, 1):
            n = quarter + 8 - parity
            lhs_f[side, parity, 0 : 8 * n, :] = stage_f[side, parity : parity + n].reshape(8 * n, WIDE).astype(BF16)
    n = quarter * 8
    for dx in range(9):
        start = 16 * (dx // 2)
        for i, (side, group) in enumerate(((0, 0), (0, 1), (1, 3), (1, 4))):
            rows = lhs_f[side, dx % 2, start : start + n, :]
            part = jnp.dot(rows, group_weights(fine_w, dx, group), preferred_element_type=F32)
            sums[i] = part if dx == 0 else sums[i] + part
    join_mid(first_in, second_in, mid_x, mid_xy, got)
    rows = mid_xy.shape[0]
    gather_staged(mid_xy, rows, 4, 3, mid_xy.shape[2], stage, mid_lhs)
    convolve(mid_lhs, mid_w, rows - 8, mid_acc)
    fine_acc[...] = own[...].reshape(fine_acc.shape)
    near, far, far_right, near_right = (sums[i].reshape(quarter, 8, WIDE) for i in range(4))
    odd = lax.rem(lax.broadcasted_iota(jnp.int32, near.shape, 1), 2) == 1
    stage_f[0, 0:quarter] = near + jnp.where(odd, 0.0, pltpu.roll(far, 7, 1))
    stage_f[1, 0:quarter] = near_right + jnp.where(odd, pltpu.roll(far_right, 1, 1), 0.0)
    for q in range(4):
        at = slice(quarter * q, quarter * q + quarter)
        fine_acc[at, 0:2, :] += stage_f[0, 0:quarter, 2 * q : 2 * q + 2, :]
        fine_acc[at, 6:8, :] += stage_f[1, 0:quarter, 2 * q : 2 * q + 2, :]


def prolong_odd(a, b, c, d):
    return 0.5625 * (b + c) - 0.0625 * (a + d)


def finish_kernel(
    counts, coarse_xy, first_in, second_in, coarse_w, fine_acc, mid_acc, out,
    crs_pad, stage, packed, crs_lhs, msg, crs_pot, wide, mid_tot,
):
    gx, gy = lax.axis_index("gx"), lax.axis_index("gy")
    nx, ny = counts
    rows_c, _, cz = coarse_xy.shape
    cells_x, cells_y, cells_z = out.shape
    mx, my, mz = cells_x // 2, cells_y // 2, cells_z // 2
    cx, cy = cells_x // 4, cells_y // 4
    crs_pad[...] = coarse_xy[...]
    received = by_order(up_first("gy", 2, 0), *(v[...].astype(F32) for v in (first_in, second_in)))
    for source, at in zip(received, (0, cy + 8)):
        msg[...] = source
        for part, first, last, top, left in quarters(rows_c, 0, 2 * cz):
            crs_pad[first:last, at : at + 5, :] += unpair(msg[part, top : top + 5, left : left + 2 * cz], cz)
    rows = rows_c - 8
    part = crs_lhs.shape[0] // 8
    per = HALF // cz
    stage[...] = jnp.zeros_like(stage)
    for a in range(per):
        stage[0:rows_c, 0:5, a * cz : (a + 1) * cz] = crs_pad[:, pl.ds(a, 5, stride=per), :]
    for q in range(2):
        for group in range(3):
            moved = stage[part * q : part * q + part + 8, group : group + 4, :]
            packed[:, 4 * q : 4 * q + 4, group * HALF : (group + 1) * HALF] = moved
    for dx in range(9):
        lhs = packed[dx : dx + part].reshape(part * 8, 3 * HALF)
        crs_lhs[:, dx * 3 * HALF : (dx + 1) * 3 * HALF] = lhs.astype(BF16)
    weights = coarse_w[...].reshape(9 * 3 * HALF, HALF)
    pot = jnp.dot(crs_lhs[...], weights, preferred_element_type=F32).reshape(part, 8, HALF)
    for q in range(2):
        for b in range(per):
            moved = pot[:, 4 * q : 4 * q + 3, b * cz : (b + 1) * cz]
            crs_pot[part * q : part * q + part, pl.ds(b, 3, stride=per), :] = moved
    pot = crs_pot[0:rows]
    keep = inside(pot.shape, 0, -2, cx, gx, nx) & inside(pot.shape, 1, -2, cy, gy, ny)
    pot = jnp.where(keep, pot, 0.0)
    n = cx + 2
    odd = prolong_odd(*(pot[s : s + n] for s in range(4)))
    even = jnp.concatenate([pot[2 : 1 + n], jnp.zeros_like(pot[:1])], axis=0) if n + 2 > rows else pot[2 : 2 + n]
    wide[:, 0] = odd
    wide[:, 1] = even
    wide_y = cy + 2
    v = wide[...].reshape((2 * n,) + pot.shape[1:])
    mid_tot[...] = jnp.zeros_like(mid_tot)
    odd = prolong_odd(*(v[:, s : s + wide_y] for s in range(4)))
    even = v[:, 2 : 1 + wide_y]
    matrix = transfer_matrix(mz, cz, True)
    mid_tot[:, pl.ds(0, wide_y, stride=2), 0:cz] = odd
    mid_tot[:, pl.ds(1, wide_y - 1, stride=2), 0:cz] = even
    total = dot_last(mid_tot[:, :, 0:cz], matrix)
    rows = mx + 3
    pot = mid_acc[...].reshape(rows, 8, WIDE)
    for b in range(4):
        mid_tot[0:rows, pl.ds(b, 3, stride=4), :] = pot[:, 0:3, b * mz : (b + 1) * mz]
    total = mid_tot[0:rows] + total[0:rows]
    keep = inside(total.shape, 0, -1, mx, gx, nx) & inside(total.shape, 1, -1, my, gy, ny)
    mid_tot[0:rows] = jnp.where(keep, total, 0.0)
    matrix = transfer_matrix(cells_z, mz, True)
    pot = fine_acc[...]
    for a in (0, 1):
        if a == 0:
            u = mid_tot[0:rows, 1 : 1 + my, :]
        else:
            u = prolong_odd(*(mid_tot[0:rows, s : s + my, :] for s in range(4)))
        u = dot_last(u, matrix)
        odd = prolong_odd(*(u[s : s + mx] for s in range(4)))
        both = jnp.stack([u[1 : 1 + mx], odd], axis=1).reshape(cells_x, my, cells_z)
        out[:, pl.ds(a, my, stride=2), :] = pot[:, :, a * HALF : a * HALF + cells_z] + both


def whole():
    return pl.BlockSpec(memory_space=pltpu.VMEM)


def call(kernel, outs, ins, scratch, flops=10**8, vmem_out=True, after=(), space=pltpu.VMEM, sems=0, limit=VMEM_LIMIT):
    n = len(ins)

    def body(*refs):
        kernel(*refs[:n], *refs[n + len(after) :])

    return pl.pallas_call(
        body,
        out_shape=[pltpu.VMEM(s, d) for s, d in outs] if vmem_out else [jax.ShapeDtypeStruct(s, d) for s, d in outs],
        in_specs=[pl.BlockSpec(memory_space=space)] * n + [pl.BlockSpec(memory_space=pl.ANY)] * len(after),
        out_specs=[whole()] * len(outs),
        scratch_shapes=[pltpu.VMEM(s, d) for s, d in scratch] + [pltpu.SemaphoreType.DMA((sems,))] * (sems > 0),
        compiler_params=pltpu.CompilerParams(vmem_limit_bytes=limit),
        cost_estimate=pl.CostEstimate(flops=flops, bytes_accessed=10**6, transcendentals=0),
    )(*ins, *after)


def swap(first, second, axis, step, size, start):
    received = []
    for message, group in ((first, start), (second, 1 - start)):
        lower = [i for i in range(size - step) if (i // step) % 2 == group]
        pairs = [(i, i + step) for i in lower] + [(i + step, i) for i in lower]
        received.append(lax.ppermute(message, axis, pairs))
    return received


def up_first(axis, step, start):
    return lax.rem(lax.axis_index(axis) // step, 2) == start


def by_order(flag, first, second):
    return jnp.where(flag, second, first), jnp.where(flag, first, second)


def local(counts, charges, kernel_fine, kernel_mid, kernel_coarse):
    nx, ny = counts
    cells_x, cells_y, cells_z = charges.shape
    mx, mz, cx, cz = cells_x // 2, cells_z // 2, cells_x // 4, cells_z // 4
    frame = cells_y
    lines = ((27, 16, HALF), F32)
    message = ((9, frame, cells_z), BF16)
    first, second, fine_own, mid_own, coarse_own, lines = call(
        functools.partial(spread_kernel, counts),
        [message, message, (charges.shape, BF16), ((mx + 3, frame, mz), F32), ((cx + 5, frame, cz), F32), lines],
        [charges, kernel_fine, kernel_mid, kernel_coarse],
        [
            ((mx + 3, frame + 24, mz), F32),
            ((mx + 3, frame + 24, mz), F32),
            ((cx + 5, frame, mz), F32),
            (charges.shape, F32),
            ((5, frame, cells_z), F32),
        ]
        + [((9, 9, 9), BF16)] * 3,
        space=pltpu.HBM,
        sems=4,
        limit=60 * 1024 * 1024,
    )
    first, second = swap(first, second, "gx", 1, nx, 1)
    fine_w, mid_w, coarse_w = bands(lines, 0, ((cells_z, 5), (mz, 3), (cz, 2)))
    rows = (cells_x + 8) // 4 + (mx + 14) // 4 + (cx + 16) // 4
    packed = ((rows, frame, cells_z), BF16)
    fine_x, mid_x, coarse_x, first, second = call(
        join_x_kernel,
        [
            ((cells_x + 8, cells_y + 8, cells_z), F32),
            ((mx + 11, frame, mz), F32),
            ((cx + 13, frame, cz), F32),
            packed,
            packed,
        ],
        [fine_own, mid_own, coarse_own, first, second],
        [((rows, frame, cells_z), F32), ((2, 5, frame, cells_z), F32)],
        after=(fine_w,),
    )
    first, second = swap(first, second, "gy", 1, ny, 1)
    (own_acc,) = call(
        own_kernel,
        [((cells_x * 8, WIDE), F32)],
        [fine_x, fine_w],
        [((2, (cells_x + 8) * 8, 5 * WIDE), BF16)],
        flops=10**9,
    )
    half = (cx + 16) // 4
    message = ((half, frame, cells_z), BF16)
    coarse_xy, last_first, last_second = call(
        functools.partial(join_y_kernel, (cells_x + 8) // 4, mx + 11),
        [
            ((cx + 13, frame + 8, cz), F32),
            message,
            message,
        ],
        [coarse_x, first, second],
        [
            ((rows, frame, cells_z), F32),
            ((rows, frame, cells_z), F32),
            ((half, frame, cells_z), F32),
            ((cx + 13, frame + 8, cz), F32),
            ((cx + 13, frame, cz), F32),
            ((cx + 13, frame, cz), F32),
        ],
        after=(own_acc,),
    )
    last_first, last_second = swap(last_first, last_second, "gy", 2, ny, 0)
    quarter = cells_x // 4
    fine_acc, mid_acc = call(
        rim_kernel,
        [((cells_x, 8, WIDE), F32), (((mx + 3) * 8, WIDE), F32)],
        [first, second, mid_x, own_acc, fine_w, mid_w],
        [
            ((2, (cells_x + 8) // 4, frame, cells_z), F32),
            ((2, quarter + 8, 8, WIDE), F32),
            ((2, 2, (quarter + 8) * 8, WIDE), BF16),
            ((mx + 11, 16, WIDE), F32),
            ((2, (mx + 12) * 8, 3 * WIDE), BF16),
            ((4, quarter * 8, WIDE), F32),
            ((mx + 11, frame + 8, mz), F32),
            ((2, rows - (cells_x + 8) // 4, frame, cells_z), F32),
        ],
        flops=10**9,
    )
    part = (cx + 6) // 2
    (out,) = call(
        functools.partial(finish_kernel, counts),
        [(charges.shape, F32)],
        [coarse_xy, last_first, last_second, coarse_w, fine_acc, mid_acc],
        [
            ((cx + 13, frame + 8, cz), F32),
            ((2 * part + 8, 8, HALF), F32),
            ((part + 8, 8, 3 * HALF), F32),
            ((part * 8, 9 * 3 * HALF), BF16),
            ((half, frame, cells_z), F32),
            ((2 * part, 16, cz), F32),
            ((cx + 2, 2, 16, cz), F32),
            ((mx + 4, 16, mz), F32),
        ],
        vmem_out=False,
    )
    return out


def solution(mesh):
    counts = (mesh.shape["gx"], mesh.shape["gy"])
    placed = (P("gx", "gy", None), P(), P(), P())
    return jax.shard_map(
        functools.partial(local, counts),
        mesh=mesh,
        in_specs=placed,
        out_specs=P("gx", "gy", None),
        check_vma=False,
    )
```

```python
import functools

import jax
import jax.numpy as jnp
from jax import lax
from jax.experimental import pallas as pl
from jax.experimental.pallas import tpu as pltpu
from jax.sharding import PartitionSpec as P

F32 = jnp.float32
BF16 = jnp.bfloat16
WIDE = 256
HALF = 128
VMEM_LIMIT = 14 * 1024 * 1024


def split_pair(v):
    high = v.astype(BF16).astype(F32)
    low = (v - high).astype(BF16).astype(F32)
    return high, low


def pair_lanes(v):
    return jnp.concatenate(split_pair(v), axis=-1)


def exact_dot(v, matrix):
    pair = pair_lanes(v).astype(BF16)
    return jnp.dot(pair, jnp.concatenate([matrix, matrix], axis=0), preferred_element_type=F32)


def transfer_matrix(fine, coarse, transpose):
    shape = (coarse, fine) if transpose else (fine, coarse)
    fine_at = lax.broadcasted_iota(jnp.int32, shape, 1 if transpose else 0)
    coarse_at = lax.broadcasted_iota(jnp.int32, shape, 0 if transpose else 1)
    d = fine_at - 2 * coarse_at
    one = jnp.where(d == 0, F32(1.0), F32(0.0))
    near = jnp.where((d == 1) | (d == -1), F32(0.5625), F32(0.0))
    far = jnp.where((d == 3) | (d == -3), F32(-0.0625), F32(0.0))
    return (one + near + far).astype(BF16)


def dot_last(v, matrix):
    lead = v.shape[:-1]
    return exact_dot(v.reshape(-1, v.shape[-1]), matrix).reshape(lead + (matrix.shape[1],))


def rows_at(v, first, low, count):
    begin, end = low - first, low - first + count
    inner = v[max(begin, 0) : min(end, v.shape[0])]
    parts = []
    if begin < 0:
        parts.append(jnp.zeros((-begin,) + v.shape[1:], v.dtype))
    parts.append(inner)
    if end > v.shape[0]:
        parts.append(jnp.zeros((end - v.shape[0],) + v.shape[1:], v.dtype))
    return jnp.concatenate(parts, axis=0) if len(parts) > 1 else inner


def weigh_restrict(even, odd0, odd_m1, odd_p1, odd_m2):
    return even + 0.5625 * (odd0 + odd_m1) - 0.0625 * (odd_p1 + odd_m2)


def restrict_rows(even, even_at, odd, odd_at, low, count):
    return weigh_restrict(
        rows_at(even, even_at, low, count),
        *(rows_at(odd, odd_at, low + s, count) for s in (0, -1, 1, -2)),
    )


def pairs_of_rows(v):
    v = v.reshape((v.shape[0] // 2, 2) + v.shape[1:])
    return v[:, 0], v[:, 1]


def inside(shape, axis, first, cells, index, count):
    at = lax.broadcasted_iota(jnp.int32, shape, axis) + first
    return ((at >= 0) | (index > 0)) & ((at < cells) | (index < count - 1))


def x_slots(count, rows):
    half = (count + 1) // 2
    y = slice(0, rows)
    return [
        (slice(0, half), rows, 0, slice(0, half), 0, y),
        (slice(half, count), rows, HALF // 2, slice(0, count - half), 0, y),
    ]


def x_pair_slots(used, rows, frame):
    top, rest = frame - used, rows - (frame - used)
    slots = [(slice(8, 9), rows, HALF // 2, slice(3, 4), 0, slice(0, rows))]
    for half in (0, 1):
        left = half * HALF // 2
        slots.append((slice(4 * half, 4 * half + 4), top, left, slice(0, 4), used, slice(0, top)))
        for g in range(4):
            x = 4 * half + g
            slots.append((slice(x, x + 1), rest, left, slice(4, 5), rest * g, slice(top, rows)))
    return slots


def spread_kernel(counts, *refs):
    outside, (first_out, second_out, fine_own, mid_own, coarse_own, lines) = refs[0:4], refs[4:10]
    (even_pad, odd_pad, crs, charges, msg), raws, sems = refs[10:15], refs[15:18], refs[18]
    copies = [
        pltpu.make_async_copy(source, target, sems.at[i])
        for i, (source, target) in enumerate(zip(outside, (charges,) + raws))
    ]
    for copy in copies:
        copy.start()
    even_pad[...] = jnp.zeros_like(even_pad)
    odd_pad[...] = jnp.zeros_like(odd_pad)
    lines[...] = jnp.zeros_like(lines)
    msg[...] = jnp.zeros_like(msg)
    copies[0].wait()
    fine_own[...] = charges[...].astype(BF16)
    gx, gy = lax.axis_index("gx"), lax.axis_index("gy")
    nx, ny = counts
    cells_x, cells_y, cells_z = charges.shape
    mx, my, mz = cells_x // 2, cells_y // 2, cells_z // 2
    cx, cy, cz = cells_x // 4, cells_y // 4, cells_z // 4
    frame = mid_own.shape[1]
    even, odd = pairs_of_rows(charges[...])
    mid = restrict_rows(even, 0, odd, 0, -1, mx + 3)
    mid = dot_last(mid, transfer_matrix(cells_z, mz, False))
    mid_own[...] = mid
    even_pad[:, 8 : 8 + my] = mid_own[:, pl.ds(0, my, stride=2), :]
    odd_pad[:, 8 : 8 + my] = mid_own[:, pl.ds(1, my, stride=2), :]
    mid = weigh_restrict(
        even_pad[:, 7 : 7 + frame],
        *(odd_pad[:, 7 + s : 7 + s + frame] for s in (0, -1, 1, -2)),
    )
    keep = inside(mid.shape, 0, -1, mx, gx, nx) & inside(mid.shape, 1, -1, my, gy, ny)
    mid = jnp.where(keep, mid, 0.0)
    mid_own[...] = mid
    odd, even = pairs_of_rows(jnp.concatenate([mid, jnp.zeros_like(mid[:1])], axis=0))
    crs[...] = restrict_rows(even, 0, odd, -1, -2, cx + 5)
    n = cx + 5
    odd_pad[:n, 8 : 8 + frame // 2] = crs[:, pl.ds(0, frame // 2, stride=2), :]
    even_pad[:n, 8 : 8 + frame // 2] = crs[:, pl.ds(1, frame // 2, stride=2), :]
    coarse = weigh_restrict(
        even_pad[:n, 6 : 6 + frame],
        *(odd_pad[:n, 7 + s : 7 + s + frame] for s in (0, -1, 1, -2)),
    )
    coarse = dot_last(coarse, transfer_matrix(mz, cz, False))
    keep = inside(coarse.shape, 0, -2, cx, gx, nx) & inside(coarse.shape, 1, -2, cy, gy, ny)
    coarse = jnp.where(keep, coarse, 0.0)
    coarse_own[...] = coarse
    def pack(out, fine_at, mid_at, coarse_at):
        out[0:4] = charges[fine_at : fine_at + 4].astype(BF16)
        for part, rows, left, tile, top, y in x_slots(7, my + 3):
            value = mid_own[mid_at + part.start : mid_at + part.stop, y, :]
            msg[tile, top : top + rows, left : left + mz] = value
        for part, rows, left, tile, top, y in x_pair_slots(my + 3, cy + 5, frame):
            value = coarse_own[coarse_at + part.start : coarse_at + part.stop, y, :]
            msg[tile, top : top + rows, left : left + 2 * cz] = pair_lanes(value)
        out[4:9] = msg[...].astype(BF16)

    flag = up_first("gx", 1, 1)

    @pl.when(flag)
    def _():
        pack(first_out, cells_x - 4, mx - 4, cx - 4)
        pack(second_out, 0, 0, 0)

    @pl.when(jnp.logical_not(flag))
    def _():
        pack(first_out, 0, 0, 0)
        pack(second_out, cells_x - 4, mx - 4, cx - 4)

    for i, raw in enumerate(raws):
        copies[i + 1].wait()
        lines[9 * i : 9 * i + 9, 0:9, 0:9] = raw[...].astype(F32)


def two_halves(v):
    half = (v.shape[0] + 1) // 2
    return jnp.concatenate([v[:half], rows_at(v, 0, half, half)], axis=-1)


def unpair(v, width):
    return v[..., :width] + v[..., width : 2 * width]


def from_halves(v, count):
    lanes = v.shape[-1] // 2
    return jnp.concatenate([v[..., :lanes], v[: count - v.shape[0], :, lanes:]], axis=0)


def fine_parts(rows):
    q = rows // 4
    return [(slice(0, q), q * r, q * r + q, 4 * r, 0) for r in range(4)]


def quarters(rows, at, lanes):
    q = -(-rows // 4)
    parts = []
    for r in range(4):
        first, last = q * r, min(q * r + q, rows)
        parts.append((slice(at, at + last - first), first, last, 8 * (r // 2), lanes * (r % 2)))
    return parts


def ninth_rows(rows, count, at, lanes):
    parts = []
    for part, first, last, top, left in quarters(rows, at, lanes):
        last = min(last, count)
        if first < last:
            parts.append((slice(part.start, part.start + last - first), first, last, top + 7, left))
    return parts


def join_x_kernel(charges, mid_own, coarse_own, first_in, second_in, mid_x, coarse_x, first_out, second_out, buf, got, edge):
    before, after = by_order(up_first("gx", 1, 1), *(v[...].astype(F32) for v in (first_in, second_in)))
    cells_x, cells_y, _ = charges.shape
    mx, cx = cells_x // 2, cells_x // 4
    mz, cz = mid_own.shape[2], coarse_own.shape[2]
    my = cells_y // 2
    ends = ((0, slice(0, 4)), (4, slice(cells_y - 4, cells_y)))
    for top, y in ends:
        edge[0:4, top : top + 4, :] = before[0:4, y]
        edge[4 : 4 + cells_x, top : top + 4, :] = charges[...].astype(F32)[:, y]
        edge[4 + cells_x : 8 + cells_x, top : top + 4, :] = after[0:4, y]
    got[0], got[1] = before[4:9], after[4:9]
    mid_x[...] = rows_at(mid_own[...], -1, -5, mx + 11)
    coarse_x[...] = rows_at(coarse_own[...], -2, -6, cx + 13)
    for side, mid_at, coarse_at in ((0, 0, 0), (1, mx + 4, cx + 4)):
        for part, rows, left, tile, top, y in x_slots(7, my + 3):
            at = slice(mid_at + part.start, mid_at + part.stop)
            mid_x[at, y, :] += got[side, tile, top : top + rows, left : left + mz]
        for part, rows, left, tile, top, y in x_pair_slots(my + 3, cells_y // 4 + 5, cells_y):
            at = slice(coarse_at + part.start, coarse_at + part.stop)
            coarse_x[at, y, :] += unpair(got[side, tile, top : top + rows, left : left + 2 * cz], cz)
    buf[...] = jnp.zeros_like(buf)

    def pack(out, fine_at, mid_at):
        for part, first, last, top, left in fine_parts(cells_x + 8):
            buf[part, top : top + 4, left:] = edge[first:last, fine_at : fine_at + 4, :]
        at = (cells_x + 8) // 4
        for part, first, last, top, left in quarters(mx + 11, at, mz):
            buf[part, top : top + 7, left : left + mz] = mid_x[first:last, mid_at : mid_at + 7, :]
        packed = pair_lanes(coarse_x[:, 0:9, :])
        for part, first, last, top, left in ninth_rows(mx + 11, cx + 13, at, 2 * cz):
            buf[part, top : top + 1, left : left + 2 * cz] = packed[first:last, 8:9, :]
        at += -(-(mx + 11) // 4)
        for part, first, last, top, left in quarters(cx + 13, at, 2 * cz):
            buf[part, top : top + 8, left : left + 2 * cz] = packed[first:last, 0:8, :]
        out[...] = buf[...].astype(BF16)

    flag = up_first("gy", 1, 1)

    @pl.when(flag)
    def _():
        pack(first_out, 4, my - 4)
        pack(second_out, 0, 0)

    @pl.when(jnp.logical_not(flag))
    def _():
        pack(first_out, 0, 0)
        pack(second_out, 4, my - 4)


def join_y_kernel(
    at, rows_m, coarse_x, first_in, second_in, coarse_xy, first_out, second_out,
    low, high, buf, side, from_low, from_high,
):
    cy = coarse_x.shape[1] // 4
    rows_c, cz = coarse_x.shape[0], coarse_x.shape[2]
    flag = up_first("gy", 1, 1)
    low[at:], high[at:] = by_order(flag, first_in[at:].astype(F32), second_in[at:].astype(F32))
    ninths = ninth_rows(rows_m, rows_c, at, 2 * cz)
    at += -(-rows_m // 4)
    for source, target in ((low, from_low), (high, from_high)):
        for part, first, last, top, left in ninths:
            target[first:last, 8:9, :] = unpair(source[part, top : top + 1, left : left + 2 * cz], cz)
        for part, first, last, top, left in quarters(rows_c, at, 2 * cz):
            target[first:last, 0:8, :] = unpair(source[part, top : top + 8, left : left + 2 * cz], cz)
    side[...] = jnp.zeros_like(side)
    side[:, 4 : 9 + cy, :] = coarse_x[:, 0 : cy + 5, :]
    coarse_xy[...] = side[...]
    coarse_xy[:, 0:9, :] += from_low[:, 0:9, :]
    buf[...] = jnp.zeros_like(buf)

    def pack(rows, out):
        rows = pair_lanes(rows)
        for part, first, last, top, left in quarters(rows_c, 0, 2 * cz):
            buf[part, top : top + 5, left : left + 2 * cz] = rows[first:last]
        out[...] = buf[...].astype(BF16)

    up = coarse_xy[:, 4 + cy : 9 + cy, :]
    coarse_xy[:, 4 + cy : 13 + cy, :] += from_high[:, 0:9, :]
    side[:, 4 + cy : 13 + cy, :] += from_high[:, 0:9, :]
    down = side[:, 4:9, :]
    flag = up_first("gy", 2, 0)
    pack(jnp.where(flag, up, down), first_out)
    pack(jnp.where(flag, down, up), second_out)


def bands_kernel(begin, levels, lines, *refs):
    outs, joint, last, turned = refs[:-3], refs[-3], refs[-2], refs[-1]
    tap = lax.broadcasted_iota(jnp.int32, (HALF, HALF), 0)
    place = lax.broadcasted_iota(jnp.int32, (HALF, HALF), 1)
    reverse = ((tap <= 8) & (place == jnp.where(tap <= 4, 4 - tap, HALF + 4 - tap))).astype(F32).astype(BF16)
    n = len(levels)
    flat = lines[9 * begin : 9 * (begin + n)].reshape(n * 9 * 16, HALF).astype(BF16)
    values = jnp.dot(flat, reverse, preferred_element_type=F32).reshape(n * 9, 16, HALF)
    turned[...] = pltpu.roll(values, 0, 2, stride=16, stride_axis=1)
    joint[...] = jnp.broadcast_to(jnp.sum(turned[:, 0:8, :], axis=1, keepdims=True), joint.shape)
    ninth = [turned[9 * i : 9 * i + 9, 8:9, :] for i in range(n)]
    ninth = functools.reduce(jnp.add, [pltpu.roll(v, 16 * i, 2) if i else v for i, v in enumerate(ninth)])
    last[...] = jnp.broadcast_to(ninth, last.shape)
    lane = lax.broadcasted_iota(jnp.int32, (8, HALF), 1)

    def one_dx(dx, carry):
        def turns(line):
            return [pltpu.roll(line, 8 * r, 1, stride=1, stride_axis=0) for r in range(16)]

        ninths = turns(last[dx])
        for level, ((depth, groups), out) in enumerate(zip(levels, outs)):
            per, steps = HALF // depth, depth // 8
            eights = turns(joint[9 * level + dx])
            for offset in range(2 * groups - 1):
                rows = []
                for a in range(per):
                    for g in range(steps):
                        full = jnp.zeros((8, HALF), F32)
                        for b in range(per):
                            line = per * offset + a - b
                            at = steps * b + g
                            if 0 <= line <= 8:
                                part = ninths[(at - 2 * level) % 16] if line == 8 else eights[(at - 2 * line) % 16]
                                full = part if per == 1 else jnp.where(lane // depth == b, part, full)
                        apart = lax.rem(lane, depth) - 8 * g - lax.broadcasted_iota(jnp.int32, (8, HALF), 0)
                        rows.append(jnp.where((apart <= 4) & (apart >= -4), full, 0.0))
                out[dx, offset] = jnp.concatenate(rows, axis=0).astype(BF16)
        return carry

    lax.fori_loop(0, 9, one_dx, 0)


def bands(lines, begin, levels, after=()):
    n = len(levels) * 9
    return call(
        functools.partial(bands_kernel, begin, levels),
        [((9, 2 * groups - 1, HALF, HALF), BF16) for _, groups in levels],
        [lines],
        [((n, 8, HALF), F32), ((9, 8, HALF), F32), ((n, 16, HALF), F32)],
        flops=10**9,
        after=after,
    )


def weights_of(blocks, dx):
    count = blocks.shape[1]
    zero = jnp.zeros((HALF, HALF), BF16)

    def block(offset):
        return blocks[dx, offset] if 0 <= offset < count else zero

    halves = range(count + 1)
    return jnp.concatenate([jnp.concatenate([block(h), block(h - 1)], axis=1) for h in halves], axis=0)


def gather_rows(field, rows, per, groups, depth, lhs):
    for parity in (0, 1):
        count = rows - parity
        for group in range(groups):
            for a in range(per):
                lane = group * WIDE + a * depth
                part = field[parity:rows, pl.ds(a + per * group, 8, stride=per), :]
                lhs[parity, 0 : count * 8, lane : lane + depth] = part.reshape(count * 8, depth).astype(BF16)


def gather_staged(field, rows, per, groups, depth, stage, lhs):
    count = field.shape[1] // per
    stage[...] = jnp.zeros_like(stage)
    for a in range(per):
        stage[:, 0:count, a * depth : (a + 1) * depth] = field[:, pl.ds(a, count, stride=per), :]
    for parity in (0, 1):
        n = (rows - parity) * 8
        for group in range(groups):
            part = stage[parity:rows, group : group + 8, :].reshape(n, WIDE)
            lhs[parity, 0:n, group * WIDE : (group + 1) * WIDE] = part.astype(BF16)


def convolve(lhs, weights, out_rows, acc):
    n = out_rows * 8
    for dx in range(9):
        start = 16 * (dx // 2)
        part = jnp.dot(lhs[dx % 2, start : start + n, :], weights_of(weights, dx), preferred_element_type=F32)
        acc[...] = part if dx == 0 else acc[...] + part


def own_kernel(charges, first_in, second_in, weights, acc, lhs, fine_x):
    rows, cells_x, cells_y = fine_x.shape[0], charges.shape[0], charges.shape[1]
    before, after = by_order(up_first("gx", 1, 1), *(v[0:4].astype(F32) for v in (first_in, second_in)))
    own = slice(4, 4 + cells_y)
    for edge in (0, 4 + cells_y):
        fine_x[:, edge : edge + 4, :] = jnp.zeros((rows, 4, charges.shape[2]), F32)
    fine_x[0:4, own, :] = before
    fine_x[4 : 4 + cells_x, own, :] = charges[...].astype(F32)
    fine_x[4 + cells_x : rows, own, :] = after
    gather_rows(fine_x, rows, 2, 5, fine_x.shape[2], lhs)
    convolve(lhs, weights, rows - 8, acc)


def group_weights(blocks, dx, group):
    return weights_of(blocks, dx)[group * WIDE : (group + 1) * WIDE]


def join_mid(first_in, second_in, mid_x, mid_xy, got):
    my, mz = mid_x.shape[1] // 2, mid_x.shape[2]
    count = got.shape[1]
    at = first_in.shape[0] - count
    got[0], got[1] = by_order(up_first("gy", 1, 1), *(v[at:].astype(F32) for v in (first_in, second_in)))
    mid_xy[...] = jnp.zeros_like(mid_xy)
    mid_xy[:, 4 : 7 + my, :] = mid_x[:, 0 : my + 3, :]
    for part, first, last, top, left in quarters(mid_x.shape[0], 0, mz):
        mid_xy[first:last, 0:7, :] += got[0, part, top : top + 7, left : left + mz]
        mid_xy[first:last, 4 + my : 11 + my, :] += got[1, part, top : top + 7, left : left + mz]


def rim_kernel(
    first_in, second_in, mid_x, own, fine_w, mid_w, fine_acc, mid_acc,
    rim, stage_f, lhs_f, stage, mid_lhs, sums, mid_xy, got,
):
    cells_x = own.shape[0] // 8
    quarter = cells_x // 4
    tiles = rim.shape[1]
    rim[0], rim[1] = by_order(up_first("gy", 1, 1), *(v[0:tiles].astype(F32) for v in (first_in, second_in)))
    for side in (0, 1):
        for q in range(4):
            for r in range(4):
                first, last = max(quarter * q, tiles * r), min(quarter * q + quarter + 8, tiles * r + tiles)
                if first < last:
                    to = slice(first - quarter * q, last - quarter * q)
                    source_rows = slice(first - tiles * r, last - tiles * r)
                    for a in (0, 1):
                        part = rim[side, source_rows, pl.ds(4 * r + a, 2, stride=2), :]
                        stage_f[side, to, 2 * q : 2 * q + 2, a * HALF : (a + 1) * HALF] = part
        for parity in (0, 1):
            n = quarter + 8 - parity
            lhs_f[side, parity, 0 : 8 * n, :] = stage_f[side, parity : parity + n].reshape(8 * n, WIDE).astype(BF16)
    n = quarter * 8
    for dx in range(9):
        start = 16 * (dx // 2)
        for i, (side, group) in enumerate(((0, 0), (0, 1), (1, 3), (1, 4))):
            rows = lhs_f[side, dx % 2, start : start + n, :]
            part = jnp.dot(rows, group_weights(fine_w, dx, group), preferred_element_type=F32)
            sums[i] = part if dx == 0 else sums[i] + part
    join_mid(first_in, second_in, mid_x, mid_xy, got)
    rows = mid_xy.shape[0]
    gather_staged(mid_xy, rows, 4, 3, mid_xy.shape[2], stage, mid_lhs)
    convolve(mid_lhs, mid_w, rows - 8, mid_acc)
    fine_acc[...] = own[...].reshape(fine_acc.shape)
    near, far, far_right, near_right = (sums[i].reshape(quarter, 8, WIDE) for i in range(4))
    odd = lax.rem(lax.broadcasted_iota(jnp.int32, near.shape, 1), 2) == 1
    stage_f[0, 0:quarter] = near + jnp.where(odd, 0.0, pltpu.roll(far, 7, 1))
    stage_f[1, 0:quarter] = near_right + jnp.where(odd, pltpu.roll(far_right, 1, 1), 0.0)
    for q in range(4):
        at = slice(quarter * q, quarter * q + quarter)
        fine_acc[at, 0:2, :] += stage_f[0, 0:quarter, 2 * q : 2 * q + 2, :]
        fine_acc[at, 6:8, :] += stage_f[1, 0:quarter, 2 * q : 2 * q + 2, :]


def prolong_odd(a, b, c, d):
    return 0.5625 * (b + c) - 0.0625 * (a + d)


def finish_kernel(
    counts, coarse_xy, first_in, second_in, coarse_w, fine_acc, mid_acc, out,
    crs_pad, stage, packed, crs_lhs, msg, crs_pot, wide, mid_tot,
):
    gx, gy = lax.axis_index("gx"), lax.axis_index("gy")
    nx, ny = counts
    rows_c, _, cz = coarse_xy.shape
    cells_x, cells_y, cells_z = out.shape
    mx, my, mz = cells_x // 2, cells_y // 2, cells_z // 2
    cx, cy = cells_x // 4, cells_y // 4
    crs_pad[...] = coarse_xy[...]
    received = by_order(up_first("gy", 2, 0), *(v[...].astype(F32) for v in (first_in, second_in)))
    for source, at in zip(received, (0, cy + 8)):
        msg[...] = source
        for part, first, last, top, left in quarters(rows_c, 0, 2 * cz):
            crs_pad[first:last, at : at + 5, :] += unpair(msg[part, top : top + 5, left : left + 2 * cz], cz)
    rows = rows_c - 8
    part = crs_lhs.shape[0] // 8
    per = HALF // cz
    stage[...] = jnp.zeros_like(stage)
    for a in range(per):
        stage[0:rows_c, 0:5, a * cz : (a + 1) * cz] = crs_pad[:, pl.ds(a, 5, stride=per), :]
    for q in range(2):
        for group in range(3):
            moved = stage[part * q : part * q + part + 8, group : group + 4, :]
            packed[:, 4 * q : 4 * q + 4, group * HALF : (group + 1) * HALF] = moved
    for dx in range(9):
        lhs = packed[dx : dx + part].reshape(part * 8, 3 * HALF)
        crs_lhs[:, dx * 3 * HALF : (dx + 1) * 3 * HALF] = lhs.astype(BF16)
    weights = coarse_w[...].reshape(9 * 3 * HALF, HALF)
    pot = jnp.dot(crs_lhs[...], weights, preferred_element_type=F32).reshape(part, 8, HALF)
    for q in range(2):
        for b in range(per):
            moved = pot[:, 4 * q : 4 * q + 3, b * cz : (b + 1) * cz]
            crs_pot[part * q : part * q + part, pl.ds(b, 3, stride=per), :] = moved
    pot = crs_pot[0:rows]
    keep = inside(pot.shape, 0, -2, cx, gx, nx) & inside(pot.shape, 1, -2, cy, gy, ny)
    pot = jnp.where(keep, pot, 0.0)
    n = cx + 2
    odd = prolong_odd(*(pot[s : s + n] for s in range(4)))
    even = jnp.concatenate([pot[2 : 1 + n], jnp.zeros_like(pot[:1])], axis=0) if n + 2 > rows else pot[2 : 2 + n]
    wide[:, 0] = odd
    wide[:, 1] = even
    wide_y = cy + 2
    v = wide[...].reshape((2 * n,) + pot.shape[1:])
    mid_tot[...] = jnp.zeros_like(mid_tot)
    odd = prolong_odd(*(v[:, s : s + wide_y] for s in range(4)))
    even = v[:, 2 : 1 + wide_y]
    matrix = transfer_matrix(mz, cz, True)
    mid_tot[:, pl.ds(0, wide_y, stride=2), 0:cz] = odd
    mid_tot[:, pl.ds(1, wide_y - 1, stride=2), 0:cz] = even
    total = dot_last(mid_tot[:, :, 0:cz], matrix)
    rows = mx + 3
    pot = mid_acc[...].reshape(rows, 8, WIDE)
    for b in range(4):
        mid_tot[0:rows, pl.ds(b, 3, stride=4), :] = pot[:, 0:3, b * mz : (b + 1) * mz]
    total = mid_tot[0:rows] + total[0:rows]
    keep = inside(total.shape, 0, -1, mx, gx, nx) & inside(total.shape, 1, -1, my, gy, ny)
    mid_tot[0:rows] = jnp.where(keep, total, 0.0)
    matrix = transfer_matrix(cells_z, mz, True)
    pot = fine_acc[...]
    for a in (0, 1):
        if a == 0:
            u = mid_tot[0:rows, 1 : 1 + my, :]
        else:
            u = prolong_odd(*(mid_tot[0:rows, s : s + my, :] for s in range(4)))
        u = dot_last(u, matrix)
        odd = prolong_odd(*(u[s : s + mx] for s in range(4)))
        both = jnp.stack([u[1 : 1 + mx], odd], axis=1).reshape(cells_x, my, cells_z)
        out[:, pl.ds(a, my, stride=2), :] = pot[:, :, a * HALF : a * HALF + cells_z] + both


def whole():
    return pl.BlockSpec(memory_space=pltpu.VMEM)


def call(kernel, outs, ins, scratch, flops=10**8, vmem_out=True, after=(), space=pltpu.VMEM, sems=0, limit=VMEM_LIMIT):
    n = len(ins)

    def body(*refs):
        kernel(*refs[:n], *refs[n + len(after) :])

    return pl.pallas_call(
        body,
        out_shape=[pltpu.VMEM(s, d) for s, d in outs] if vmem_out else [jax.ShapeDtypeStruct(s, d) for s, d in outs],
        in_specs=[pl.BlockSpec(memory_space=space)] * n + [pl.BlockSpec(memory_space=pl.ANY)] * len(after),
        out_specs=[whole()] * len(outs),
        scratch_shapes=[pltpu.VMEM(s, d) for s, d in scratch] + [pltpu.SemaphoreType.DMA((sems,))] * (sems > 0),
        compiler_params=pltpu.CompilerParams(vmem_limit_bytes=limit),
        cost_estimate=pl.CostEstimate(flops=flops, bytes_accessed=10**6, transcendentals=0),
    )(*ins, *after)


def swap(first, second, axis, step, size, start):
    received = []
    for message, group in ((first, start), (second, 1 - start)):
        lower = [i for i in range(size - step) if (i // step) % 2 == group]
        pairs = [(i, i + step) for i in lower] + [(i + step, i) for i in lower]
        received.append(lax.ppermute(message, axis, pairs))
    return received


def up_first(axis, step, start):
    return lax.rem(lax.axis_index(axis) // step, 2) == start


def by_order(flag, first, second):
    return jnp.where(flag, second, first), jnp.where(flag, first, second)


def local(counts, charges, kernel_fine, kernel_mid, kernel_coarse):
    nx, ny = counts
    cells_x, cells_y, cells_z = charges.shape
    mx, mz, cx, cz = cells_x // 2, cells_z // 2, cells_x // 4, cells_z // 4
    frame = cells_y
    lines = ((27, 16, HALF), F32)
    message = ((9, frame, cells_z), BF16)
    first, second, fine_own, mid_own, coarse_own, lines = call(
        functools.partial(spread_kernel, counts),
        [message, message, (charges.shape, BF16), ((mx + 3, frame, mz), F32), ((cx + 5, frame, cz), F32), lines],
        [charges, kernel_fine, kernel_mid, kernel_coarse],
        [
            ((mx + 3, frame + 24, mz), F32),
            ((mx + 3, frame + 24, mz), F32),
            ((cx + 5, frame, mz), F32),
            (charges.shape, F32),
            ((5, frame, cells_z), F32),
        ]
        + [((9, 9, 9), BF16)] * 3,
        space=pltpu.HBM,
        sems=4,
        limit=60 * 1024 * 1024,
    )
    first, second = swap(first, second, "gx", 1, nx, 1)
    fine_w, mid_w, coarse_w = bands(lines, 0, ((cells_z, 5), (mz, 3), (cz, 2)))
    rows = (cells_x + 8) // 4 + (mx + 14) // 4 + (cx + 16) // 4
    packed = ((rows, frame, cells_z), BF16)
    first_x, second_x = first, second
    mid_x, coarse_x, first, second = call(
        join_x_kernel,
        [
            ((mx + 11, frame, mz), F32),
            ((cx + 13, frame, cz), F32),
            packed,
            packed,
        ],
        [fine_own, mid_own, coarse_own, first, second],
        [((rows, frame, cells_z), F32), ((2, 5, frame, cells_z), F32), ((cells_x + 8, 8, cells_z), F32)],
        after=(fine_w,),
    )
    first, second = swap(first, second, "gy", 1, ny, 1)
    (own_acc,) = call(
        own_kernel,
        [((cells_x * 8, WIDE), F32)],
        [fine_own, first_x, second_x, fine_w],
        [((2, (cells_x + 8) * 8, 5 * WIDE), BF16), ((cells_x + 8, cells_y + 8, cells_z), F32)],
        flops=10**9,
    )
    half = (cx + 16) // 4
    message = ((half, frame, cells_z), BF16)
    coarse_xy, last_first, last_second = call(
        functools.partial(join_y_kernel, (cells_x + 8) // 4, mx + 11),
        [
            ((cx + 13, frame + 8, cz), F32),
            message,
            message,
        ],
        [coarse_x, first, second],
        [
            ((rows, frame, cells_z), F32),
            ((rows, frame, cells_z), F32),
            ((half, frame, cells_z), F32),
            ((cx + 13, frame + 8, cz), F32),
            ((cx + 13, frame, cz), F32),
            ((cx + 13, frame, cz), F32),
        ],
        after=(own_acc,),
    )
    last_first, last_second = swap(last_first, last_second, "gy", 2, ny, 0)
    quarter = cells_x // 4
    fine_acc, mid_acc = call(
        rim_kernel,
        [((cells_x, 8, WIDE), F32), (((mx + 3) * 8, WIDE), F32)],
        [first, second, mid_x, own_acc, fine_w, mid_w],
        [
            ((2, (cells_x + 8) // 4, frame, cells_z), F32),
            ((2, quarter + 8, 8, WIDE), F32),
            ((2, 2, (quarter + 8) * 8, WIDE), BF16),
            ((mx + 11, 16, WIDE), F32),
            ((2, (mx + 12) * 8, 3 * WIDE), BF16),
            ((4, quarter * 8, WIDE), F32),
            ((mx + 11, frame + 8, mz), F32),
            ((2, rows - (cells_x + 8) // 4, frame, cells_z), F32),
        ],
        flops=10**9,
    )
    part = (cx + 6) // 2
    (out,) = call(
        functools.partial(finish_kernel, counts),
        [(charges.shape, F32)],
        [coarse_xy, last_first, last_second, coarse_w, fine_acc, mid_acc],
        [
            ((cx + 13, frame + 8, cz), F32),
            ((2 * part + 8, 8, HALF), F32),
            ((part + 8, 8, 3 * HALF), F32),
            ((part * 8, 9 * 3 * HALF), BF16),
            ((half, frame, cells_z), F32),
            ((2 * part, 16, cz), F32),
            ((cx + 2, 2, 16, cz), F32),
            ((mx + 4, 16, mz), F32),
        ],
        vmem_out=False,
    )
    return out


def solution(mesh):
    counts = (mesh.shape["gx"], mesh.shape["gy"])
    placed = (P("gx", "gy", None), P(), P(), P())
    return jax.shard_map(
        functools.partial(local, counts),
        mesh=mesh,
        in_specs=placed,
        out_specs=P("gx", "gy", None),
        check_vma=False,
    )
```
